32 devices in a mesh: replica: 4 (over z), fsdp: 8 (over y, x, core).
Axes of the slice: x: 2, y: 2, z: 4, core: 2. Of those that a mesh axis runs over, the one named last changes fastest.
Arguments:
- node_feats: bfloat16 [4096, 1024], P(('replica', 'fsdp')), may hold values from -6 to 6
- neighbor_src: int32 [12, 4096], P(None, ('replica', 'fsdp')), may hold values from 0 to 1023, as said below
- distances: float32 [12, 4096], P(None, ('replica', 'fsdp')), may hold values from 0.8 to 5
- graph_ids: int32 [4, 1024], P('replica', 'fsdp'), may hold values from 0 to 7, never falling along the last dimension, each value on 1 to 256 neighbouring positions
- msg_weight: bfloat16 [1024, 1024], P('fsdp'), may hold values from -0.1875 to 0.1875
- out_weight: bfloat16 [1024, 1024], P('fsdp'), may hold values from -0.1875 to 0.1875
- radial_weight: float32 [8, 1024], replicated, may hold values from -6 to 6
- cotangent: bfloat16 [4096, 1024], P(('replica', 'fsdp')), may hold values from -6 to 6
- fragment: int32 [1], replicated, may hold values from 0 to 7
Outputs:
- node_out: bfloat16 [4096, 1024], P(('replica', 'fsdp'))
- grad_msg: bfloat16 [4, 1024, 1024], P('replica', 'fsdp')
- grad_out: bfloat16 [4, 1024, 1024], P('replica', 'fsdp')
- outer_sum: float32 [2, 1024, 128], P(None, 'fsdp')
The draws below stay inside these ranges and needn't reach their ends.
Inputs may be any that keep to these rules, and one draw needn't show every extreme that they name: `neighbor_src`: each neighbour index lies within 32 positions of its own atom's index in the group, never equal to it, and inside the group. `graph_ids`: within each group the graph numbers never fall and every graph has at least one atom.
All inputs are finite; a program needn't handle non-finite values. Where the reference program divides by a largest or mean magnitude, that divisor is 1e-20 or more.
Results may differ from the reference program's by a relative error of at most 0.02.
Values may be sent and summed in bfloat16 or wider, within the bound.
No kernel may reach another device: no remote copies, remote signals or barrier semaphores. Data moves between devices by JAX's collectives and lax.ppermute only.
A program may use at most 64 MiB of HBM per device.

```python
import math
import jax
import jax.numpy as jnp
import numpy as np
from jax import lax

CHANNELS = 1024
BASIS = 8
NEIGHBORS = 12
FRAG = 128
GRAPHS = 8
A_DEV = 128
HALO = 32
GROUP_ATOMS = 1024
ATOMS = 4096
N_REPLICA = 4
N_FSDP = 8


def draw_neighbor_src(key, part):
    first_key = jax.random.fold_in(key, 11)
    second_key = jax.random.fold_in(key, 23)
    position = jnp.arange(ATOMS, dtype=jnp.int32) % GROUP_ATOMS
    magnitude = jax.random.randint(first_key, (NEIGHBORS, ATOMS), 1, HALO + 1, dtype=jnp.int32)
    direction = jax.random.randint(second_key, (NEIGHBORS, ATOMS), 0, 2, dtype=jnp.int32) * 2 - 1
    offset = magnitude * direction
    candidate = position[None, :] + offset
    outside = (candidate < 0) | (candidate >= GROUP_ATOMS)
    return jnp.where(outside, position[None, :] - offset, candidate).astype(jnp.int32)


def level_of(own_key, dims, cuts, least, top_value):
    loudness, own = 1.0, jax.random.fold_in(own_key, 6)
    for dim, shards_of in cuts:
        heights = jnp.exp(jax.random.uniform(jax.random.fold_in(own, dim), (shards_of,), jnp.float32, least / len(cuts), top_value / len(cuts)))
        loudness = loudness * jnp.repeat(heights, dims[dim] // shards_of).reshape([-1 if axis == dim else 1 for axis in range(len(dims))])
    return loudness


def split_up(count, total, reach, lean):
    weights = [(1 << 20) // math.isqrt(grade ** lean) + 1 for grade in range(2, count + 1)]
    surplus, holding = total - reach - (count - 1), [1] * (count - 1)
    while surplus > 0:
        candidates = [i for i in range(count - 1) if holding[i] < reach]
        pool, left = sum([weights[i] for i in candidates]), surplus
        for i in candidates:
            more = min(reach - holding[i], max(1, left * weights[i] // pool), surplus)
            holding[i] = holding[i] + more
            surplus = surplus - more
    return np.array([reach] + holding)


def uneven_parts(own_key, count, total, reach, slope):
    if count == 2:
        one = jax.random.randint(own_key, (), max(1, total - reach), min(reach, total - 1) + 1)
        return jnp.stack([one, total - one])
    sizes = jnp.asarray(split_up(count, total, reach, slope), jnp.int32)
    twos = (count - 1) // 2
    source_of, receiver = sizes[1:1 + 2 * twos:2], sizes[2:2 + 2 * twos:2]
    room = jnp.minimum(source_of - 1, reach - receiver)
    moved = jax.random.randint(jax.random.fold_in(own_key, 1), (twos,), 0, 1 << 20) % (room + 1)
    sizes = sizes.at[1:1 + 2 * twos:2].set(source_of - moved).at[2:2 + 2 * twos:2].set(receiver + moved)
    return sizes[jax.random.permutation(jax.random.fold_in(own_key, 2), count)]


def bell_draw(stream_key, shape, scale, limit, cuts=(), held_as=jnp.bfloat16):
    level = level_of(stream_key, shape, cuts, -0.22, 0.18) if cuts else 1.0
    entries = jax.random.normal(stream_key, shape, jnp.float32) * scale * level
    return jnp.minimum(jnp.maximum(entries, -limit), limit).astype(held_as)


def setup_inputs(seed: int = 0) -> dict:
    key_of = jax.random.split(jax.random.key(seed), 10)
    node_feats = bell_draw(key_of[0], (ATOMS, CHANNELS), 1.0, 6.0, ((0, 32),))
    neighbor_src = draw_neighbor_src(jax.random.fold_in(key_of[9], 71), 0)
    distances = jnp.clip(0.8 + 4.2 * jax.random.uniform(key_of[2], (NEIGHBORS, ATOMS), jnp.float32) ** level_of(key_of[2], (NEIGHBORS, ATOMS), ((1, 32),), -0.2, 0.2), 0.8, 5.0)
    graph_ids = jax.vmap(lambda own: jnp.searchsorted(jnp.cumsum(uneven_parts(own, GRAPHS, GROUP_ATOMS, GROUP_ATOMS // 4, 2)), jnp.arange(GROUP_ATOMS), side="right"))(jax.random.split(key_of[3], N_REPLICA)).reshape((N_REPLICA, GROUP_ATOMS)).astype(jnp.int32)
    msg_weight = bell_draw(key_of[4], (CHANNELS, CHANNELS), CHANNELS ** -0.5, 0.1875, ((0, 8),))
    out_weight = bell_draw(key_of[5], (CHANNELS, CHANNELS), CHANNELS ** -0.5, 0.1875, ((0, 8),))
    radial_weight = bell_draw(key_of[6], (BASIS, CHANNELS), 1.0, 6.0, (), jnp.float32)
    cotangent = bell_draw(key_of[7], (ATOMS, CHANNELS), 1.0, 6.0, ((0, 32),))
    fragment = jax.random.randint(key_of[8], (1,), 0, CHANNELS // FRAG).astype(jnp.int32)
    return dict(node_feats=node_feats, neighbor_src=neighbor_src, distances=distances, graph_ids=graph_ids, msg_weight=msg_weight, out_weight=out_weight, radial_weight=radial_weight, cotangent=cotangent, fragment=fragment)


cutoff = 5.0
sharpness = 2.0
tiny = 1e-06

def radial(dist_row, radial_weight):
    basis_count = radial_weight.shape[0]
    centers = cutoff * jnp.arange(basis_count).astype(jnp.float32) / (basis_count - 1)
    envelope = 0.5 * (jnp.cos(jnp.pi * dist_row / cutoff) + 1.0)
    basis = jnp.exp(-sharpness * (dist_row[:, None] - centers[None, :]) ** 2) * envelope[:, None]
    return jnp.dot(basis, radial_weight, precision=lax.Precision.HIGHEST, preferred_element_type=jnp.float32)

def block_grads(left, right):
    left_blocks = left.reshape(N_FSDP, A_DEV, left.shape[1])
    right_blocks = right.reshape(N_FSDP, A_DEV, right.shape[1])

    def step(total, pair):
        partial_sum = lax.dot_general(pair[0], pair[1], (((0,), (0,)), ((), ())), preferred_element_type=jnp.float32)
        rounded = lax.optimization_barrier(partial_sum.astype(jnp.bfloat16))
        return (total + rounded.astype(jnp.float32), None)
    start_total = jnp.zeros((left.shape[1], right.shape[1]), jnp.float32)
    total, _ = lax.scan(step, start_total, (left_blocks, right_blocks))
    return total

def reference(node_feats, neighbor_src, distances, graph_ids, msg_weight, out_weight, radial_weight, cotangent, fragment):
    width = node_feats.shape[1]
    norm = 1.0 / math.sqrt(NEIGHBORS)
    feats_all = node_feats.reshape(N_REPLICA, GROUP_ATOMS, width)
    cot_all = cotangent.reshape(N_REPLICA, GROUP_ATOMS, width)
    src_all = jnp.transpose(neighbor_src.reshape(NEIGHBORS, N_REPLICA, GROUP_ATOMS), (1, 0, 2))
    dist_all = jnp.transpose(distances.reshape(NEIGHBORS, N_REPLICA, GROUP_ATOMS), (1, 0, 2))
    column = (fragment[0] * FRAG).astype(jnp.int32)

    def one_group(inputs):
        feats, src, dist, ids, cot = inputs
        projected = jnp.dot(feats, msg_weight, preferred_element_type=jnp.float32).astype(jnp.bfloat16)

        def gather_step(k, acc):
            rows = jnp.take(projected, src[k], axis=0).astype(jnp.float32)
            return acc + radial(dist[k], radial_weight) * rows
        agg = lax.fori_loop(0, NEIGHBORS, gather_step, jnp.zeros((GROUP_ATOMS, width), jnp.float32)) * norm
        act = jax.nn.silu(agg).astype(jnp.bfloat16)
        node_out = (feats.astype(jnp.float32) + jnp.dot(act, out_weight, preferred_element_type=jnp.float32)).astype(jnp.bfloat16)
        onehot = (ids[:, None] == jnp.arange(GRAPHS, dtype=jnp.int32)[None, :]).astype(jnp.float32)
        count = lax.optimization_barrier(jnp.sum(onehot, axis=0))
        weight = lax.optimization_barrier(jnp.sum(onehot * lax.rsqrt(count)[None, :], axis=1))
        dout = (weight[:, None] * cot.astype(jnp.float32)).astype(jnp.bfloat16)
        out_sum = block_grads(act, dout)
        dact = lax.dot_general(dout, out_weight, (((1,), (1,)), ((), ())), preferred_element_type=jnp.float32)
        sig = jax.nn.sigmoid(agg)
        dagg = dact * sig * (1.0 + agg * (1.0 - sig))

        def spread_step(k, acc):
            return acc.at[src[k]].add(radial(dist[k], radial_weight) * dagg * norm)
        dproj = lax.fori_loop(0, NEIGHBORS, spread_step, jnp.zeros((GROUP_ATOMS, width), jnp.float32)).astype(jnp.bfloat16)
        msg_sum = block_grads(feats, dproj)
        pieces = jnp.stack([lax.dynamic_slice_in_dim(msg_sum, column, FRAG, 1), lax.dynamic_slice_in_dim(out_sum, column, FRAG, 1)])
        scale = (lax.optimization_barrier(jnp.max(jnp.abs(pieces), axis=-1, keepdims=True)) + tiny).astype(jnp.bfloat16)
        code = (pieces / scale.astype(jnp.float32)).astype(jnp.bfloat16)
        terms = scale.astype(jnp.float32) * code.astype(jnp.float32)
        return (node_out, msg_sum.astype(jnp.bfloat16), out_sum.astype(jnp.bfloat16), terms)
    node_out, grad_msg, grad_out, terms = lax.map(one_group, (feats_all, src_all, dist_all, graph_ids, cot_all))
    return (node_out.reshape(N_REPLICA * GROUP_ATOMS, width), grad_msg, grad_out, lax.optimization_barrier(jnp.sum(terms, axis=0)))
```

```python
import functools
import math

import jax
import jax.numpy as jnp
from jax import lax
from jax.experimental import pallas as pl
from jax.experimental.pallas import tpu as pltpu
from jax.sharding import PartitionSpec as P

FRAG = 128
GRAPHS = 8
LANES = 128
SLOT = 16

cutoff = 5.0
sharpness = 2.0
tiny = 1e-06

bf16 = jnp.bfloat16
f32 = jnp.float32


def rows_at(index, count):
    return pl.ds(pl.multiple_of(index * count, count), count)


def column_of(k, neighbors):
    free = SLOT - neighbors
    return (k // free) * SLOT + neighbors + k % free


def pack_kernel(n, width, weight, src, dist, ids, radial_weight, *rest):
    packed, own_radial, (blocks, radials, group) = rest[: n // 2], rest[n // 2], rest[n // 2 + 1 :]
    me = lax.axis_index("fsdp")
    rows = weight.shape[0]
    neighbors, atoms = src.shape
    if width < LANES:
        blocks[...] = jnp.zeros_like(blocks)
        radials[...] = jnp.zeros_like(radials)
    for e in range(n):
        blocks[e, :, :width] = weight[:, e * width : (e + 1) * width]
        radials[e, :, :width] = radial_weight[:, e * width : (e + 1) * width]
    own_radial[...] = radials[me]
    position = lax.broadcasted_iota(jnp.int32, src.shape, 1) + me * atoms
    group[...] = jnp.zeros_like(group)
    group[:neighbors] = (src[...] - position).astype(f32)
    group[neighbors : neighbors + 1] = ids[...].astype(f32)
    meta = [group[...].astype(bf16)]
    group[...] = jnp.ones_like(group)
    group[:neighbors] = dist[...]
    left = group[...]
    for _ in range(3):
        part = left.astype(bf16)
        meta.append(part)
        left = left - part.astype(f32)
    for c in range(n // 2):
        packed[c][:rows] = blocks[me ^ (2 * c)]
        packed[c][rows : 2 * rows] = blocks[me ^ (2 * c + 1)]
        for i, part in enumerate(meta):
            packed[c][2 * rows + i * SLOT : 2 * rows + (i + 1) * SLOT] = part


def fill_filters(neighbors, own_radial, filters, filters_low):
    basis = own_radial.shape[0]
    row = lax.broadcasted_iota(jnp.int32, (basis * SLOT, LANES), 0)
    spread = jnp.concatenate(
        [jnp.broadcast_to(own_radial[b : b + 1], (SLOT, LANES)) for b in range(basis)], axis=0
    )
    high = spread.astype(bf16).astype(f32)
    low = spread - high
    for k in range(neighbors):
        mine = row % SLOT == k
        lanes = slice(k * LANES, (k + 1) * LANES)
        part = jnp.where(mine, high, 0.0).astype(bf16)
        filters[: basis * SLOT, lanes] = part
        filters[basis * SLOT :, lanes] = part
        filters_low[:, lanes] = jnp.where(mine, low, 0.0).astype(bf16)


def filter_block(split, filters, filters_low, out):
    span = 2 * LANES
    half = split.shape[1] // 2

    def step(j, _):
        lanes = pl.ds(pl.multiple_of(j * span, span), span)
        out[:, lanes] = jnp.dot(
            split, filters[:, lanes], preferred_element_type=f32
        ) + jnp.dot(split[:, :half], filters_low[:, lanes], preferred_element_type=f32)
        return 0

    lax.fori_loop(0, out.shape[1] // span, step, 0)


def forward_kernel(n, margin, group_blocks, norm, *refs):
    m = n // 2
    feats, near, far, own_radial = refs[:n], refs[n : n + m], refs[n + m : 2 * n], refs[2 * n]
    outs = refs[2 * n + 1 :]
    sends, (weighted, slope, split, offsets) = outs[:m], outs[m : m + 4]
    (
        weights,
        dists,
        graph_weight,
        stacked,
        columns,
        projected,
        filters,
        filters_low,
        values,
        onehot,
        act,
    ) = outs[m + 4 :]
    me = lax.axis_index("fsdp")
    atoms = feats[0].shape[0]
    basis = own_radial.shape[0]
    neighbors = onehot.shape[0] // (2 * margin)
    rows = weights.shape[0] // n
    fill_filters(neighbors, own_radial, filters, filters_low)

    for d in range(n):
        e = me ^ d
        block = near[d // 2] if d % 2 == 0 else far[d // 2]
        first = (d % 2) * rows
        weights[rows_at(e, rows)] = block[first : first + rows]
        meta = block[2 * rows :].astype(f32)
        offsets[rows_at(e, SLOT)] = meta[:SLOT]
        dists[rows_at(e, SLOT)] = (
            meta[SLOT : 2 * SLOT] + meta[2 * SLOT : 3 * SLOT] + meta[3 * SLOT :]
        )
    slots = lax.broadcasted_iota(jnp.int32, offsets.shape, 0) % SLOT
    ids = jnp.where(slots == neighbors, offsets[...], -1.0)
    weight = jnp.zeros_like(ids)
    for g in range(GRAPHS):
        member = ids == float(g)
        count = jnp.sum(jnp.where(member, 1.0, 0.0), axis=(0, 1), keepdims=True)
        weight = weight + jnp.where(member, lax.rsqrt(jnp.maximum(count, 1.0)), 0.0)
    graph_weight[...] = weight

    def columns_step(e, _):
        dist = dists[rows_at(e, SLOT)]
        envelope = 0.5 * (jnp.cos(jnp.pi * dist / cutoff) + 1.0)
        for b in range(basis):
            center = cutoff * b / (basis - 1)
            stacked[b * SLOT : (b + 1) * SLOT] = (
                jnp.exp(-sharpness * (dist - center) ** 2) * envelope
            )
        offset = offsets[rows_at(e, SLOT)]
        for k in range(neighbors):
            at = column_of(k, neighbors)
            stacked[at : at + 1] = offset[k : k + 1]
        at = column_of(neighbors, neighbors)
        stacked[at : at + 1] = graph_weight[rows_at(e, SLOT)][neighbors : neighbors + 1]
        turned = stacked[...].T
        columns[rows_at(e, atoms)] = turned
        high = turned.astype(bf16)
        split[rows_at(e, atoms), : basis * SLOT] = high
        split[rows_at(e, atoms), basis * SLOT :] = (turned - high.astype(f32)).astype(bf16)
        return 0

    lax.fori_loop(0, n, columns_step, 0)

    projected[...] = jnp.zeros_like(projected)
    for d in range(n):
        e = me ^ d
        start = pl.multiple_of(e * atoms + margin, margin)
        projected[pl.ds(start, atoms)] = jnp.dot(
            feats[d][...], weights[...], preferred_element_type=f32
        ).astype(bf16)

    tile = 2 * margin
    shift = (
        lax.broadcasted_iota(jnp.int32, (tile, 2 * tile), 1)
        - lax.broadcasted_iota(jnp.int32, (tile, 2 * tile), 0)
        - margin
    ).astype(f32)
    span = group_blocks * atoms

    def group_step(group, _):
        filter_block(split[rows_at(group, span)], filters, filters_low, values)

        def tile_step(t, _):
            where = group * (span // tile) + t
            turned = columns[rows_at(where, tile)]
            for k in range(neighbors):
                at = column_of(k, neighbors)
                onehot[k * tile : (k + 1) * tile] = jnp.where(
                    turned[:, at : at + 1] == shift, 1.0, 0.0
                ).astype(bf16)
            window = projected[pl.ds(pl.multiple_of(where * tile, tile), 2 * tile)]
            gathered = jnp.dot(onehot[...], window, preferred_element_type=f32)
            total = jnp.zeros((tile, LANES), f32)
            for k in range(neighbors):
                total = total + (
                    values[rows_at(t, tile), k * LANES : (k + 1) * LANES]
                    * gathered[k * tile : (k + 1) * tile]
                )
            agg = total * norm
            sig = 1.0 / (1.0 + jnp.exp(-agg))
            active = (agg * sig).astype(bf16)
            at = column_of(neighbors, neighbors)
            graph = turned[:, at : at + 1]
            act[rows_at(where, tile)] = active
            weighted[rows_at(where, tile)] = (active.astype(f32) * graph).astype(bf16)
            slope[rows_at(where, tile)] = sig * (1.0 + agg * (1.0 - sig)) * (graph * norm)
            return 0

        lax.fori_loop(0, span // tile, tile_step, 0)
        return 0

    lax.fori_loop(0, n // group_blocks, group_step, 0)
    for c in range(m):
        sends[c][:atoms] = act[rows_at(me ^ (2 * c), atoms)]
        sends[c][atoms:] = act[rows_at(me ^ (2 * c + 1), atoms)]


def backward_kernel(n, margin, group_blocks, *refs):
    m = n // 2
    cots, feats, (out_weight, own_radial, slope, split, offsets) = (
        refs[:n],
        refs[n : 2 * n],
        refs[2 * n : 2 * n + 5],
    )
    sends = refs[2 * n + 5 : 2 * n + 5 + m]
    (rows_padded, dagg, filters, filters_low, values, terms, onehot, spread, turned, grads) = refs[
        2 * n + 5 + m :
    ]
    me = lax.axis_index("fsdp")
    atoms = feats[0].shape[0]
    neighbors = terms.shape[0] // atoms
    rows = out_weight.shape[0]
    fill_filters(neighbors, own_radial, filters, filters_low)
    if rows < LANES:
        rows_padded[...] = jnp.zeros_like(rows_padded)
    rows_padded[:rows] = out_weight[...]
    for d in range(n):
        e = me ^ d
        dact = lax.dot_general(
            cots[d][...],
            rows_padded[...],
            (((1,), (1,)), ((), ())),
            preferred_element_type=f32,
        )
        dagg[rows_at(e, atoms)] = dact * slope[rows_at(e, atoms)]
    spread[...] = jnp.zeros_like(spread)
    reach = atoms + 2 * margin
    shift = (
        lax.broadcasted_iota(jnp.int32, (reach, atoms), 0)
        - lax.broadcasted_iota(jnp.int32, (reach, atoms), 1)
        - margin
    ).astype(f32)
    span = group_blocks * atoms

    def group_step(group, _):
        filter_block(split[rows_at(group, span)], filters, filters_low, values)

        def block_step(i, _):
            e = group * group_blocks + i
            flow = dagg[rows_at(e, atoms)]
            offset = offsets[rows_at(e, SLOT)]
            for k in range(neighbors):
                lanes = slice(k * LANES, (k + 1) * LANES)
                terms[k * atoms : (k + 1) * atoms] = (
                    values[rows_at(i, atoms), lanes] * flow
                ).astype(bf16)
                onehot[:, k * atoms : (k + 1) * atoms] = jnp.where(
                    offset[k : k + 1] == shift, 1.0, 0.0
                ).astype(bf16)
            window = pl.ds(pl.multiple_of(e * atoms, atoms), reach)
            spread[window] += jnp.dot(onehot[...], terms[...], preferred_element_type=f32)
            return 0

        lax.fori_loop(0, group_blocks, block_step, 0)
        return 0

    lax.fori_loop(0, n // group_blocks, group_step, 0)

    for d in range(n):
        e = me ^ d
        start = pl.multiple_of(e * atoms + margin, margin)
        turned[:, d * atoms : (d + 1) * atoms] = spread[pl.ds(start, atoms)].T.astype(bf16)
    total = jnp.zeros((LANES, feats[0].shape[1]), f32)
    for d in range(n):
        total = total + jnp.dot(
            turned[:, d * atoms : (d + 1) * atoms], feats[d][...], preferred_element_type=f32
        )
    for q in range(total.shape[1] // LANES):
        grads[q * LANES : (q + 1) * LANES] = total[:, q * LANES : (q + 1) * LANES].T.astype(bf16)
    for c in range(m):
        sends[c][:rows] = grads[rows_at(me ^ (2 * c), rows)]
        sends[c][rows:] = grads[rows_at(me ^ (2 * c + 1), rows)]


def write_code(piece, code):
    rows = piece.shape[0]
    scale = (jnp.max(jnp.abs(piece), axis=-1, keepdims=True) + tiny).astype(bf16)
    wide = jnp.broadcast_to(scale.astype(f32), piece.shape)
    code[:rows] = (piece / wide).astype(bf16)
    if rows < LANES:
        wide = jnp.concatenate([wide, jnp.zeros((LANES - rows, LANES), f32)], axis=0)
    code[rows:] = wide.T[:SLOT].astype(bf16)


def out_grad_kernel(n, fragment, weighted, *refs):
    cots, grad, code, total = refs[:n], refs[n], refs[n + 1], refs[n + 2]
    me = lax.axis_index("fsdp")
    atoms = cots[0].shape[0]
    rows = grad.shape[1]
    for d in range(n):
        e = me ^ d
        left = weighted[rows_at(e, atoms)].astype(f32).T.astype(bf16)
        term = jnp.dot(left, cots[d][...], preferred_element_type=f32)
        total[...] = term if d == 0 else total[...] + term
    grad[0] = total[:rows].astype(bf16)
    lanes = pl.ds(pl.multiple_of(fragment[0] * FRAG, FRAG), FRAG)
    write_code(total[:rows, lanes], code)


def msg_grad_kernel(n, fragment, *refs):
    m = n // 2
    near, far, grad, code, blocks = refs[:m], refs[m:n], refs[n], refs[n + 1], refs[n + 2]
    me = lax.axis_index("fsdp")
    rows = grad.shape[1]
    width = grad.shape[2] // n
    for c in range(m):
        blocks[me ^ (2 * c)] = near[c][:rows]
        blocks[me ^ (2 * c + 1)] = far[c][rows:]
    for e in range(n):
        grad[0, :, e * width : (e + 1) * width] = blocks[e][:, :width]
    lanes = pl.ds(pl.multiple_of(fragment[0] * FRAG, FRAG), FRAG)
    write_code(grad[0, :, lanes].astype(f32), code)


def node_kernel(n, feats, *refs):
    m = n // 2
    near, far, weights, out = refs[:m], refs[m:n], refs[n : 2 * n], refs[2 * n]
    atoms = feats.shape[0]
    rows = weights[0].shape[0]
    total = feats[...].astype(f32)
    for d in range(n):
        left = near[d // 2][:atoms, :rows] if d % 2 == 0 else far[d // 2][atoms:, :rows]
        total = total + jnp.dot(left, weights[d][...], preferred_element_type=f32)
    out[...] = total.astype(bf16)


def outer_kernel(count, *refs):
    codes, out = refs[: 2 * count], refs[2 * count]
    rows = out.shape[1]
    for piece in range(2):
        total = jnp.zeros((rows, FRAG), f32)
        for r in range(count):
            code = codes[piece * count + r]
            wide = jnp.broadcast_to(code[rows:].astype(f32)[:1], (LANES, LANES)).T
            total = total + wide[:rows] * code[:rows].astype(f32)
        out[piece] = total


def run(kernel, outs, scratch, args, memory=48, scalars=0):
    whole = pl.BlockSpec(memory_space=pltpu.VMEM)
    scalar = pl.BlockSpec(memory_space=pltpu.SMEM)
    return pl.pallas_call(
        kernel,
        out_shape=[jax.ShapeDtypeStruct(shape, dtype) for shape, dtype in outs],
        in_specs=[scalar] * scalars + [whole] * (len(args) - scalars),
        out_specs=[whole] * len(outs),
        scratch_shapes=[pltpu.VMEM(shape, dtype) for shape, dtype in scratch],
        compiler_params=pltpu.CompilerParams(vmem_limit_bytes=memory << 20),
    )(*args)


def hop(value, axis, step):
    count = lax.axis_size(axis)
    return lax.ppermute(value, axis, [(i, i ^ step) for i in range(count)])


def from_chips(sends):
    near = [sends[0]] + [hop(sends[c], "fsdp", 2 * c) for c in range(1, len(sends))]
    return near, [hop(value, "fsdp", 1) for value in near]


def gathered(value, n):
    near, far = from_chips([value] * (n // 2))
    return [piece for pair in zip(near, far) for piece in pair]


def shards(
    node_feats,
    neighbor_src,
    distances,
    graph_ids,
    msg_weight,
    out_weight,
    radial_weight,
    cotangent,
    fragment,
):
    n = lax.axis_size("fsdp")
    replicas = lax.axis_size("replica")
    m = n // 2
    atoms, channels = node_feats.shape
    neighbors = neighbor_src.shape[0]
    basis = radial_weight.shape[0]
    rows = msg_weight.shape[0]
    width = channels // n
    margin = atoms // 4
    norm = 1.0 / math.sqrt(neighbors)
    group_blocks = min(n, 8)
    all_atoms = n * atoms
    lanes = neighbors * LANES
    filter_scratch = [
        ((2 * basis * SLOT, lanes), bf16),
        ((basis * SLOT, lanes), bf16),
        ((group_blocks * atoms, lanes), f32),
    ]

    feats = gathered(node_feats, n)
    *packed, own_radial = run(
        functools.partial(pack_kernel, n, width),
        [((2 * rows + 4 * SLOT, LANES), bf16)] * m + [((basis, LANES), f32)],
        [((n, rows, LANES), bf16), ((n, basis, LANES), f32), ((SLOT, LANES), f32)],
        [msg_weight, neighbor_src, distances, graph_ids, radial_weight],
    )
    near, far = from_chips(packed)
    *act_sends, weighted, slope, split, offsets = run(
        functools.partial(forward_kernel, n, margin, group_blocks, norm),
        [((2 * atoms, LANES), bf16)] * m
        + [
            ((all_atoms, LANES), bf16),
            ((all_atoms, LANES), f32),
            ((all_atoms, 2 * basis * SLOT), bf16),
            ((n * SLOT, LANES), f32),
        ],
        [
            ((channels, LANES), bf16),
            ((n * SLOT, LANES), f32),
            ((n * SLOT, LANES), f32),
            ((basis * SLOT, LANES), f32),
            ((all_atoms, basis * SLOT), f32),
            ((all_atoms + 2 * margin, LANES), bf16),
        ]
        + filter_scratch
        + [((neighbors * 2 * margin, 4 * margin), bf16), ((all_atoms, LANES), bf16)],
        [*feats, *near, *far, own_radial],
    )
    cots = gathered(cotangent, n)
    grad_sends = run(
        functools.partial(backward_kernel, n, margin, group_blocks),
        [((2 * rows, LANES), bf16)] * m,
        [((LANES, channels), bf16), ((all_atoms, LANES), f32)]
        + filter_scratch
        + [
            ((neighbors * atoms, LANES), bf16),
            ((atoms + 2 * margin, neighbors * atoms), bf16),
            ((all_atoms + 2 * margin, LANES), f32),
            ((LANES, all_atoms), bf16),
            ((channels, LANES), bf16),
        ],
        [*cots, *feats, out_weight, own_radial, slope, split, offsets],
    )
    grad_out, out_code = run(
        functools.partial(out_grad_kernel, n),
        [((1, rows, channels), bf16), ((rows + SLOT, FRAG), bf16)],
        [((LANES, channels), f32)],
        [fragment, weighted, *cots],
        scalars=1,
    )
    near, far = from_chips(grad_sends)
    grad_msg, msg_code = run(
        functools.partial(msg_grad_kernel, n),
        [((1, rows, channels), bf16), ((rows + SLOT, FRAG), bf16)],
        [((n, rows, LANES), bf16)],
        [fragment, *near, *far],
        scalars=1,
    )
    near, far = from_chips(act_sends)
    (node_out,) = run(
        functools.partial(node_kernel, n),
        [((atoms, channels), bf16)],
        [],
        [node_feats, *near, *far, *gathered(out_weight, n)],
    )
    codes = [
        piece if d == 0 else hop(piece, "replica", d)
        for piece in (msg_code, out_code)
        for d in range(replicas)
    ]
    (outer_sum,) = run(
        functools.partial(outer_kernel, replicas), [((2, rows, FRAG), f32)], [], codes
    )
    return node_out, grad_msg, grad_out, outer_sum


def solution(mesh):
    placed = (
        P(("replica", "fsdp"), None),
        P(None, ("replica", "fsdp")),
        P(None, ("replica", "fsdp")),
        P("replica", "fsdp"),
        P("fsdp", None),
        P("fsdp", None),
        P(),
        P(("replica", "fsdp"), None),
        P(),
    )
    return jax.shard_map(
        shards,
        mesh=mesh,
        in_specs=placed,
        out_specs=(
            P(("replica", "fsdp"), None),
            P("replica", "fsdp", None),
            P("replica", "fsdp", None),
            P(None, "fsdp", None),
        ),
        check_vma=False,
    )
```

```python
import functools
import math

import jax
import jax.numpy as jnp
from jax import lax
from jax.experimental import pallas as pl
from jax.experimental.pallas import tpu as pltpu
from jax.sharding import PartitionSpec as P

FRAG = 128
GRAPHS = 8
LANES = 128
SLOT = 16

cutoff = 5.0
sharpness = 2.0
tiny = 1e-06

bf16 = jnp.bfloat16
f32 = jnp.float32


def rows_at(index, count):
    return pl.ds(pl.multiple_of(index * count, count), count)


def column_of(k, neighbors):
    free = SLOT - neighbors
    return (k // free) * SLOT + neighbors + k % free


def pack_kernel(n, width, weight, src, dist, ids, radial_weight, *rest):
    packed, own_radial, (blocks, radials, group) = rest[: n // 2], rest[n // 2], rest[n // 2 + 1 :]
    me = lax.axis_index("fsdp")
    rows = weight.shape[0]
    neighbors, atoms = src.shape
    if width < LANES:
        blocks[...] = jnp.zeros_like(blocks)
        radials[...] = jnp.zeros_like(radials)
    for e in range(n):
        blocks[e, :, :width] = weight[:, e * width : (e + 1) * width]
        radials[e, :, :width] = radial_weight[:, e * width : (e + 1) * width]
    own_radial[...] = radials[me]
    position = lax.broadcasted_iota(jnp.int32, src.shape, 1) + me * atoms
    group[...] = jnp.zeros_like(group)
    group[:neighbors] = (src[...] - position).astype(f32)
    group[neighbors : neighbors + 1] = ids[...].astype(f32)
    meta = [group[...].astype(bf16)]
    group[...] = jnp.ones_like(group)
    group[:neighbors] = dist[...]
    left = group[...]
    for _ in range(3):
        part = left.astype(bf16)
        meta.append(part)
        left = left - part.astype(f32)
    for c in range(n // 2):
        packed[c][:rows] = blocks[me ^ (2 * c)]
        packed[c][rows : 2 * rows] = blocks[me ^ (2 * c + 1)]
        for i, part in enumerate(meta):
            packed[c][2 * rows + i * SLOT : 2 * rows + (i + 1) * SLOT] = part


def fill_filters(neighbors, own_radial, filters):
    basis = own_radial.shape[0]
    half = basis * SLOT
    row = lax.broadcasted_iota(jnp.int32, (half, LANES), 0) % SLOT
    spread = jnp.concatenate(
        [jnp.broadcast_to(own_radial[b : b + 1], (SLOT, LANES)) for b in range(basis)], axis=0
    )
    high = spread.astype(bf16).astype(f32)
    low = spread - high
    for k in range(neighbors):
        lanes = slice(k * LANES, (k + 1) * LANES)
        filters[:half, lanes] = jnp.where(row == k, high, 0.0).astype(bf16)
        filters[half:, lanes] = jnp.where(row == k, low, 0.0).astype(bf16)


def fill_values(columns, filters, values):
    high = columns.astype(bf16)
    both = jnp.concatenate([high, high], axis=1)
    span = 2 * LANES

    def step(j, _):
        lanes = pl.ds(pl.multiple_of(j * span, span), span)
        values[:, lanes] = jnp.dot(both, filters[:, lanes], preferred_element_type=f32)
        return 0

    steps = values.shape[1] // span
    lax.fori_loop(0, steps, step, 0, unroll=steps)


def fill_pick(margin, neighbors, turned, pick):
    tile = 2 * margin
    tiles = turned.shape[0] // tile
    shift = (
        lax.broadcasted_iota(jnp.int32, (tile, 2 * tile), 1)
        - lax.broadcasted_iota(jnp.int32, (tile, 2 * tile), 0)
        - margin
    ).astype(f32)
    for t in range(tiles):
        own = turned[t * tile : (t + 1) * tile]
        for k in range(neighbors):
            at = column_of(k, neighbors)
            pick[k * tile : (k + 1) * tile, t * 2 * tile : (t + 1) * 2 * tile] = jnp.where(
                own[:, at : at + 1] == shift, 1.0, 0.0
            ).astype(bf16)


def fill_place(margin, neighbors, offset, place):
    atoms = offset.shape[1]
    shape = (atoms + 2 * margin, atoms)
    shift = (
        lax.broadcasted_iota(jnp.int32, shape, 0)
        - lax.broadcasted_iota(jnp.int32, shape, 1)
        - margin
    ).astype(f32)
    for k in range(neighbors):
        place[:, k * atoms : (k + 1) * atoms] = jnp.where(
            offset[k : k + 1] == shift, 1.0, 0.0
        ).astype(bf16)


def lists_kernel(n, margin, neighbors, ahead, *refs):
    m = n // 2
    near, far, own_radial = refs[:m], refs[m:n], refs[n]
    weights, columns, offsets = refs[n + 1 : n + 4]
    made = refs[n + 4 : n + 7] if ahead else ()
    dists, graph_weight, stacked, filters = refs[n + 4 + len(made) :]
    me = lax.axis_index("fsdp")
    basis = own_radial.shape[0]
    rows = weights.shape[0] // n
    atoms = columns.shape[0] // n
    for d in range(n):
        e = me ^ d
        block = near[d // 2] if d % 2 == 0 else far[d // 2]
        first = (d % 2) * rows
        weights[rows_at(e, rows)] = block[first : first + rows]
        meta = block[2 * rows :].astype(f32)
        offsets[rows_at(e, SLOT)] = meta[:SLOT]
        dists[rows_at(e, SLOT)] = (
            meta[SLOT : 2 * SLOT] + meta[2 * SLOT : 3 * SLOT] + meta[3 * SLOT :]
        )
    slots = lax.broadcasted_iota(jnp.int32, offsets.shape, 0) % SLOT
    ids = jnp.where(slots == neighbors, offsets[...], -1.0)
    weight = jnp.zeros_like(ids)
    for g in range(GRAPHS):
        member = ids == float(g)
        count = jnp.sum(jnp.where(member, 1.0, 0.0), axis=(0, 1), keepdims=True)
        weight = weight + jnp.where(member, lax.rsqrt(jnp.maximum(count, 1.0)), 0.0)
    graph_weight[...] = weight

    def columns_step(e, _):
        dist = dists[rows_at(e, SLOT)]
        envelope = 0.5 * (jnp.cos(jnp.pi * dist / cutoff) + 1.0)
        own = stacked.at[e % stacked.shape[0]]
        for b in range(basis):
            center = cutoff * b / (basis - 1)
            own[b * SLOT : (b + 1) * SLOT] = jnp.exp(-sharpness * (dist - center) ** 2) * envelope
        offset = offsets[rows_at(e, SLOT)]
        for k in range(neighbors):
            at = column_of(k, neighbors)
            own[at : at + 1] = offset[k : k + 1]
        at = column_of(neighbors, neighbors)
        own[at : at + 1] = graph_weight[rows_at(e, SLOT)][neighbors : neighbors + 1]
        columns[rows_at(e, atoms)] = own[...].T
        return 0

    lax.fori_loop(0, n, columns_step, 0, unroll=stacked.shape[0])
    if ahead:
        values, pick, place = made
        fill_filters(neighbors, own_radial, filters)
        fill_values(columns[...], filters, values)

        def block_step(e, _):
            span = neighbors * 2 * margin
            fill_pick(margin, neighbors, columns[rows_at(e, atoms)], pick.at[rows_at(e, span)])
            fill_place(
                margin,
                neighbors,
                offsets[rows_at(e, SLOT)],
                place.at[rows_at(e, atoms + 2 * margin)],
            )
            return 0

        lax.fori_loop(0, n, block_step, 0, unroll=2)


def block_diagonal(first, second):
    zero = jnp.zeros_like(first)
    return jnp.concatenate(
        [jnp.concatenate([first, zero], axis=1), jnp.concatenate([zero, second], axis=1)], axis=0
    )


def forward_kernel(n, margin, neighbors, norm, ahead, *refs):
    feats, (weights, columns, own_radial) = refs[:n], refs[n : n + 3]
    made = refs[n + 3 : n + 5] if ahead else ()
    keep, give, weighted, slope, projected = refs[n + 3 + len(made) : n + 8 + len(made)]
    scratch = refs[n + 8 + len(made) :]
    me = lax.axis_index("fsdp")
    core = me % 2
    atoms = feats[0].shape[0]
    projected[:margin] = jnp.zeros_like(projected[:margin])
    projected[n * atoms + margin :] = jnp.zeros_like(projected[:margin])
    for d in range(n):
        e = me ^ d
        start = pl.multiple_of(e * atoms + margin, margin)
        projected[pl.ds(start, atoms)] = jnp.dot(
            feats[d][...], weights[...], preferred_element_type=f32
        ).astype(bf16)
    if ahead:
        values, pick = made
    else:
        filters, values, pick = scratch
        fill_filters(neighbors, own_radial, filters)
    tile = 2 * margin
    span = neighbors * tile

    def block_step(e, _):
        turned = columns[rows_at(e, atoms)]
        if ahead:
            own_values = values.at[rows_at(e, atoms)]
            own_pick = pick[rows_at(e, span)]
        else:
            own_values = values
            fill_values(turned, filters, values)
            fill_pick(margin, neighbors, turned, pick)
            own_pick = pick[...]
        start = pl.multiple_of(e * atoms, atoms)
        windows = [projected[pl.ds(start + t * tile, 2 * tile)] for t in range(2)]
        found = jnp.dot(own_pick, block_diagonal(*windows), preferred_element_type=f32)
        halves = []
        for t in range(2):
            total = jnp.zeros((tile, LANES), f32)
            for k in range(neighbors):
                total = total + (
                    own_values[t * tile : (t + 1) * tile, k * LANES : (k + 1) * LANES]
                    * found[k * tile : (k + 1) * tile, t * LANES : (t + 1) * LANES]
                )
            halves.append(total)
        agg = jnp.concatenate(halves, axis=0) * norm
        sig = 1.0 / (1.0 + jnp.exp(-agg))
        active = (agg * sig).astype(bf16)
        at = column_of(neighbors, neighbors)
        graph = turned[:, at : at + 1]
        weighted[rows_at(e, atoms)] = (active.astype(f32) * graph).astype(bf16)
        slope[rows_at(e, atoms)] = sig * (1.0 + agg * (1.0 - sig)) * (graph * norm)

        @pl.when(e % 2 == core)
        def _():
            keep[rows_at(e // 2, atoms)] = active

        @pl.when(e % 2 != core)
        def _():
            give[rows_at(e // 2, atoms)] = active

        return 0

    lax.fori_loop(0, n, block_step, 0, unroll=min(n, 8) if ahead else 1)


def backward_kernel(n, margin, neighbors, ahead, *refs):
    m = n // 2
    cots, feats, (out_weight, own_radial, slope, columns, offsets) = (
        refs[:n],
        refs[n : 2 * n],
        refs[2 * n : 2 * n + 5],
    )
    made = refs[2 * n + 5 : 2 * n + 7] if ahead else ()
    refs = refs[2 * n + 5 + len(made) :]
    sends, (rows_padded, dagg, terms, spread, turned, grads) = refs[:m], refs[m : m + 6]
    scratch = refs[m + 6 :]
    me = lax.axis_index("fsdp")
    atoms = feats[0].shape[0]
    rows = out_weight.shape[0]
    if rows < LANES:
        rows_padded[...] = jnp.zeros_like(rows_padded)
    rows_padded[:rows] = out_weight[...]
    for d in range(n):
        e = me ^ d
        dact = lax.dot_general(
            cots[d][...],
            rows_padded[...],
            (((1,), (1,)), ((), ())),
            preferred_element_type=f32,
        )
        dagg[rows_at(e, atoms)] = dact * slope[rows_at(e, atoms)]
    spread[...] = jnp.zeros_like(spread)
    reach = atoms + 2 * margin
    if ahead:
        values, place = made
    else:
        filters, values, place = scratch
        fill_filters(neighbors, own_radial, filters)

    def block_step(e, _):
        flow = dagg[rows_at(e, atoms)]
        if ahead:
            own_values = values.at[rows_at(e, atoms)]
            own_place = place[rows_at(e, reach)]
        else:
            own_values = values
            fill_values(columns[rows_at(e, atoms)], filters, values)
            fill_place(margin, neighbors, offsets[rows_at(e, SLOT)], place)
            own_place = place[...]
        own = terms.at[e % terms.shape[0]]
        for k in range(neighbors):
            own[k * atoms : (k + 1) * atoms] = (
                own_values[:, k * LANES : (k + 1) * LANES] * flow
            ).astype(bf16)
        window = pl.ds(pl.multiple_of(e * atoms, atoms), reach)
        spread[window] += jnp.dot(own_place, own[...], preferred_element_type=f32)
        return 0

    lax.fori_loop(0, n, block_step, 0, unroll=min(n, 8) if ahead else 1)

    for d in range(n):
        e = me ^ d
        start = pl.multiple_of(e * atoms + margin, margin)
        turned[:, d * atoms : (d + 1) * atoms] = spread[pl.ds(start, atoms)].T.astype(bf16)
    total = jnp.zeros((LANES, feats[0].shape[1]), f32)
    for d in range(n):
        total = total + jnp.dot(
            turned[:, d * atoms : (d + 1) * atoms], feats[d][...], preferred_element_type=f32
        )
    for q in range(total.shape[1] // LANES):
        grads[q * LANES : (q + 1) * LANES] = total[:, q * LANES : (q + 1) * LANES].T.astype(bf16)
    for c in range(m):
        sends[c][:rows] = grads[rows_at(me ^ (2 * c), rows)]
        sends[c][rows:] = grads[rows_at(me ^ (2 * c + 1), rows)]


def write_code(piece, code):
    rows = piece.shape[0]
    scale = (jnp.max(jnp.abs(piece), axis=-1, keepdims=True) + tiny).astype(bf16)
    wide = jnp.broadcast_to(scale.astype(f32), piece.shape)
    code[:rows] = (piece / wide).astype(bf16)
    if rows < LANES:
        wide = jnp.concatenate([wide, jnp.zeros((LANES - rows, LANES), f32)], axis=0)
    code[rows:] = wide.T[:SLOT].astype(bf16)


def out_grad_kernel(n, fragment, weighted, *refs):
    cots, grad, code, total = refs[:n], refs[n], refs[n + 1], refs[n + 2]
    me = lax.axis_index("fsdp")
    atoms = cots[0].shape[0]
    rows = grad.shape[1]
    for d in range(n):
        e = me ^ d
        left = weighted[rows_at(e, atoms)].astype(f32).T.astype(bf16)
        term = jnp.dot(left, cots[d][...], preferred_element_type=f32)
        total[...] = term if d == 0 else total[...] + term
    grad[0] = total[:rows].astype(bf16)
    lanes = pl.ds(pl.multiple_of(fragment[0] * FRAG, FRAG), FRAG)
    write_code(total[:rows, lanes], code)


def msg_grad_kernel(n, fragment, *refs):
    m = n // 2
    near, far, grad, code, blocks = refs[:m], refs[m:n], refs[n], refs[n + 1], refs[n + 2]
    me = lax.axis_index("fsdp")
    rows = grad.shape[1]
    width = grad.shape[2] // n
    for c in range(m):
        blocks[me ^ (2 * c)] = near[c][:rows]
        blocks[me ^ (2 * c + 1)] = far[c][rows:]
    for e in range(n):
        grad[0, :, e * width : (e + 1) * width] = blocks[e][:, :width]
    lanes = pl.ds(pl.multiple_of(fragment[0] * FRAG, FRAG), FRAG)
    write_code(grad[0, :, lanes].astype(f32), code)


def partial_kernel(n, width, keep, got, own_weight, other_weight, *sends):
    me = lax.axis_index("fsdp")
    atoms = keep.shape[0] // (n // 2)
    for c in range(n // 2):
        block = rows_at((me // 2) ^ c, atoms)
        sends[c][...] = (
            jnp.dot(keep[block][:, :width], own_weight[...], preferred_element_type=f32)
            + jnp.dot(got[block][:, :width], other_weight[...], preferred_element_type=f32)
        ).astype(bf16)


def node_kernel(feats, *refs):
    parts, out = refs[:-1], refs[-1]
    total = feats[...].astype(f32)
    for part in parts:
        total = total + part[...].astype(f32)
    out[...] = total.astype(bf16)


def outer_kernel(count, *refs):
    codes, out = refs[: 2 * count], refs[2 * count]
    rows = out.shape[1]
    for piece in range(2):
        total = jnp.zeros((rows, FRAG), f32)
        for r in range(count):
            code = codes[piece * count + r]
            wide = jnp.broadcast_to(code[rows:].astype(f32)[:1], (LANES, LANES)).T
            total = total + wide[:rows] * code[:rows].astype(f32)
        out[piece] = total


def run(kernel, outs, scratch, args, micros, memory=16, scalars=0):
    whole = pl.BlockSpec(memory_space=pltpu.VMEM)
    scalar = pl.BlockSpec(memory_space=pltpu.SMEM)
    return pl.pallas_call(
        kernel,
        out_shape=[jax.ShapeDtypeStruct(shape, dtype) for shape, dtype in outs],
        in_specs=[scalar] * scalars + [whole] * (len(args) - scalars),
        out_specs=[whole] * len(outs),
        scratch_shapes=[pltpu.VMEM(shape, dtype) for shape, dtype in scratch],
        compiler_params=pltpu.CompilerParams(vmem_limit_bytes=memory << 20),
        cost_estimate=pl.CostEstimate(
            flops=int(micros * 1e9), bytes_accessed=int(micros * 3e6), transcendentals=0
        ),
    )(*args)


def hop(value, axis, step):
    count = lax.axis_size(axis)
    return lax.ppermute(value, axis, [(i, i ^ step) for i in range(count)])


def from_chips(sends):
    near = [sends[0]] + [hop(sends[c], "fsdp", 2 * c) for c in range(1, len(sends))]
    return near, [hop(value, "fsdp", 1) for value in near]


def gathered(value, n):
    near, far = from_chips([value] * (n // 2))
    return [piece for pair in zip(near, far) for piece in pair]


def shards(
    node_feats,
    neighbor_src,
    distances,
    graph_ids,
    msg_weight,
    out_weight,
    radial_weight,
    cotangent,
    fragment,
):
    n = lax.axis_size("fsdp")
    replicas = lax.axis_size("replica")
    m = n // 2
    atoms, channels = node_feats.shape
    neighbors = neighbor_src.shape[0]
    basis = radial_weight.shape[0]
    rows = msg_weight.shape[0]
    width = channels // n
    margin = atoms // 4
    reach = atoms + 2 * margin
    norm = 1.0 / math.sqrt(neighbors)
    all_atoms = n * atoms
    lanes = neighbors * LANES
    ahead = all_atoms * lanes * 4 <= 8 << 20
    memory = 24 if ahead else 56
    step_scratch = [
        ((2 * basis * SLOT, lanes), bf16),
        ((atoms, lanes), f32),
    ]

    feats = gathered(node_feats, n)
    *packed, own_radial = run(
        functools.partial(pack_kernel, n, width),
        [((2 * rows + 4 * SLOT, LANES), bf16)] * m + [((basis, LANES), f32)],
        [((n, rows, LANES), bf16), ((n, basis, LANES), f32), ((SLOT, LANES), f32)],
        [msg_weight, neighbor_src, distances, graph_ids, radial_weight],
        1,
    )
    near, far = from_chips(packed)
    weights, columns, offsets, *made = run(
        functools.partial(lists_kernel, n, margin, neighbors, ahead),
        [
            ((channels, LANES), bf16),
            ((all_atoms, LANES), f32),
            ((n * SLOT, LANES), f32),
        ]
        + [
            ((all_atoms, lanes), f32),
            ((n * neighbors * 2 * margin, 8 * margin), bf16),
            ((n * reach, neighbors * atoms), bf16),
        ]
        * ahead,
        [
            ((n * SLOT, LANES), f32),
            ((n * SLOT, LANES), f32),
            ((min(n, 8), basis * SLOT, LANES), f32),
            ((2 * basis * SLOT, lanes), bf16),
        ],
        [*near, *far, own_radial],
        6,
        memory,
    )
    keep, give, weighted, slope = run(
        functools.partial(forward_kernel, n, margin, neighbors, norm, ahead),
        [
            ((all_atoms // 2, LANES), bf16),
            ((all_atoms // 2, LANES), bf16),
            ((all_atoms, LANES), bf16),
            ((all_atoms, LANES), f32),
        ],
        [((all_atoms + 2 * margin, LANES), bf16)]
        + (step_scratch + [((neighbors * 2 * margin, 8 * margin), bf16)]) * (not ahead),
        [*feats, weights, columns, own_radial, *made[:2]],
        4,
        memory,
    )
    cots = gathered(cotangent, n)
    grad_sends = run(
        functools.partial(backward_kernel, n, margin, neighbors, ahead),
        [((2 * rows, LANES), bf16)] * m,
        [
            ((LANES, channels), bf16),
            ((all_atoms, LANES), f32),
            ((min(n, 8) if ahead else 1, neighbors * atoms, LANES), bf16),
            ((all_atoms + 2 * margin, LANES), f32),
            ((LANES, all_atoms), bf16),
            ((channels, LANES), bf16),
        ]
        + (step_scratch + [((reach, neighbors * atoms), bf16)]) * (not ahead),
        [*cots, *feats, out_weight, own_radial, slope, columns, offsets, *made[::2]],
        4,
        memory,
    )
    grad_out, out_code = run(
        functools.partial(out_grad_kernel, n),
        [((1, rows, channels), bf16), ((rows + SLOT, FRAG), bf16)],
        [((LANES, channels), f32)],
        [fragment, weighted, *cots],
        1,
        memory,
        scalars=1,
    )
    near, far = from_chips(grad_sends)
    grad_msg, msg_code = run(
        functools.partial(msg_grad_kernel, n),
        [((1, rows, channels), bf16), ((rows + SLOT, FRAG), bf16)],
        [((n, rows, LANES), bf16)],
        [fragment, *near, *far],
        1,
        memory,
        scalars=1,
    )
    sums = run(
        functools.partial(partial_kernel, n, width),
        [((atoms, channels), bf16)] * m,
        [],
        [keep, hop(give, "fsdp", 1), out_weight, hop(out_weight, "fsdp", 1)],
        1,
        memory,
    )
    (node_out,) = run(
        node_kernel,
        [((atoms, channels), bf16)],
        [],
        [node_feats, sums[0]] + [hop(sums[c], "fsdp", 2 * c) for c in range(1, m)],
        1,
        memory,
    )
    codes = [
        piece if d == 0 else hop(piece, "replica", d)
        for piece in (msg_code, out_code)
        for d in range(replicas)
    ]
    (outer_sum,) = run(
        functools.partial(outer_kernel, replicas), [((2, rows, FRAG), f32)], [], codes, 1, memory
    )
    return node_out, grad_msg, grad_out, outer_sum


def solution(mesh):
    placed = (
        P(("replica", "fsdp"), None),
        P(None, ("replica", "fsdp")),
        P(None, ("replica", "fsdp")),
        P("replica", "fsdp"),
        P("fsdp", None),
        P("fsdp", None),
        P(),
        P(("replica", "fsdp"), None),
        P(),
    )
    return jax.shard_map(
        shards,
        mesh=mesh,
        in_specs=placed,
        out_specs=(
            P(("replica", "fsdp"), None),
            P("replica", "fsdp", None),
            P("replica", "fsdp", None),
            P(None, "fsdp", None),
        ),
        check_vma=False,
    )
```

```python
import functools
import math

import jax
import jax.numpy as jnp
from jax import lax
from jax.experimental import pallas as pl
from jax.experimental.pallas import tpu as pltpu
from jax.sharding import PartitionSpec as P

FRAG = 128
GRAPHS = 8
LANES = 128
SLOT = 16

cutoff = 5.0
sharpness = 2.0
tiny = 1e-06

bf16 = jnp.bfloat16
f32 = jnp.float32


def rows_at(index, count):
    return pl.ds(pl.multiple_of(index * count, count), count)


def column_of(k, neighbors):
    free = SLOT - neighbors
    return (k // free) * SLOT + neighbors + k % free


def pack_kernel(n, width, *refs):
    far, refs = refs[:5], refs[5:]
    packed, own_radial, (blocks, radials, group) = refs[: n // 2], refs[n // 2], refs[n // 2 + 1 : n // 2 + 4]
    held, done = refs[n // 2 + 4 : n // 2 + 9], refs[n // 2 + 9]
    copies = [pltpu.make_async_copy(a, b, done.at[i]) for i, (a, b) in enumerate(zip(far, held))]
    for copy in copies:
        copy.start()
    for copy in copies:
        copy.wait()
    weight, src, dist, ids, radial_weight = held
    me = lax.axis_index("fsdp")
    rows = weight.shape[0]
    neighbors, atoms = src.shape
    if width < LANES:
        blocks[...] = jnp.zeros_like(blocks)
        radials[...] = jnp.zeros_like(radials)
    for e in range(n):
        blocks[e, :, :width] = weight[:, e * width : (e + 1) * width]
        radials[e, :, :width] = radial_weight[:, e * width : (e + 1) * width]
    own_radial[...] = radials[me]
    position = lax.broadcasted_iota(jnp.int32, src.shape, 1) + me * atoms
    group[...] = jnp.zeros_like(group)
    group[:neighbors] = (src[...] - position).astype(f32)
    group[neighbors : neighbors + 1] = ids[...].astype(f32)
    meta = [group[...].astype(bf16)]
    group[...] = jnp.ones_like(group)
    group[:neighbors] = dist[...]
    left = group[...]
    for _ in range(3):
        part = left.astype(bf16)
        meta.append(part)
        left = left - part.astype(f32)
    for c in range(n // 2):
        packed[c][:rows] = blocks[me ^ (2 * c)]
        packed[c][rows : 2 * rows] = blocks[me ^ (2 * c + 1)]
        for i, part in enumerate(meta):
            packed[c][2 * rows + i * SLOT : 2 * rows + (i + 1) * SLOT] = part


def merge_kernel(m, *refs):
    parts, out = refs[:m], refs[-1]
    rows = parts[0].shape[0]
    for c, part in enumerate(parts):
        out[c * rows : (c + 1) * rows] = part[...]


def gate_kernel(_value, _after, _out):
    pass


def fill_filters(neighbors, own_radial, filters):
    basis = own_radial.shape[0]
    half = basis * SLOT
    row = lax.broadcasted_iota(jnp.int32, (half, LANES), 0) % SLOT
    spread = jnp.concatenate(
        [jnp.broadcast_to(own_radial[b : b + 1], (SLOT, LANES)) for b in range(basis)], axis=0
    )
    high = spread.astype(bf16).astype(f32)
    low = spread - high
    for k in range(neighbors):
        lanes = slice(k * LANES, (k + 1) * LANES)
        filters[:half, lanes] = jnp.where(row == k, high, 0.0).astype(bf16)
        filters[half:, lanes] = jnp.where(row == k, low, 0.0).astype(bf16)


def fill_values(columns, filters, values):
    high = columns.astype(bf16)
    both = jnp.concatenate([high, high], axis=1)
    span = 2 * LANES

    def step(j, _):
        lanes = pl.ds(pl.multiple_of(j * span, span), span)
        values[:, lanes] = jnp.dot(both, filters[:, lanes], preferred_element_type=f32)
        return 0

    steps = values.shape[1] // span
    lax.fori_loop(0, steps, step, 0, unroll=steps)


def fill_pick(margin, neighbors, turned, pick):
    tile = 2 * margin
    tiles = turned.shape[0] // tile
    shift = (
        lax.broadcasted_iota(jnp.int32, (tile, 2 * tile), 1)
        - lax.broadcasted_iota(jnp.int32, (tile, 2 * tile), 0)
        - margin
    ).astype(f32)
    for t in range(tiles):
        own = turned[t * tile : (t + 1) * tile]
        for k in range(neighbors):
            at = column_of(k, neighbors)
            pick[k * tile : (k + 1) * tile, t * 2 * tile : (t + 1) * 2 * tile] = jnp.where(
                own[:, at : at + 1] == shift, 1.0, 0.0
            ).astype(bf16)


def fill_place(margin, neighbors, offset, place):
    atoms = offset.shape[1]
    shape = (atoms + 2 * margin, atoms)
    shift = (
        lax.broadcasted_iota(jnp.int32, shape, 0)
        - lax.broadcasted_iota(jnp.int32, shape, 1)
        - margin
    ).astype(f32)
    for k in range(neighbors):
        place[:, k * atoms : (k + 1) * atoms] = jnp.where(
            offset[k : k + 1] == shift, 1.0, 0.0
        ).astype(bf16)


def lists_kernel(n, margin, neighbors, ahead, *refs):
    m = n // 2
    near, far, own_radial = refs[:m], refs[m], refs[m + 1]
    weights, columns, offsets = refs[m + 2 : m + 5]
    made = refs[m + 5 : m + 8] if ahead else ()
    dists, graph_weight, stacked, filters = refs[m + 5 + len(made) :]
    me = lax.axis_index("fsdp")
    basis = own_radial.shape[0]
    rows = weights.shape[0] // n
    atoms = columns.shape[0] // n
    for d in range(n):
        e = me ^ d
        head = 2 * rows + 4 * SLOT
        block = near[d // 2] if d % 2 == 0 else far.at[d // 2 * head : (d // 2 + 1) * head]
        weights[rows_at(e, rows), d % 2 * LANES : (d % 2 + 1) * LANES] = block[:rows]
        weights[rows_at(e, rows), (1 - d % 2) * LANES : (2 - d % 2) * LANES] = block[
            rows : 2 * rows
        ]
        meta = block[2 * rows :].astype(f32)
        offsets[rows_at(e, SLOT)] = meta[:SLOT]
        dists[rows_at(e, SLOT)] = (
            meta[SLOT : 2 * SLOT] + meta[2 * SLOT : 3 * SLOT] + meta[3 * SLOT :]
        )
    slots = lax.broadcasted_iota(jnp.int32, offsets.shape, 0) % SLOT
    ids = jnp.where(slots == neighbors, offsets[...], -1.0)
    weight = jnp.zeros_like(ids)
    for g in range(GRAPHS):
        member = ids == float(g)
        count = jnp.sum(jnp.where(member, 1.0, 0.0), axis=(0, 1), keepdims=True)
        weight = weight + jnp.where(member, lax.rsqrt(jnp.maximum(count, 1.0)), 0.0)
    graph_weight[...] = weight

    def columns_step(e, _):
        dist = dists[rows_at(e, SLOT)]
        envelope = 0.5 * (jnp.cos(jnp.pi * dist / cutoff) + 1.0)
        own = stacked.at[e % stacked.shape[0]]
        for b in range(basis):
            center = cutoff * b / (basis - 1)
            own[b * SLOT : (b + 1) * SLOT] = jnp.exp(-sharpness * (dist - center) ** 2) * envelope
        offset = offsets[rows_at(e, SLOT)]
        for k in range(neighbors):
            at = column_of(k, neighbors)
            own[at : at + 1] = offset[k : k + 1]
        at = column_of(neighbors, neighbors)
        own[at : at + 1] = graph_weight[rows_at(e, SLOT)][neighbors : neighbors + 1]
        columns[rows_at(e, atoms)] = own[...].T
        return 0

    lax.fori_loop(0, n, columns_step, 0, unroll=stacked.shape[0])
    if ahead:
        values, pick, place = made
        fill_filters(neighbors, own_radial, filters)
        fill_values(columns[...], filters, values)

        def block_step(e, _):
            span = neighbors * 2 * margin
            fill_pick(margin, neighbors, columns[rows_at(e, atoms)], pick.at[rows_at(e, span)])
            fill_place(
                margin,
                neighbors,
                offsets[rows_at(e, SLOT)],
                place.at[rows_at(e, atoms + 2 * margin)],
            )
            return 0

        lax.fori_loop(0, n, block_step, 0, unroll=2)


def block_diagonal(first, second):
    zero = jnp.zeros_like(first)
    return jnp.concatenate(
        [jnp.concatenate([first, zero], axis=1), jnp.concatenate([zero, second], axis=1)], axis=0
    )


def products_kernel(n, weights, own_weight, other_weight, *refs):
    m = n // 2
    feats, cots, (keep, give, held_feats, both) = refs[:m], refs[m : 2 * m], refs[2 * m :]
    me = lax.axis_index("fsdp")
    atoms = feats[0].shape[0]
    half = m * atoms
    rows = own_weight.shape[0]
    if rows < LANES:
        both[...] = jnp.zeros_like(both)
    both[:rows] = own_weight[...]
    both[LANES : LANES + rows] = other_weight[...]
    for c in range(m):
        held_feats[c * atoms : (c + 1) * atoms] = feats[c][...]
        projected = jnp.dot(
            feats[c][...], weights[...], preferred_element_type=f32
        ).astype(bf16)
        dact = lax.dot_general(
            cots[c][...], both[...], (((1,), (1,)), ((), ())), preferred_element_type=f32
        ).astype(bf16)
        chip = (me // 2) ^ c
        keep[rows_at(chip, atoms)] = projected[:, :LANES]
        give[rows_at(chip, atoms)] = projected[:, LANES:]
        keep[rows_at(chip + m, atoms)] = dact[:, :LANES]
        give[rows_at(chip + m, atoms)] = dact[:, LANES:]


def forward_kernel(n, margin, neighbors, norm, ahead, *refs):
    own, got, columns, own_radial = refs[:4]
    made = refs[4:6] if ahead else ()
    keep, give, dagg, projected = refs[4 + len(made) : 8 + len(made)]
    scratch = refs[8 + len(made) :]
    me = lax.axis_index("fsdp")
    core = me % 2
    atoms = columns.shape[0] // n
    half = n // 2 * atoms
    projected[:margin] = jnp.zeros_like(projected[:margin])
    projected[n * atoms + margin :] = jnp.zeros_like(projected[:margin])
    for c in range(n // 2):
        for source, parity in ((own, core), (got, 1 - core)):
            start = pl.multiple_of((2 * c + parity) * atoms + margin, margin)
            projected[pl.ds(start, atoms)] = source[c * atoms : (c + 1) * atoms]
            dact = source[half + c * atoms : half + (c + 1) * atoms]
            dagg[rows_at(2 * c + parity, atoms)] = dact.astype(f32)
    if ahead:
        values, pick = made
    else:
        filters, values, pick = scratch
        fill_filters(neighbors, own_radial, filters)
    tile = 2 * margin
    span = neighbors * tile

    def block_step(e, _):
        turned = columns[rows_at(e, atoms)]
        if ahead:
            own_values = values.at[rows_at(e, atoms)]
            own_pick = pick[rows_at(e, span)]
        else:
            own_values = values
            fill_values(turned, filters, values)
            fill_pick(margin, neighbors, turned, pick)
            own_pick = pick[...]
        start = pl.multiple_of(e * atoms, atoms)
        windows = [projected[pl.ds(start + t * tile, 2 * tile)] for t in range(2)]
        found = jnp.dot(own_pick, block_diagonal(*windows), preferred_element_type=f32)
        halves = []
        for t in range(2):
            total = jnp.zeros((tile, LANES), f32)
            for k in range(neighbors):
                total = total + (
                    own_values[t * tile : (t + 1) * tile, k * LANES : (k + 1) * LANES]
                    * found[k * tile : (k + 1) * tile, t * LANES : (t + 1) * LANES]
                )
            halves.append(total)
        agg = jnp.concatenate(halves, axis=0) * norm
        sig = 1.0 / (1.0 + jnp.exp(-agg))
        active = (agg * sig).astype(bf16)
        at = column_of(neighbors, neighbors)
        graph = turned[:, at : at + 1]
        slope = sig * (1.0 + agg * (1.0 - sig)) * (graph * norm)
        dagg[rows_at(e, atoms)] = dagg[rows_at(e, atoms)] * slope

        @pl.when(e % 2 == core)
        def _():
            keep[rows_at(e // 2, atoms)] = active

        @pl.when(e % 2 != core)
        def _():
            give[rows_at(e // 2, atoms)] = active

        return 0

    lax.fori_loop(0, n, block_step, 0, unroll=min(n, 8) if ahead else 1)


def backward_kernel(n, margin, neighbors, channels, ahead, *refs):
    m = n // 2
    feats, (dagg, own_radial, columns, offsets) = refs[:2], refs[2:6]
    made = refs[6:8] if ahead else ()
    refs = refs[6 + len(made) :]
    sends, (terms, spread, turned, grads) = refs[:m], refs[m : m + 4]
    scratch = refs[m + 4 :]
    me = lax.axis_index("fsdp")
    atoms = columns.shape[0] // n
    rows = channels // n
    spread[...] = jnp.zeros_like(spread)
    reach = atoms + 2 * margin
    if ahead:
        values, place = made
    else:
        filters, values, place = scratch
        fill_filters(neighbors, own_radial, filters)

    def block_step(e, _):
        flow = dagg[rows_at(e, atoms)]
        if ahead:
            own_values = values.at[rows_at(e, atoms)]
            own_place = place[rows_at(e, reach)]
        else:
            own_values = values
            fill_values(columns[rows_at(e, atoms)], filters, values)
            fill_place(margin, neighbors, offsets[rows_at(e, SLOT)], place)
            own_place = place[...]
        own = terms.at[e % terms.shape[0]]
        for k in range(neighbors):
            own[k * atoms : (k + 1) * atoms] = (
                own_values[:, k * LANES : (k + 1) * LANES] * flow
            ).astype(bf16)
        window = pl.ds(pl.multiple_of(e * atoms, atoms), reach)
        spread[window] += jnp.dot(own_place, own[...], preferred_element_type=f32)
        return 0

    lax.fori_loop(0, n, block_step, 0, unroll=min(n, 8) if ahead else 1)

    half = m * atoms
    for k in range(2):
        for c in range(m):
            e = me ^ (2 * c + k)
            start = pl.multiple_of(e * atoms + margin, margin)
            turned[:, k * half + c * atoms : k * half + (c + 1) * atoms] = (
                spread[pl.ds(start, atoms)].T.astype(bf16)
            )
    total = jnp.dot(turned[:, :half], feats[0][...], preferred_element_type=f32)
    total = total + jnp.dot(turned[:, half:], feats[1][...], preferred_element_type=f32)
    for q in range(total.shape[1] // LANES):
        grads[q * LANES : (q + 1) * LANES] = total[:, q * LANES : (q + 1) * LANES].T.astype(bf16)
    for c in range(m):
        sends[c][:rows] = grads[rows_at(me ^ (2 * c), rows)]
        sends[c][rows:] = grads[rows_at(me ^ (2 * c + 1), rows)]


def write_code(piece, code):
    rows = piece.shape[0]
    scale = (jnp.max(jnp.abs(piece), axis=-1, keepdims=True) + tiny).astype(bf16)
    wide = jnp.broadcast_to(scale.astype(f32), piece.shape)
    code[:rows] = (piece / wide).astype(bf16)
    if rows < LANES:
        wide = jnp.concatenate([wide, jnp.zeros((LANES - rows, LANES), f32)], axis=0)
    code[rows:] = wide.T[:SLOT].astype(bf16)


def chip_kernel(n, margin, neighbors, width, *refs):
    m = n // 2
    columns, keep, got, own_weight, other_weight, _after = refs[:6]
    cots, sends, (own, give) = refs[6 : 6 + m], refs[6 + m : 6 + 2 * m], refs[6 + 2 * m :]
    me = lax.axis_index("fsdp")
    atoms = cots[0].shape[0]
    rows = give.shape[0]
    at = column_of(neighbors, neighbors)
    totals = [None, None]
    for c in range(m):
        block = rows_at((me // 2) ^ c, atoms)
        sends[c][...] = (
            jnp.dot(keep[block][:, :width], own_weight[...], preferred_element_type=f32)
            + jnp.dot(got[block][:, :width], other_weight[...], preferred_element_type=f32)
        ).astype(bf16)
        graph = columns[rows_at(me ^ (2 * c), atoms)][:, at : at + 1]
        for i, act in enumerate((keep, got)):
            left = (act[block].astype(f32) * graph).T.astype(bf16)
            term = jnp.dot(left, cots[c][...], preferred_element_type=f32)
            totals[i] = term if c == 0 else totals[i] + term
    own[...] = totals[0][:rows]
    give[...] = totals[1][:rows].astype(bf16)


def grads_kernel(n, fragment, *refs):
    m = n // 2
    near, far, own_part, got_part = refs[:m], refs[m:n], refs[n], refs[n + 1]
    msg_grad, out_grad, code, blocks, total = refs[n + 2 :]
    me = lax.axis_index("fsdp")
    rows = msg_grad.shape[1]
    width = msg_grad.shape[2] // n
    lanes = pl.ds(pl.multiple_of(fragment[0] * FRAG, FRAG), FRAG)
    for c in range(m):
        blocks[me ^ (2 * c)] = near[c][:rows]
        blocks[me ^ (2 * c + 1)] = far[c][rows:]
    for e in range(n):
        msg_grad[0, :, e * width : (e + 1) * width] = blocks[e][:, :width]
    write_code(msg_grad[0, :, lanes].astype(f32), code.at[: rows + SLOT])
    total[...] = own_part[...] + got_part[...].astype(f32)
    out_grad[0] = total[...].astype(bf16)
    write_code(total[:, lanes], code.at[rows + SLOT :])


def node_kernel(feats, *refs):
    parts, out = refs[:-1], refs[-1]
    total = feats[...].astype(f32)
    for part in parts:
        total = total + part[...].astype(f32)
    out[...] = total.astype(bf16)


def pair_kernel(*refs):
    codes, out = refs[:-1], refs[-1]
    rows = out.shape[1]
    for piece in range(2):
        total = jnp.zeros((rows, FRAG), f32)
        for code in codes:
            own = code.at[piece * (rows + SLOT) : (piece + 1) * (rows + SLOT)]
            wide = jnp.broadcast_to(own[rows:].astype(f32)[:1], (LANES, LANES)).T
            total = total + wide[:rows] * own[:rows].astype(f32)
        out[piece] = total.astype(out.dtype)


def outer_kernel(own, other, out):
    out[...] = (own[...].astype(f32) + other[...].astype(f32)).astype(out.dtype)


def run(kernel, outs, scratch, args, micros, memory=16, scalars=0, outside=0):
    whole = pl.BlockSpec(memory_space=pltpu.VMEM)
    scalar = pl.BlockSpec(memory_space=pltpu.SMEM)
    remote = pl.BlockSpec(memory_space=pltpu.HBM)
    return pl.pallas_call(
        kernel,
        out_shape=[jax.ShapeDtypeStruct(shape, dtype) for shape, dtype in outs],
        in_specs=[scalar] * scalars
        + [whole] * (len(args) - scalars - outside)
        + [remote] * outside,
        out_specs=[whole] * len(outs),
        scratch_shapes=[
            pltpu.SemaphoreType.DMA(shape) if dtype is None else pltpu.VMEM(shape, dtype)
            for shape, dtype in scratch
        ],
        compiler_params=pltpu.CompilerParams(vmem_limit_bytes=memory << 20),
        cost_estimate=pl.CostEstimate(
            flops=int(micros * 1e9), bytes_accessed=int(micros * 3e6), transcendentals=0
        ),
    )(*args)


def hop(value, axis, step):
    count = lax.axis_size(axis)
    return lax.ppermute(value, axis, [(i, i ^ step) for i in range(count)])


def across_chips(sends):
    return [sends[0]] + [hop(sends[c], "fsdp", 2 * c) for c in range(1, len(sends))]


def exchanged(first, second, n):
    bits = [1 << i for i in range((n // 2).bit_length() - 1)]
    found = [{0: value} for value in (first, second)]
    for c in range(1, n // 2):
        used = [bit for bit in bits if c & bit]
        for pieces, bit in zip(found, (used[0], used[-1])):
            pieces[c] = hop(pieces[c ^ bit], "fsdp", 2 * bit)
    return [[pieces[c] for c in range(n // 2)] for pieces in found]


def from_chips(sends):
    near = across_chips(sends)
    return near, [hop(value, "fsdp", 1) for value in near]


def shards(
    node_feats,
    neighbor_src,
    distances,
    graph_ids,
    msg_weight,
    out_weight,
    radial_weight,
    cotangent,
    fragment,
):
    n = lax.axis_size("fsdp")
    replicas = lax.axis_size("replica")
    m = n // 2
    atoms, channels = node_feats.shape
    neighbors = neighbor_src.shape[0]
    basis = radial_weight.shape[0]
    rows = msg_weight.shape[0]
    width = channels // n
    margin = atoms // 4
    reach = atoms + 2 * margin
    norm = 1.0 / math.sqrt(neighbors)
    all_atoms = n * atoms
    lanes = neighbors * LANES
    ahead = all_atoms * lanes * 4 <= 8 << 20
    memory = 24 if ahead else 56
    step_scratch = [
        ((2 * basis * SLOT, lanes), bf16),
        ((atoms, lanes), f32),
    ]

    pack_inputs = [
        msg_weight,
        neighbor_src,
        distances,
        graph_ids,
        radial_weight,
    ]
    bundle = 2 * rows + 4 * SLOT
    *packed, own_radial = run(
        functools.partial(pack_kernel, n, width),
        [((bundle, LANES), bf16)] * m + [((basis, LANES), f32)],
        [((n, rows, LANES), bf16), ((n, basis, LANES), f32), ((SLOT, LANES), f32)]
        + [(piece.shape, piece.dtype) for piece in pack_inputs]
        + [((len(pack_inputs),), None)],
        pack_inputs,
        1,
        60,
        outside=len(pack_inputs),
    )
    near = across_chips(packed)
    feats, cots = exchanged(node_feats, cotangent, n)
    (give_lists,) = run(
        functools.partial(merge_kernel, m),
        [((m * bundle, LANES), bf16)],
        [],
        [*near, feats[m // 2], cots[1]],
        0,
        memory,
    )
    far = hop(give_lists, "fsdp", 1)
    weights, columns, offsets, *made = run(
        functools.partial(lists_kernel, n, margin, neighbors, ahead),
        [
            ((channels, 2 * LANES), bf16),
            ((all_atoms, LANES), f32),
            ((n * SLOT, LANES), f32),
        ]
        + [
            ((all_atoms, lanes), f32),
            ((n * neighbors * 2 * margin, 8 * margin), bf16),
            ((n * reach, neighbors * atoms), bf16),
        ]
        * ahead,
        [
            ((n * SLOT, LANES), f32),
            ((n * SLOT, LANES), f32),
            ((min(n, 8), basis * SLOT, LANES), f32),
            ((2 * basis * SLOT, lanes), bf16),
        ],
        [*near, far, own_radial],
        0,
        memory,
    )
    other_weight = hop(out_weight, "fsdp", 1)
    own_products, give_products, held_feats = run(
        functools.partial(products_kernel, n),
        [((all_atoms, LANES), bf16)] * 2 + [((all_atoms // 2, channels), bf16)],
        [((2 * LANES, channels), bf16)],
        [weights, out_weight, other_weight, *feats, *cots],
        1,
        memory,
    )
    got_products = hop(give_products, "fsdp", 1)
    held_feats = pl.pallas_call(
        gate_kernel,
        out_shape=jax.ShapeDtypeStruct(held_feats.shape, bf16),
        in_specs=[pl.BlockSpec(memory_space=pl.ANY)] * 2,
        out_specs=pl.BlockSpec(memory_space=pl.ANY),
        input_output_aliases={0: 0},
        compiler_params=pltpu.CompilerParams(vmem_limit_bytes=1 << 20),
    )(held_feats, got_products)
    keep, give, dagg = run(
        functools.partial(forward_kernel, n, margin, neighbors, norm, ahead),
        [
            ((all_atoms // 2, LANES), bf16),
            ((all_atoms // 2, LANES), bf16),
            ((all_atoms, LANES), f32),
        ],
        [((all_atoms + 2 * margin, LANES), bf16)]
        + (step_scratch + [((neighbors * 2 * margin, 8 * margin), bf16)]) * (not ahead),
        [own_products, got_products, columns, own_radial, *made[:2]],
        1,
        memory,
    )
    other_act = hop(give, "fsdp", 1)
    grad_sends = run(
        functools.partial(backward_kernel, n, margin, neighbors, channels, ahead),
        [((2 * rows, LANES), bf16)] * m,
        [
            ((min(n, 8) if ahead else 1, neighbors * atoms, LANES), bf16),
            ((all_atoms + 2 * margin, LANES), f32),
            ((LANES, all_atoms), bf16),
            ((channels, LANES), bf16),
        ]
        + (step_scratch + [((reach, neighbors * atoms), bf16)]) * (not ahead),
        [
            held_feats,
            hop(held_feats, "fsdp", 1),
            dagg,
            own_radial,
            columns,
            offsets,
            *made[::2],
        ],
        4,
        memory,
    )
    near, far = from_chips(grad_sends)
    *sums, own_part, give_part = run(
        functools.partial(chip_kernel, n, margin, neighbors, width),
        [((atoms, channels), bf16)] * m + [((rows, channels), f32), ((rows, channels), bf16)],
        [],
        [columns, keep, other_act, out_weight, other_weight, grad_sends[0], *cots],
        1,
        memory,
    )
    grad_msg, grad_out, code = run(
        functools.partial(grads_kernel, n),
        [((1, rows, channels), bf16)] * 2 + [((2 * (rows + SLOT), FRAG), bf16)],
        [((n, rows, LANES), bf16), ((rows, channels), f32)],
        [fragment, *near, *far, own_part, hop(give_part, "fsdp", 1)],
        1,
        memory,
        scalars=1,
    )
    (node_out,) = run(
        node_kernel,
        [((atoms, channels), bf16)],
        [],
        [node_feats, sums[0]] + [hop(sums[c], "fsdp", 2 * c) for c in range(1, m)],
        1,
        memory,
    )
    step = 1
    codes = [code]
    if replicas > 1:
        codes.append(hop(code, "replica", step))
    (outer_sum,) = run(
        pair_kernel, [((2, rows, FRAG), f32 if replicas <= 2 else bf16)], [], codes, 0, memory
    )
    while 2 * step < replicas:
        step = 2 * step
        last = 2 * step >= replicas
        (outer_sum,) = run(
            outer_kernel,
            [((2, rows, FRAG), f32 if last else bf16)],
            [],
            [outer_sum, hop(outer_sum, "replica", step)],
            0,
            memory,
        )
    return node_out, grad_msg, grad_out, outer_sum


def solution(mesh):
    placed = (
        P(("replica", "fsdp"), None),
        P(None, ("replica", "fsdp")),
        P(None, ("replica", "fsdp")),
        P("replica", "fsdp"),
        P("fsdp", None),
        P("fsdp", None),
        P(),
        P(("replica", "fsdp"), None),
        P(),
    )
    return jax.shard_map(
        shards,
        mesh=mesh,
        in_specs=placed,
        out_specs=(
            P(("replica", "fsdp"), None),
            P("replica", "fsdp", None),
            P("replica", "fsdp", None),
            P(None, "fsdp", None),
        ),
        check_vma=False,
    )
```

```python
import functools
import math

import jax
import jax.numpy as jnp
from jax import lax
from jax.experimental import pallas as pl
from jax.experimental.pallas import tpu as pltpu
from jax.sharding import PartitionSpec as P

FRAG = 128
GRAPHS = 8
LANES = 128
SLOT = 16

cutoff = 5.0
sharpness = 2.0
tiny = 1e-06

bf16 = jnp.bfloat16
f32 = jnp.float32


def rows_at(index, count):
    return pl.ds(pl.multiple_of(index * count, count), count)


def column_of(k, neighbors):
    free = SLOT - neighbors
    return (k // free) * SLOT + neighbors + k % free


def pack_kernel(n, width, *refs):
    far, refs = refs[:5], refs[5:]
    packed, own_radial, (blocks, radials, group) = refs[: n // 2], refs[n // 2], refs[n // 2 + 1 : n // 2 + 4]
    held, done = refs[n // 2 + 4 : n // 2 + 9], refs[n // 2 + 9]
    copies = [pltpu.make_async_copy(a, b, done.at[i]) for i, (a, b) in enumerate(zip(far, held))]
    for copy in copies:
        copy.start()
    for copy in copies:
        copy.wait()
    weight, src, dist, ids, radial_weight = held
    me = lax.axis_index("fsdp")
    rows = weight.shape[0]
    neighbors, atoms = src.shape
    if width < LANES:
        blocks[...] = jnp.zeros_like(blocks)
        radials[...] = jnp.zeros_like(radials)
    for e in range(n):
        blocks[e, :, :width] = weight[:, e * width : (e + 1) * width]
        radials[e, :, :width] = radial_weight[:, e * width : (e + 1) * width]
    own_radial[...] = radials[me]
    position = lax.broadcasted_iota(jnp.int32, src.shape, 1) + me * atoms
    group[...] = jnp.zeros_like(group)
    group[:neighbors] = (src[...] - position).astype(f32)
    group[neighbors : neighbors + 1] = ids[...].astype(f32)
    meta = [group[...].astype(bf16)]
    group[...] = jnp.ones_like(group)
    group[:neighbors] = dist[...]
    left = group[...]
    for _ in range(3):
        part = left.astype(bf16)
        meta.append(part)
        left = left - part.astype(f32)
    for c in range(n // 2):
        packed[c][:rows] = blocks[me ^ (2 * c)]
        packed[c][rows : 2 * rows] = blocks[me ^ (2 * c + 1)]
        for i, part in enumerate(meta):
            packed[c][2 * rows + i * SLOT : 2 * rows + (i + 1) * SLOT] = part


def merge_kernel(m, *refs):
    parts, out = refs[:m], refs[-1]
    rows = parts[0].shape[0]
    for c, part in enumerate(parts):
        out[c * rows : (c + 1) * rows] = part[...]


def swap_kernel(*refs):
    parts, last, out = refs[:-2], refs[-2], refs[-1]
    rows = parts[0].shape[0] // 2
    for c, part in enumerate(parts):
        out[c * rows : (c + 1) * rows] = part[rows:]
    out[len(parts) * rows :] = last[...]


def gate_kernel(_value, _after, _out):
    pass


def fill_filters(neighbors, own_radial, filters):
    basis = own_radial.shape[0]
    half = basis * SLOT
    row = lax.broadcasted_iota(jnp.int32, (half, LANES), 0) % SLOT
    spread = jnp.concatenate(
        [jnp.broadcast_to(own_radial[b : b + 1], (SLOT, LANES)) for b in range(basis)], axis=0
    )
    high = spread.astype(bf16).astype(f32)
    low = spread - high
    for k in range(neighbors):
        lanes = slice(k * LANES, (k + 1) * LANES)
        filters[:half, lanes] = jnp.where(row == k, high, 0.0).astype(bf16)
        filters[half:, lanes] = jnp.where(row == k, low, 0.0).astype(bf16)


def fill_values(columns, filters, values):
    high = columns.astype(bf16)
    both = jnp.concatenate([high, high], axis=1)
    span = 2 * LANES

    def step(j, _):
        lanes = pl.ds(pl.multiple_of(j * span, span), span)
        values[:, lanes] = jnp.dot(both, filters[:, lanes], preferred_element_type=f32)
        return 0

    steps = values.shape[1] // span
    lax.fori_loop(0, steps, step, 0, unroll=steps)


def fill_pick(margin, neighbors, turned, pick):
    tile = 2 * margin
    tiles = turned.shape[0] // tile
    shift = (
        lax.broadcasted_iota(jnp.int32, (tile, 2 * tile), 1)
        - lax.broadcasted_iota(jnp.int32, (tile, 2 * tile), 0)
        - margin
    ).astype(f32)
    for t in range(tiles):
        own = turned[t * tile : (t + 1) * tile]
        for k in range(neighbors):
            at = column_of(k, neighbors)
            pick[k * tile : (k + 1) * tile, t * 2 * tile : (t + 1) * 2 * tile] = jnp.where(
                own[:, at : at + 1] == shift, 1.0, 0.0
            ).astype(bf16)


def fill_place(margin, neighbors, offset, place):
    tile = 2 * margin
    shape = (2 * tile, 2 * tile)
    shift = (
        lax.broadcasted_iota(jnp.int32, shape, 0)
        - lax.broadcasted_iota(jnp.int32, shape, 1) % tile
        - margin
    ).astype(f32)
    for t in range(offset.shape[1] // tile):
        for k in range(0, neighbors, 2):
            row = jnp.concatenate(
                [offset[k + i : k + i + 1, t * tile : (t + 1) * tile] for i in range(2)], axis=1
            )
            place[t * 2 * tile : (t + 1) * 2 * tile, k * tile : (k + 2) * tile] = jnp.where(
                row == shift, 1.0, 0.0
            ).astype(bf16)


def lists_kernel(n, margin, neighbors, ahead, *refs):
    m = n // 2
    near, far, own_radial = refs[:m], refs[m], refs[m + 1]
    weights, columns, offsets = refs[m + 2 : m + 5]
    made = refs[m + 5 : m + 8] if ahead else ()
    dists, graph_weight, stacked, filters = refs[m + 5 + len(made) :]
    me = lax.axis_index("fsdp")
    basis = own_radial.shape[0]
    rows = weights.shape[0] // n
    atoms = columns.shape[0] // n
    for d in range(n):
        e = me ^ d
        head = 2 * rows + 4 * SLOT
        block = near[d // 2] if d % 2 == 0 else far.at[d // 2 * head : (d // 2 + 1) * head]
        weights[rows_at(e, rows), d % 2 * LANES : (d % 2 + 1) * LANES] = block[:rows]
        weights[rows_at(e, rows), (1 - d % 2) * LANES : (2 - d % 2) * LANES] = block[
            rows : 2 * rows
        ]
        meta = block[2 * rows :].astype(f32)
        offsets[rows_at(e, SLOT)] = meta[:SLOT]
        dists[rows_at(e, SLOT)] = (
            meta[SLOT : 2 * SLOT] + meta[2 * SLOT : 3 * SLOT] + meta[3 * SLOT :]
        )
    slots = lax.broadcasted_iota(jnp.int32, offsets.shape, 0) % SLOT
    ids = jnp.where(slots == neighbors, offsets[...], -1.0)
    weight = jnp.zeros_like(ids)
    for g in range(GRAPHS):
        member = ids == float(g)
        count = jnp.sum(jnp.where(member, 1.0, 0.0), axis=(0, 1), keepdims=True)
        weight = weight + jnp.where(member, lax.rsqrt(jnp.maximum(count, 1.0)), 0.0)
    graph_weight[...] = weight

    def columns_step(e, _):
        dist = dists[rows_at(e, SLOT)]
        envelope = 0.5 * (jnp.cos(jnp.pi * dist / cutoff) + 1.0)
        own = stacked.at[e % stacked.shape[0]]
        for b in range(basis):
            center = cutoff * b / (basis - 1)
            own[b * SLOT : (b + 1) * SLOT] = jnp.exp(-sharpness * (dist - center) ** 2) * envelope
        offset = offsets[rows_at(e, SLOT)]
        for k in range(neighbors):
            at = column_of(k, neighbors)
            own[at : at + 1] = offset[k : k + 1]
        at = column_of(neighbors, neighbors)
        own[at : at + 1] = graph_weight[rows_at(e, SLOT)][neighbors : neighbors + 1]
        columns[rows_at(e, atoms)] = own[...].T
        return 0

    lax.fori_loop(0, n, columns_step, 0, unroll=stacked.shape[0])
    if ahead:
        values, pick, place = made
        fill_filters(neighbors, own_radial, filters)
        fill_values(columns[...], filters, values)

        def block_step(e, _):
            span = neighbors * 2 * margin
            fill_pick(margin, neighbors, columns[rows_at(e, atoms)], pick.at[rows_at(e, span)])
            fill_place(
                margin,
                neighbors,
                offsets[rows_at(e, SLOT)],
                place.at[rows_at(e, 2 * atoms)],
            )
            return 0

        lax.fori_loop(0, n, block_step, 0, unroll=2)


def products_kernel(n, weights, own_weight, other_weight, *refs):
    m = n // 2
    feats, cots, (keep, give, held_feats, both) = refs[:m], refs[m : 2 * m], refs[2 * m :]
    me = lax.axis_index("fsdp")
    atoms = feats[0].shape[0]
    half = m * atoms
    rows = own_weight.shape[0]
    if rows < LANES:
        both[...] = jnp.zeros_like(both)
    both[:rows] = own_weight[...]
    both[LANES : LANES + rows] = other_weight[...]
    for c in range(m):
        held_feats[c * atoms : (c + 1) * atoms] = feats[c][...]
        projected = jnp.dot(
            feats[c][...], weights[...], preferred_element_type=f32
        ).astype(bf16)
        dact = lax.dot_general(
            cots[c][...], both[...], (((1,), (1,)), ((), ())), preferred_element_type=f32
        ).astype(bf16)
        chip = (me // 2) ^ c
        keep[rows_at(chip, atoms)] = projected[:, :LANES]
        give[rows_at(chip, atoms)] = projected[:, LANES:]
        keep[rows_at(chip + m, atoms)] = dact[:, :LANES]
        give[rows_at(chip + m, atoms)] = dact[:, LANES:]


def forward_kernel(n, margin, neighbors, norm, ahead, *refs):
    own, got, columns, own_radial = refs[:4]
    made = refs[4:6] if ahead else ()
    keep, give, dagg, projected, act = refs[4 + len(made) : 9 + len(made)]
    scratch = refs[9 + len(made) :]
    me = lax.axis_index("fsdp")
    core = me % 2
    atoms = columns.shape[0] // n
    half = n // 2 * atoms
    projected[:margin] = jnp.zeros_like(projected[:margin])
    projected[n * atoms + margin :] = jnp.zeros_like(projected[:margin])
    for c in range(n // 2):
        for source, parity in ((own, core), (got, 1 - core)):
            start = pl.multiple_of((2 * c + parity) * atoms + margin, margin)
            projected[pl.ds(start, atoms)] = source[c * atoms : (c + 1) * atoms]
            dact = source[half + c * atoms : half + (c + 1) * atoms]
            dagg[rows_at(2 * c + parity, atoms)] = dact.astype(f32)
    if ahead:
        values, pick = made
    else:
        filters, values, pick = scratch
        fill_filters(neighbors, own_radial, filters)
    tile = 2 * margin
    span = neighbors * tile

    def block_step(e, _):
        turned = columns[rows_at(e, atoms)]
        if ahead:
            own_values = values.at[rows_at(e, atoms)]
            own_pick = pick[rows_at(e, span)]
        else:
            own_values = values
            fill_values(turned, filters, values)
            fill_pick(margin, neighbors, turned, pick)
            own_pick = pick[...]
        start = pl.multiple_of(e * atoms, atoms)
        halves = []
        for t in range(2):
            found = jnp.dot(
                own_pick[:, t * 2 * tile : (t + 1) * 2 * tile],
                projected[pl.ds(start + t * tile, 2 * tile)],
                preferred_element_type=f32,
            )
            total = jnp.zeros((tile, LANES), f32)
            for k in range(neighbors):
                total = total + (
                    own_values[t * tile : (t + 1) * tile, k * LANES : (k + 1) * LANES]
                    * found[k * tile : (k + 1) * tile]
                )
            halves.append(total)
        agg = jnp.concatenate(halves, axis=0) * norm
        sig = 1.0 / (1.0 + jnp.exp(-agg))
        active = (agg * sig).astype(bf16)
        at = column_of(neighbors, neighbors)
        graph = turned[:, at : at + 1]
        slope = sig * (1.0 + agg * (1.0 - sig)) * (graph * norm)
        dagg[rows_at(e, atoms)] = dagg[rows_at(e, atoms)] * slope
        act[rows_at(e, atoms)] = active
        return 0

    lax.fori_loop(0, n, block_step, 0, unroll=min(n, 8) if ahead else 1)
    for c in range(n // 2):
        keep[c * atoms : (c + 1) * atoms] = act[rows_at(2 * c + core, atoms)]
        give[c * atoms : (c + 1) * atoms] = act[rows_at(2 * c + 1 - core, atoms)]


def backward_kernel(n, margin, neighbors, ahead, *refs):
    m = n // 2
    dagg, own_radial, columns, offsets = refs[:4]
    made = refs[4:6] if ahead else ()
    refs = refs[4 + len(made) :]
    turned, terms, spread = refs[:3]
    scratch = refs[3:]
    me = lax.axis_index("fsdp")
    atoms = columns.shape[0] // n
    tile = 2 * margin
    spread[0, n * atoms :] = jnp.zeros_like(spread[0, n * atoms :])
    spread[1, :tile] = jnp.zeros_like(spread[1, :tile])
    if ahead:
        values, place = made
    else:
        filters, values, place = scratch
        fill_filters(neighbors, own_radial, filters)

    def block_step(e, _):
        flow = dagg[rows_at(e, atoms)]
        if ahead:
            own_values = values.at[rows_at(e, atoms)]
            own_place = place.at[rows_at(e, 2 * atoms)]
        else:
            own_values = values
            fill_values(columns[rows_at(e, atoms)], filters, values)
            fill_place(margin, neighbors, offsets[rows_at(e, SLOT)], place)
            own_place = place
        for t in range(2):
            own = terms.at[2 * (e % (terms.shape[0] // 2)) + t]
            here = slice(t * tile, (t + 1) * tile)
            for k in range(neighbors):
                own[k * tile : (k + 1) * tile] = (
                    own_values[here, k * LANES : (k + 1) * LANES] * flow[here]
                ).astype(bf16)
            window = pl.ds(pl.multiple_of(e * atoms + t * tile, tile), 2 * tile)
            spread[t, window] = jnp.dot(
                own_place[t * 2 * tile : (t + 1) * 2 * tile], own[...], preferred_element_type=f32
            )
        return 0

    lax.fori_loop(0, n, block_step, 0, unroll=min(n, 8) if ahead else 1)

    half = m * atoms
    for k in range(2):
        for c in range(m):
            e = me ^ (2 * c + k)
            start = pl.multiple_of(e * atoms + margin, margin)
            turned[:, k * half + c * atoms : k * half + (c + 1) * atoms] = (
                (spread[0, pl.ds(start, atoms)] + spread[1, pl.ds(start, atoms)]).T.astype(bf16)
            )


def gradient_kernel(n, rows, turned, own_feats, other_feats, *refs):
    m = n // 2
    sends, grads = refs[:m], refs[m]
    me = lax.axis_index("fsdp")
    half = own_feats.shape[0]
    total = jnp.dot(turned[:, :half], own_feats[...], preferred_element_type=f32)
    total = total + jnp.dot(turned[:, half:], other_feats[...], preferred_element_type=f32)
    for q in range(total.shape[1] // LANES):
        grads[q * LANES : (q + 1) * LANES] = total[:, q * LANES : (q + 1) * LANES].T.astype(bf16)
    for c in range(m):
        sends[c][:rows] = grads[rows_at(me ^ (2 * c), rows)]
        sends[c][rows:] = grads[rows_at(me ^ (2 * c + 1), rows)]


def write_code(piece, code):
    rows = piece.shape[0]
    scale = (jnp.max(jnp.abs(piece), axis=-1, keepdims=True) + tiny).astype(bf16)
    wide = jnp.broadcast_to(scale.astype(f32), piece.shape)
    code[:rows] = (piece / wide).astype(bf16)
    if rows < LANES:
        wide = jnp.concatenate([wide, jnp.zeros((LANES - rows, LANES), f32)], axis=0)
    code[rows:] = wide.T[:SLOT].astype(bf16)


def chip_kernel(n, margin, neighbors, width, *refs):
    m = n // 2
    columns, keep, got, own_weight, other_weight, _after = refs[:6]
    cots, sends, (own, give) = refs[6 : 6 + m], refs[6 + m : 6 + 2 * m], refs[6 + 2 * m :]
    me = lax.axis_index("fsdp")
    atoms = cots[0].shape[0]
    rows = own.shape[0]
    at = column_of(neighbors, neighbors)
    totals = [None, None]
    for c in range(m):
        block = rows_at((me // 2) ^ c, atoms)
        sends[c][...] = (
            jnp.dot(keep[block][:, :width], own_weight[...], preferred_element_type=f32)
            + jnp.dot(got[block][:, :width], other_weight[...], preferred_element_type=f32)
        ).astype(bf16)
        graph = columns[rows_at(me ^ (2 * c), atoms)][:, at : at + 1]
        for i, act in enumerate((keep, got)):
            left = (act[block].astype(f32) * graph).T.astype(bf16)
            term = jnp.dot(left, cots[c][...], preferred_element_type=f32)
            totals[i] = term if c == 0 else totals[i] + term
    own[...] = totals[0][:rows]
    for q in range(own.shape[1] // LANES):
        give[q * rows : (q + 1) * rows] = totals[1][:rows, q * LANES : (q + 1) * LANES].astype(bf16)


def grads_kernel(n, fragment, *refs):
    m = n // 2
    near, far, own_part = refs[:m], refs[m], refs[m + 1]
    msg_grad, out_grad, code, blocks, total = refs[m + 2 :]
    me = lax.axis_index("fsdp")
    rows = msg_grad.shape[1]
    width = msg_grad.shape[2] // n
    lanes = pl.ds(pl.multiple_of(fragment[0] * FRAG, FRAG), FRAG)
    for c in range(m):
        blocks[me ^ (2 * c)] = near[c][:rows]
        blocks[me ^ (2 * c + 1)] = far[c * rows : (c + 1) * rows]
    for e in range(n):
        msg_grad[0, :, e * width : (e + 1) * width] = blocks[e][:, :width]
    write_code(msg_grad[0, :, lanes].astype(f32), code.at[: rows + SLOT])
    for q in range(total.shape[1] // LANES):
        part = slice(q * LANES, (q + 1) * LANES)
        start = (m + q) * rows
        total[:, part] = own_part[:, part] + far[start : start + rows].astype(f32)
    out_grad[0] = total[...].astype(bf16)
    write_code(total[:, lanes], code.at[rows + SLOT :])


def node_kernel(feats, *refs):
    parts, out = refs[:-1], refs[-1]
    total = feats[...].astype(f32)
    for part in parts:
        total = total + part[...].astype(f32)
    out[...] = total.astype(bf16)


def pair_kernel(*refs):
    codes, out = refs[:-1], refs[-1]
    rows = out.shape[1]
    for piece in range(2):
        total = jnp.zeros((rows, FRAG), f32)
        for code in codes:
            own = code.at[piece * (rows + SLOT) : (piece + 1) * (rows + SLOT)]
            wide = jnp.broadcast_to(own[rows:].astype(f32)[:1], (LANES, LANES)).T
            total = total + wide[:rows] * own[:rows].astype(f32)
        out[piece] = total.astype(out.dtype)


def outer_kernel(own, other, out):
    out[...] = (own[...].astype(f32) + other[...].astype(f32)).astype(out.dtype)


def run(kernel, outs, scratch, args, micros, memory=16, scalars=0, outside=0):
    whole = pl.BlockSpec(memory_space=pltpu.VMEM)
    scalar = pl.BlockSpec(memory_space=pltpu.SMEM)
    remote = pl.BlockSpec(memory_space=pltpu.HBM)
    return pl.pallas_call(
        kernel,
        out_shape=[jax.ShapeDtypeStruct(shape, dtype) for shape, dtype in outs],
        in_specs=[scalar] * scalars
        + [whole] * (len(args) - scalars - outside)
        + [remote] * outside,
        out_specs=[whole] * len(outs),
        scratch_shapes=[
            pltpu.SemaphoreType.DMA(shape) if dtype is None else pltpu.VMEM(shape, dtype)
            for shape, dtype in scratch
        ],
        compiler_params=pltpu.CompilerParams(vmem_limit_bytes=memory << 20),
        cost_estimate=pl.CostEstimate(
            flops=int(micros * 1e9), bytes_accessed=int(micros * 3e6), transcendentals=0
        ),
    )(*args)


def hop(value, axis, step):
    count = lax.axis_size(axis)
    return lax.ppermute(value, axis, [(i, i ^ step) for i in range(count)])


def across_chips(sends):
    return [sends[0]] + [hop(sends[c], "fsdp", 2 * c) for c in range(1, len(sends))]


def exchanged(first, second, n):
    bits = [1 << i for i in range((n // 2).bit_length() - 1)]
    found = [{0: value} for value in (first, second)]
    for c in range(1, n // 2):
        used = [bit for bit in bits if c & bit]
        for pieces, bit in zip(found, (used[0], used[-1])):
            pieces[c] = hop(pieces[c ^ bit], "fsdp", 2 * bit)
    return [[pieces[c] for c in range(n // 2)] for pieces in found]


def shards(
    node_feats,
    neighbor_src,
    distances,
    graph_ids,
    msg_weight,
    out_weight,
    radial_weight,
    cotangent,
    fragment,
):
    n = lax.axis_size("fsdp")
    replicas = lax.axis_size("replica")
    m = n // 2
    atoms, channels = node_feats.shape
    neighbors = neighbor_src.shape[0]
    basis = radial_weight.shape[0]
    rows = msg_weight.shape[0]
    width = channels // n
    margin = atoms // 4
    norm = 1.0 / math.sqrt(neighbors)
    all_atoms = n * atoms
    lanes = neighbors * LANES
    ahead = all_atoms * lanes * 4 <= 8 << 20
    memory = 24 if ahead else 56
    step_scratch = [
        ((2 * basis * SLOT, lanes), bf16),
        ((atoms, lanes), f32),
    ]

    pack_inputs = [
        msg_weight,
        neighbor_src,
        distances,
        graph_ids,
        radial_weight,
    ]
    bundle = 2 * rows + 4 * SLOT
    *packed, own_radial = run(
        functools.partial(pack_kernel, n, width),
        [((bundle, LANES), bf16)] * m + [((basis, LANES), f32)],
        [((n, rows, LANES), bf16), ((n, basis, LANES), f32), ((SLOT, LANES), f32)]
        + [(piece.shape, piece.dtype) for piece in pack_inputs]
        + [((len(pack_inputs),), None)],
        pack_inputs,
        1,
        60,
        outside=len(pack_inputs),
    )
    near = across_chips(packed)
    feats, cots = exchanged(node_feats, cotangent, n)
    (give_lists,) = run(
        functools.partial(merge_kernel, m),
        [((m * bundle, LANES), bf16)],
        [],
        [*near, feats[m // 2], cots[1]],
        0,
        memory,
    )
    far = hop(give_lists, "fsdp", 1)
    weights, columns, offsets, *made = run(
        functools.partial(lists_kernel, n, margin, neighbors, ahead),
        [
            ((channels, 2 * LANES), bf16),
            ((all_atoms, LANES), f32),
            ((n * SLOT, LANES), f32),
        ]
        + [
            ((all_atoms, lanes), f32),
            ((n * neighbors * 2 * margin, 8 * margin), bf16),
            ((2 * all_atoms, neighbors * 2 * margin), bf16),
        ]
        * ahead,
        [
            ((n * SLOT, LANES), f32),
            ((n * SLOT, LANES), f32),
            ((min(n, 8), basis * SLOT, LANES), f32),
            ((2 * basis * SLOT, lanes), bf16),
        ],
        [*near, far, own_radial],
        0,
        memory,
    )
    other_weight = hop(out_weight, "fsdp", 1)
    own_products, give_products, held_feats = run(
        functools.partial(products_kernel, n),
        [((all_atoms, LANES), bf16)] * 2 + [((all_atoms // 2, channels), bf16)],
        [((2 * LANES, channels), bf16)],
        [weights, out_weight, other_weight, *feats, *cots],
        1,
        memory,
    )
    got_products = hop(give_products, "fsdp", 1)
    held_feats = pl.pallas_call(
        gate_kernel,
        out_shape=jax.ShapeDtypeStruct(held_feats.shape, bf16),
        in_specs=[pl.BlockSpec(memory_space=pl.ANY)] * 2,
        out_specs=pl.BlockSpec(memory_space=pl.ANY),
        input_output_aliases={0: 0},
        compiler_params=pltpu.CompilerParams(vmem_limit_bytes=1 << 20),
    )(held_feats, got_products)
    keep, give, dagg = run(
        functools.partial(forward_kernel, n, margin, neighbors, norm, ahead),
        [
            ((all_atoms // 2, LANES), bf16),
            ((all_atoms // 2, LANES), bf16),
            ((all_atoms, LANES), f32),
        ],
        [((all_atoms + 2 * margin, LANES), bf16), ((all_atoms, LANES), bf16)]
        + (step_scratch + [((neighbors * 2 * margin, 8 * margin), bf16)]) * (not ahead),
        [own_products, got_products, columns, own_radial, *made[:2]],
        1,
        memory,
    )
    other_act = hop(give, "fsdp", 1)
    (turned,) = run(
        functools.partial(backward_kernel, n, margin, neighbors, ahead),
        [((LANES, all_atoms), bf16)],
        [
            ((2 * min(n, 8) if ahead else 2, neighbors * 2 * margin, LANES), bf16),
            ((2, all_atoms + 2 * margin, LANES), f32),
        ]
        + (step_scratch + [((2 * atoms, neighbors * 2 * margin), bf16)]) * (not ahead),
        [dagg, own_radial, columns, offsets, *made[::2]],
        1,
        memory,
    )
    grad_sends = run(
        functools.partial(gradient_kernel, n, rows),
        [((2 * rows, LANES), bf16)] * m,
        [((channels, LANES), bf16)],
        [turned, held_feats, hop(held_feats, "fsdp", 1)],
        1,
        memory,
    )
    near = across_chips(grad_sends)
    *sums, own_part, give_part = run(
        functools.partial(chip_kernel, n, margin, neighbors, width),
        [((atoms, channels), bf16)] * m + [((rows, channels), f32), ((channels // LANES * rows, LANES), bf16)],
        [],
        [columns, keep, other_act, out_weight, other_weight, grad_sends[0], *cots],
        1,
        memory,
    )
    (swap,) = run(
        swap_kernel,
        [(((m + channels // LANES) * rows, LANES), bf16)],
        [],
        [*near, give_part],
        0,
        memory,
    )
    grad_msg, grad_out, code = run(
        functools.partial(grads_kernel, n),
        [((1, rows, channels), bf16)] * 2 + [((2 * (rows + SLOT), FRAG), bf16)],
        [((n, rows, LANES), bf16), ((rows, channels), f32)],
        [fragment, *near, hop(swap, "fsdp", 1), own_part],
        1,
        memory,
        scalars=1,
    )
    (node_out,) = run(
        node_kernel,
        [((atoms, channels), bf16)],
        [],
        [node_feats, sums[0]] + [hop(sums[c], "fsdp", 2 * c) for c in range(1, m)],
        1,
        memory,
    )
    step = 1
    codes = [code]
    if replicas > 1:
        codes.append(hop(code, "replica", step))
    (outer_sum,) = run(
        pair_kernel, [((2, rows, FRAG), f32 if replicas <= 2 else bf16)], [], codes, 0, memory
    )
    while 2 * step < replicas:
        step = 2 * step
        last = 2 * step >= replicas
        (outer_sum,) = run(
            outer_kernel,
            [((2, rows, FRAG), f32 if last else bf16)],
            [],
            [outer_sum, hop(outer_sum, "replica", step)],
            0,
            memory,
        )
    return node_out, grad_msg, grad_out, outer_sum


def solution(mesh):
    placed = (
        P(("replica", "fsdp"), None),
        P(None, ("replica", "fsdp")),
        P(None, ("replica", "fsdp")),
        P("replica", "fsdp"),
        P("fsdp", None),
        P("fsdp", None),
        P(),
        P(("replica", "fsdp"), None),
        P(),
    )
    return jax.shard_map(
        shards,
        mesh=mesh,
        in_specs=placed,
        out_specs=(
            P(("replica", "fsdp"), None),
            P("replica", "fsdp", None),
            P("replica", "fsdp", None),
            P(None, "fsdp", None),
        ),
        check_vma=False,
    )
```

```python
import functools
import math

import jax
import jax.numpy as jnp
from jax import lax
from jax.experimental import pallas as pl
from jax.experimental.pallas import tpu as pltpu
from jax.sharding import PartitionSpec as P

FRAG = 128
GRAPHS = 8
LANES = 128
SLOT = 16

cutoff = 5.0
sharpness = 2.0
tiny = 1e-06

bf16 = jnp.bfloat16
f32 = jnp.float32


def rows_at(index, count):
    return pl.ds(pl.multiple_of(index * count, count), count)


def column_of(k, neighbors):
    free = SLOT - neighbors
    return (k // free) * SLOT + neighbors + k % free


def chunk_of(rows, pieces):
    return -(-rows // (pieces * SLOT)) * SLOT


def pack_kernel(n, width, *refs):
    far, refs = refs[:7], refs[7:]
    m = n // 2
    packed, (feats_out, cot_out, own_radial) = refs[: m - 2], refs[m - 2 : m + 1]
    (blocks, radials, group, bundle), refs = refs[m + 1 : m + 5], refs[m + 5 :]
    held, done = refs[:7], refs[7]
    copies = [pltpu.make_async_copy(a, b, done.at[i]) for i, (a, b) in enumerate(zip(far, held))]
    for copy in copies:
        copy.start()
    for copy in copies:
        copy.wait()
    weight, src, dist, ids, radial_weight, feats, cot = held
    me = lax.axis_index("fsdp")
    rows = weight.shape[0]
    neighbors, atoms = src.shape
    if width < LANES:
        blocks[...] = jnp.zeros_like(blocks)
        radials[...] = jnp.zeros_like(radials)
    for e in range(n):
        blocks[e, :, :width] = weight[:, e * width : (e + 1) * width]
        radials[e, :, :width] = radial_weight[:, e * width : (e + 1) * width]
    own_radial[...] = radials[me]
    position = lax.broadcasted_iota(jnp.int32, src.shape, 1) + me * atoms
    group[...] = jnp.zeros_like(group)
    group[:neighbors] = (src[...] - position).astype(f32)
    group[neighbors : neighbors + 1] = ids[...].astype(f32)
    meta = [group[...].astype(bf16)]
    group[...] = jnp.ones_like(group)
    group[:neighbors] = dist[...]
    left = group[...]
    for _ in range(3):
        part = left.astype(bf16)
        meta.append(part)
        left = left - part.astype(f32)
    feats_out[:atoms] = feats[...]
    cot_out[:atoms] = cot[...]
    direct = 0
    for c in range(m):
        wide = {1: feats_out, m // 2: cot_out}.get(c)
        if wide is None:
            target = packed[direct]
            direct += 1
        else:
            target = bundle
        target[:rows] = blocks[me ^ (2 * c)]
        target[rows : 2 * rows] = blocks[me ^ (2 * c + 1)]
        for i, part in enumerate(meta):
            target[2 * rows + i * SLOT : 2 * rows + (i + 1) * SLOT] = part
        if wide is not None:
            size = wide.shape[0] - atoms
            for q in range(wide.shape[1] // LANES):
                stop = min((q + 1) * size, bundle.shape[0])
                if stop > q * size:
                    wide[atoms : atoms + stop - q * size, q * LANES : (q + 1) * LANES] = bundle[
                        q * size : stop
                    ]


def merge_kernel(m, rows, *refs):
    direct, (feats, cot, own_weight), refs = list(refs[: m - 2]), refs[m - 2 : m + 1], refs[m + 1 :]
    for value, held in zip(refs[:2], refs[2:4]):
        held[...] = value[...]
    lists, weights, bundle = refs[4:]
    size = 4 * SLOT
    for c in range(m):
        wide = {1: feats, m // 2: cot}.get(c)
        if wide is None:
            source = direct.pop(0)
        else:
            source = bundle
            height = chunk_of(bundle.shape[0], wide.shape[1] // LANES)
            for q in range(wide.shape[1] // LANES):
                stop = min((q + 1) * height, bundle.shape[0])
                if stop > q * height:
                    bundle[q * height : stop] = wide[
                        wide.shape[0] - height : wide.shape[0] - height + stop - q * height,
                        q * LANES : (q + 1) * LANES,
                    ]
        weights[2 * c * rows : 2 * (c + 1) * rows] = source[: 2 * rows]
        lists[c * size : (c + 1) * size] = source[2 * rows :]
    for q in range(own_weight.shape[1] // LANES):
        start = (2 * m + q) * rows
        weights[start : start + rows] = own_weight[:, q * LANES : (q + 1) * LANES]


def gate_kernel(*_):
    pass


def fill_filters(neighbors, own_radial, filters):
    basis = own_radial.shape[0]
    half = basis * SLOT
    row = lax.broadcasted_iota(jnp.int32, (half, LANES), 0) % SLOT
    spread = jnp.concatenate(
        [jnp.broadcast_to(own_radial[b : b + 1], (SLOT, LANES)) for b in range(basis)], axis=0
    )
    high = spread.astype(bf16).astype(f32)
    low = spread - high
    for k in range(neighbors):
        lanes = slice(k * LANES, (k + 1) * LANES)
        filters[:half, lanes] = jnp.where(row == k, high, 0.0).astype(bf16)
        filters[half:, lanes] = jnp.where(row == k, low, 0.0).astype(bf16)


def fill_values(columns, filters, values):
    high = columns.astype(bf16)
    both = jnp.concatenate([high, high], axis=1)
    span = 2 * LANES

    def step(j, _):
        lanes = pl.ds(pl.multiple_of(j * span, span), span)
        values[:, lanes] = jnp.dot(both, filters[:, lanes], preferred_element_type=f32)
        return 0

    steps = values.shape[1] // span
    lax.fori_loop(0, steps, step, 0, unroll=steps)


def fill_pick(margin, neighbors, turned, pick):
    tile = 2 * margin
    tiles = turned.shape[0] // tile
    shift = (
        lax.broadcasted_iota(jnp.int32, (tile, 2 * tile), 1)
        - lax.broadcasted_iota(jnp.int32, (tile, 2 * tile), 0)
        - margin
    ).astype(f32)
    for t in range(tiles):
        own = turned[t * tile : (t + 1) * tile]
        for k in range(neighbors):
            at = column_of(k, neighbors)
            pick[k * tile : (k + 1) * tile, t * 2 * tile : (t + 1) * 2 * tile] = jnp.where(
                own[:, at : at + 1] == shift, 1.0, 0.0
            ).astype(bf16)


def fill_place(margin, neighbors, offset, place):
    tile = 2 * margin
    shape = (2 * tile, 2 * tile)
    shift = (
        lax.broadcasted_iota(jnp.int32, shape, 0)
        - lax.broadcasted_iota(jnp.int32, shape, 1) % tile
        - margin
    ).astype(f32)
    for t in range(offset.shape[1] // tile):
        for k in range(0, neighbors, 2):
            row = jnp.concatenate(
                [offset[k + i : k + i + 1, t * tile : (t + 1) * tile] for i in range(2)], axis=1
            )
            place[t * 2 * tile : (t + 1) * 2 * tile, k * tile : (k + 2) * tile] = jnp.where(
                row == shift, 1.0, 0.0
            ).astype(bf16)


def lists_kernel(n, margin, neighbors, ahead, *refs):
    m = n // 2
    near, far, own_radial = refs[:3]
    columns, offsets = refs[3:5]
    made = refs[5:8] if ahead else ()
    dists, graph_weight, stacked, filters = refs[5 + len(made) :]
    me = lax.axis_index("fsdp")
    basis = own_radial.shape[0]
    atoms = columns.shape[0] // n
    for d in range(n):
        e = me ^ d
        meta = (far if d % 2 else near)[d // 2 * 4 * SLOT : (d // 2 + 1) * 4 * SLOT].astype(f32)
        offsets[rows_at(e, SLOT)] = meta[:SLOT]
        dists[rows_at(e, SLOT)] = (
            meta[SLOT : 2 * SLOT] + meta[2 * SLOT : 3 * SLOT] + meta[3 * SLOT :]
        )
    slots = lax.broadcasted_iota(jnp.int32, offsets.shape, 0) % SLOT
    ids = jnp.where(slots == neighbors, offsets[...], -1.0)
    weight = jnp.zeros_like(ids)
    for g in range(GRAPHS):
        member = ids == float(g)
        count = jnp.sum(jnp.where(member, 1.0, 0.0), axis=(0, 1), keepdims=True)
        weight = weight + jnp.where(member, lax.rsqrt(jnp.maximum(count, 1.0)), 0.0)
    graph_weight[...] = weight

    def columns_step(e, _):
        dist = dists[rows_at(e, SLOT)]
        envelope = 0.5 * (jnp.cos(jnp.pi * dist / cutoff) + 1.0)
        own = stacked.at[e % stacked.shape[0]]
        for b in range(basis):
            center = cutoff * b / (basis - 1)
            own[b * SLOT : (b + 1) * SLOT] = jnp.exp(-sharpness * (dist - center) ** 2) * envelope
        offset = offsets[rows_at(e, SLOT)]
        for k in range(neighbors):
            at = column_of(k, neighbors)
            own[at : at + 1] = offset[k : k + 1]
        at = column_of(neighbors, neighbors)
        own[at : at + 1] = graph_weight[rows_at(e, SLOT)][neighbors : neighbors + 1]
        columns[rows_at(e, atoms)] = own[...].T
        return 0

    lax.fori_loop(0, n, columns_step, 0, unroll=stacked.shape[0])
    if ahead:
        values, pick, place = made
        fill_filters(neighbors, own_radial, filters)
        fill_values(columns[...], filters, values)

        def block_step(e, _):
            span = neighbors * 2 * margin
            fill_pick(margin, neighbors, columns[rows_at(e, atoms)], pick.at[rows_at(e, span)])
            fill_place(
                margin,
                neighbors,
                offsets[rows_at(e, SLOT)],
                place.at[rows_at(e, 2 * atoms)],
            )
            return 0

        lax.fori_loop(0, n, block_step, 0, unroll=8)


def products_kernel(n, near, far, own_weight, *refs):
    m = n // 2
    feats, cots, refs = refs[:m], refs[m : 2 * m], refs[2 * m :]
    keep, give, held_feats, both, weights = refs
    me = lax.axis_index("fsdp")
    atoms = feats[0].shape[0]
    half = m * atoms
    rows = own_weight.shape[0]
    if rows < LANES:
        both[...] = jnp.zeros_like(both)
    both[:rows] = own_weight[...]
    for q in range(both.shape[1] // LANES):
        start = (2 * m + q) * rows
        both[LANES : LANES + rows, q * LANES : (q + 1) * LANES] = far[start : start + rows]
    for c in range(m):
        for k, source in enumerate((near, far)):
            block = rows_at(me ^ (2 * c + k), rows)
            for i in range(2):
                start = (2 * c + i) * rows
                side = slice(LANES, None) if i != k else slice(0, LANES)
                weights[block, side] = source[start : start + rows]
    for c in range(m):
        piece = feats[c][:atoms]
        held_feats[c * atoms : (c + 1) * atoms] = piece
        projected = jnp.dot(piece, weights[...], preferred_element_type=f32).astype(bf16)
        dact = lax.dot_general(
            cots[c][:atoms], both[...], (((1,), (1,)), ((), ())), preferred_element_type=f32
        ).astype(bf16)
        chip = (me // 2) ^ c
        keep[rows_at(chip, atoms)] = projected[:, :LANES]
        give[rows_at(chip, atoms)] = projected[:, LANES:]
        keep[rows_at(chip + m, atoms)] = dact[:, :LANES]
        give[rows_at(chip + m, atoms)] = dact[:, LANES:]


def forward_kernel(n, margin, neighbors, norm, ahead, *refs):
    own, got, columns, own_radial = refs[:4]
    made = refs[4:6] if ahead else ()
    keep, give, dagg, projected, act = refs[4 + len(made) : 9 + len(made)]
    scratch = refs[9 + len(made) :]
    me = lax.axis_index("fsdp")
    core = me % 2
    atoms = columns.shape[0] // n
    half = n // 2 * atoms
    projected[:margin] = jnp.zeros_like(projected[:margin])
    projected[n * atoms + margin :] = jnp.zeros_like(projected[:margin])
    for c in range(n // 2):
        for source, parity in ((own, core), (got, 1 - core)):
            start = pl.multiple_of((2 * c + parity) * atoms + margin, margin)
            projected[pl.ds(start, atoms)] = source[c * atoms : (c + 1) * atoms]
            dact = source[half + c * atoms : half + (c + 1) * atoms]
            dagg[rows_at(2 * c + parity, atoms)] = dact.astype(f32)
    if ahead:
        values, pick = made
    else:
        filters, values, pick = scratch
        fill_filters(neighbors, own_radial, filters)
    tile = 2 * margin
    span = neighbors * tile

    def block_step(e, _):
        turned = columns[rows_at(e, atoms)]
        if ahead:
            own_values = values.at[rows_at(e, atoms)]
            own_pick = pick[rows_at(e, span)]
        else:
            own_values = values
            fill_values(turned, filters, values)
            fill_pick(margin, neighbors, turned, pick)
            own_pick = pick[...]
        start = pl.multiple_of(e * atoms, atoms)
        halves = []
        for t in range(2):
            found = jnp.dot(
                own_pick[:, t * 2 * tile : (t + 1) * 2 * tile],
                projected[pl.ds(start + t * tile, 2 * tile)],
                preferred_element_type=f32,
            )
            total = jnp.zeros((tile, LANES), f32)
            for k in range(neighbors):
                total = total + (
                    own_values[t * tile : (t + 1) * tile, k * LANES : (k + 1) * LANES]
                    * found[k * tile : (k + 1) * tile]
                )
            halves.append(total)
        agg = jnp.concatenate(halves, axis=0) * norm
        sig = 1.0 / (1.0 + jnp.exp(-agg))
        active = (agg * sig).astype(bf16)
        at = column_of(neighbors, neighbors)
        graph = turned[:, at : at + 1]
        slope = sig * (1.0 + agg * (1.0 - sig)) * (graph * norm)
        dagg[rows_at(e, atoms)] = dagg[rows_at(e, atoms)] * slope
        act[rows_at(e, atoms)] = active
        return 0

    lax.fori_loop(0, n, block_step, 0, unroll=min(n, 8) if ahead else 1)
    for c in range(n // 2):
        keep[c * atoms : (c + 1) * atoms] = act[rows_at(2 * c + core, atoms)]
        give[c * atoms : (c + 1) * atoms] = act[rows_at(2 * c + 1 - core, atoms)]


def backward_kernel(n, margin, neighbors, ahead, *refs):
    m = n // 2
    dagg, own_radial, columns, offsets = refs[:4]
    made = refs[4:6] if ahead else ()
    refs = refs[4 + len(made) :]
    turned, terms, spread = refs[:3]
    scratch = refs[3:]
    me = lax.axis_index("fsdp")
    atoms = columns.shape[0] // n
    tile = 2 * margin
    spread[0, n * atoms :] = jnp.zeros_like(spread[0, n * atoms :])
    spread[1, :tile] = jnp.zeros_like(spread[1, :tile])
    if ahead:
        values, place = made
    else:
        filters, values, place = scratch
        fill_filters(neighbors, own_radial, filters)

    def block_step(e, _):
        flow = dagg[rows_at(e, atoms)]
        if ahead:
            own_values = values.at[rows_at(e, atoms)]
            own_place = place.at[rows_at(e, 2 * atoms)]
        else:
            own_values = values
            fill_values(columns[rows_at(e, atoms)], filters, values)
            fill_place(margin, neighbors, offsets[rows_at(e, SLOT)], place)
            own_place = place
        for t in range(2):
            own = terms.at[2 * (e % (terms.shape[0] // 2)) + t]
            here = slice(t * tile, (t + 1) * tile)
            for k in range(neighbors):
                own[k * tile : (k + 1) * tile] = (
                    own_values[here, k * LANES : (k + 1) * LANES] * flow[here]
                ).astype(bf16)
            window = pl.ds(pl.multiple_of(e * atoms + t * tile, tile), 2 * tile)
            spread[t, window] = jnp.dot(
                own_place[t * 2 * tile : (t + 1) * 2 * tile], own[...], preferred_element_type=f32
            )
        return 0

    lax.fori_loop(0, n, block_step, 0, unroll=min(n, 8) if ahead else 1)

    half = m * atoms
    for k in range(2):
        for c in range(m):
            e = me ^ (2 * c + k)
            start = pl.multiple_of(e * atoms + margin, margin)
            turned[:, k * half + c * atoms : k * half + (c + 1) * atoms] = (
                (spread[0, pl.ds(start, atoms)] + spread[1, pl.ds(start, atoms)]).T.astype(bf16)
            )


def gradient_kernel(n, rows, turned, own_feats, other_feats, *refs):
    m = n // 2
    keep, give, grads = refs
    me = lax.axis_index("fsdp")
    half = own_feats.shape[0]
    total = jnp.dot(turned[:, :half], own_feats[...], preferred_element_type=f32)
    total = total + jnp.dot(turned[:, half:], other_feats[...], preferred_element_type=f32)
    for q in range(total.shape[1] // LANES):
        grads[q * LANES : (q + 1) * LANES] = total[:, q * LANES : (q + 1) * LANES].T
    for c in range(m):
        keep[c * rows : (c + 1) * rows] = grads[rows_at(me ^ (2 * c), rows)].astype(bf16)
        give[c * rows : (c + 1) * rows] = grads[rows_at(me ^ (2 * c + 1), rows)]


def join_kernel(keep, got, *sends):
    rows = sends[0].shape[0]
    for c, send in enumerate(sends):
        send[:, :LANES] = keep[c * rows : (c + 1) * rows]
        send[:, LANES:] = got[c * rows : (c + 1) * rows].astype(bf16)


def write_code(piece, code):
    rows = piece.shape[0]
    scale = (jnp.max(jnp.abs(piece), axis=-1, keepdims=True) + tiny).astype(bf16)
    wide = jnp.broadcast_to(scale.astype(f32), piece.shape)
    code[:rows] = (piece / wide).astype(bf16)
    if rows < LANES:
        wide = jnp.concatenate([wide, jnp.zeros((LANES - rows, LANES), f32)], axis=0)
    code[rows:] = wide.T[:SLOT].astype(bf16)


def chip_kernel(n, margin, neighbors, width, *refs):
    m = n // 2
    columns, keep, got, own_weight, other_weight, _after = refs[:6]
    cots, sends, (own, give) = refs[6 : 6 + m], refs[6 + m : 6 + 2 * m], refs[6 + 2 * m :]
    me = lax.axis_index("fsdp")
    atoms = cots[0].shape[0]
    rows = own.shape[0]
    at = column_of(neighbors, neighbors)
    pieces = own_weight.shape[1] // LANES
    first = other_weight.shape[0] - pieces * rows
    other_weight = jnp.concatenate(
        [other_weight[first + q * rows : first + (q + 1) * rows] for q in range(pieces)], axis=1
    )
    totals = [None, None]
    for c in range(m):
        block = rows_at((me // 2) ^ c, atoms)
        sends[c][...] = (
            jnp.dot(keep[block][:, :width], own_weight[...], preferred_element_type=f32)
            + jnp.dot(got[block][:, :width], other_weight, preferred_element_type=f32)
        ).astype(bf16)
        graph = columns[rows_at(me ^ (2 * c), atoms)][:, at : at + 1]
        for i, act in enumerate((keep, got)):
            left = (act[block].astype(f32) * graph).T.astype(bf16)
            term = jnp.dot(left, cots[c][:atoms], preferred_element_type=f32)
            totals[i] = term if c == 0 else totals[i] + term
    own[...] = totals[0][:rows]
    give[...] = totals[1][:rows].astype(bf16)


def grads_kernel(n, fragment, *refs):
    m = n // 2
    near, got_part, own_part = refs[:m], refs[m], refs[m + 1]
    msg_grad, out_grad, code, blocks, total = refs[m + 2 :]
    me = lax.axis_index("fsdp")
    rows = msg_grad.shape[1]
    width = msg_grad.shape[2] // n
    lanes = pl.ds(pl.multiple_of(fragment[0] * FRAG, FRAG), FRAG)
    for c in range(m):
        blocks[me ^ (2 * c)] = near[c][:, :LANES]
        blocks[me ^ (2 * c + 1)] = near[c][:, LANES:]
    for e in range(n):
        msg_grad[0, :, e * width : (e + 1) * width] = blocks[e][:, :width]
    write_code(msg_grad[0, :, lanes].astype(f32), code.at[: rows + SLOT])
    total[...] = own_part[...] + got_part[...].astype(f32)
    out_grad[0] = total[...].astype(bf16)
    write_code(total[:, lanes], code.at[rows + SLOT :])


def pair_kernel(*refs):
    codes, out = refs[:-1], refs[-1]
    rows = out.shape[1]
    for piece in range(2):
        total = jnp.zeros((rows, FRAG), f32)
        for code in codes:
            own = code.at[piece * (rows + SLOT) : (piece + 1) * (rows + SLOT)]
            wide = jnp.broadcast_to(own[rows:].astype(f32)[:1], (LANES, LANES)).T
            total = total + wide[:rows] * own[:rows].astype(f32)
        out[piece] = total.astype(out.dtype)


def outer_kernel(own, other, out):
    out[...] = (own[...].astype(f32) + other[...].astype(f32)).astype(out.dtype)


def last_kernel(count, *refs):
    pair, (feats, *parts), (outer, node) = refs[:count], refs[count:-2], refs[-2:]
    outer[...] = functools.reduce(jnp.add, [value[...].astype(f32) for value in pair])
    total = feats[...].astype(f32)
    for part in parts:
        total = total + part[...].astype(f32)
    node[...] = total.astype(bf16)


def run(kernel, outs, scratch, args, micros, memory=16, scalars=0, outside=0):
    whole = pl.BlockSpec(memory_space=pltpu.VMEM)
    scalar = pl.BlockSpec(memory_space=pltpu.SMEM)
    remote = pl.BlockSpec(memory_space=pltpu.HBM)
    return pl.pallas_call(
        kernel,
        out_shape=[jax.ShapeDtypeStruct(shape, dtype) for shape, dtype in outs],
        in_specs=[scalar] * scalars
        + [whole] * (len(args) - scalars - outside)
        + [remote] * outside,
        out_specs=[whole] * len(outs),
        scratch_shapes=[
            pltpu.SemaphoreType.DMA(shape) if dtype is None else pltpu.VMEM(shape, dtype)
            for shape, dtype in scratch
        ],
        compiler_params=pltpu.CompilerParams(vmem_limit_bytes=memory << 20),
        cost_estimate=pl.CostEstimate(
            flops=int(micros * 1e9), bytes_accessed=int(micros * 3e6), transcendentals=0
        ),
    )(*args)


def after(values, other, micros):
    anywhere = pl.BlockSpec(memory_space=pl.ANY)
    return pl.pallas_call(
        gate_kernel,
        out_shape=[jax.ShapeDtypeStruct(value.shape, value.dtype) for value in values],
        in_specs=[anywhere] * (len(values) + 1),
        out_specs=[anywhere] * len(values),
        input_output_aliases={i: i for i in range(len(values))},
        compiler_params=pltpu.CompilerParams(vmem_limit_bytes=1 << 20),
        cost_estimate=pl.CostEstimate(
            flops=int(micros * 1e9), bytes_accessed=int(micros * 3e6), transcendentals=0
        ),
    )(*values, other)


def hop(value, axis, step):
    count = lax.axis_size(axis)
    return lax.ppermute(value, axis, [(i, i ^ step) for i in range(count)])


def across_chips(sends):
    return [sends[0]] + [hop(sends[c], "fsdp", 2 * c) for c in range(1, len(sends))]


def exchanged(value, held, m, side):
    pieces = {0: value, **held}
    for c in range(1, m):
        if c not in pieces:
            used = [1 << i for i in range(m.bit_length()) if c >> i & 1][side]
            pieces[c] = hop(pieces[c ^ used], "fsdp", 2 * used)
    return [pieces[c] for c in range(m)]


def shards(
    node_feats,
    neighbor_src,
    distances,
    graph_ids,
    msg_weight,
    out_weight,
    radial_weight,
    cotangent,
    fragment,
):
    n = lax.axis_size("fsdp")
    replicas = lax.axis_size("replica")
    m = n // 2
    atoms, channels = node_feats.shape
    neighbors = neighbor_src.shape[0]
    basis = radial_weight.shape[0]
    rows = msg_weight.shape[0]
    width = channels // n
    margin = atoms // 4
    norm = 1.0 / math.sqrt(neighbors)
    all_atoms = n * atoms
    lanes = neighbors * LANES
    ahead = all_atoms * lanes * 4 <= 8 << 20
    memory = 24 if ahead else 56
    step_scratch = [
        ((2 * basis * SLOT, lanes), bf16),
        ((atoms, lanes), f32),
    ]

    pack_inputs = [
        msg_weight,
        neighbor_src,
        distances,
        graph_ids,
        radial_weight,
        node_feats,
        cotangent,
    ]
    bundle = 2 * rows + 4 * SLOT
    wide = (atoms + chunk_of(bundle, channels // LANES), channels)
    *packed, wide_feats, wide_cot, own_radial = run(
        functools.partial(pack_kernel, n, width),
        [((bundle, LANES), bf16)] * (m - 2) + [(wide, bf16)] * 2 + [((basis, LANES), f32)],
        [
            ((n, rows, LANES), bf16),
            ((n, basis, LANES), f32),
            ((SLOT, LANES), f32),
            ((bundle, LANES), bf16),
        ]
        + [(piece.shape, piece.dtype) for piece in pack_inputs]
        + [((len(pack_inputs),), None)],
        pack_inputs,
        1,
        60,
        outside=len(pack_inputs),
    )
    others = [c for c in range(1, m) if c not in (1, m // 2)]
    feats = exchanged(node_feats, {1: hop(wide_feats, "fsdp", 2)}, m, 0)
    cots = exchanged(cotangent, {m // 2: hop(wide_cot, "fsdp", 2 * (m // 2))}, m, -1)
    own_feats, own_cot, near_lists, near_weights = run(
        functools.partial(merge_kernel, m, rows),
        [((atoms, channels), bf16)] * 2
        + [
            ((m * 4 * SLOT, LANES), bf16),
            (((2 * m + channels // LANES) * rows, LANES), bf16),
        ],
        [((bundle, LANES), bf16)],
        [packed[0]]
        + list(after([hop(value, "fsdp", 2 * c) for c, value in zip(others, packed[1:])], own_radial, 10))
        + [feats[1], cots[m // 2], out_weight, node_feats, cotangent],
        0,
        memory,
    )
    far_weights = hop(near_weights, "fsdp", 1)
    columns, offsets, *made = run(
        functools.partial(lists_kernel, n, margin, neighbors, ahead),
        [
            ((all_atoms, LANES), f32),
            ((n * SLOT, LANES), f32),
        ]
        + [
            ((all_atoms, lanes), f32),
            ((n * neighbors * 2 * margin, 8 * margin), bf16),
            ((2 * all_atoms, neighbors * 2 * margin), bf16),
        ]
        * ahead,
        [
            ((n * SLOT, LANES), f32),
            ((n * SLOT, LANES), f32),
            ((min(n, 8), basis * SLOT, LANES), f32),
            ((2 * basis * SLOT, lanes), bf16),
        ],
        [near_lists, hop(near_lists, "fsdp", 1), own_radial],
        0,
        memory,
    )
    feats[0], cots[0] = own_feats, own_cot
    passed = [(pieces, c) for pieces in (feats, cots) for c in range(1, m) if c & (c - 1)]
    held = after([pieces[c] for pieces, c in passed], offsets, 10)
    for (pieces, c), value in zip(passed, held):
        pieces[c] = value
    own_products, give_products, held_feats = run(
        functools.partial(products_kernel, n),
        [((all_atoms, LANES), bf16)] * 2 + [((all_atoms // 2, channels), bf16)],
        [((2 * LANES, channels), bf16), ((channels, 2 * LANES), bf16)],
        [near_weights, far_weights, out_weight, *feats, *cots],
        1,
        memory,
    )
    got_products = hop(give_products, "fsdp", 1)
    (held_feats,) = after([held_feats], got_products, 0)
    keep, give, dagg = run(
        functools.partial(forward_kernel, n, margin, neighbors, norm, ahead),
        [
            ((all_atoms // 2, LANES), bf16),
            ((all_atoms // 2, LANES), bf16),
            ((all_atoms, LANES), f32),
        ],
        [((all_atoms + 2 * margin, LANES), bf16), ((all_atoms, LANES), bf16)]
        + (step_scratch + [((neighbors * 2 * margin, 8 * margin), bf16)]) * (not ahead),
        [own_products, got_products, columns, own_radial, *made[:2]],
        1,
        memory,
    )
    other_act = hop(give, "fsdp", 1)
    (turned,) = run(
        functools.partial(backward_kernel, n, margin, neighbors, ahead),
        [((LANES, all_atoms), bf16)],
        [
            ((2 * min(n, 8) if ahead else 2, neighbors * 2 * margin, LANES), bf16),
            ((2, all_atoms + 2 * margin, LANES), f32),
        ]
        + (step_scratch + [((2 * atoms, neighbors * 2 * margin), bf16)]) * (not ahead),
        [dagg, own_radial, columns, offsets, *made[::2]],
        1,
        memory,
    )
    keep_grads, give_grads = run(
        functools.partial(gradient_kernel, n, rows),
        [((m * rows, LANES), bf16), ((m * rows, LANES), f32)],
        [((channels, LANES), f32)],
        [turned, held_feats, hop(held_feats, "fsdp", 1)],
        1,
        memory,
    )
    *sums, own_part, give_part = run(
        functools.partial(chip_kernel, n, margin, neighbors, width),
        [((atoms, channels), bf16)] * m + [((rows, channels), f32), ((rows, channels), bf16)],
        [],
        [columns, keep, other_act, out_weight, far_weights, give_grads, *cots],
        1,
        memory,
    )
    grad_sends = run(
        join_kernel,
        [((rows, 2 * LANES), bf16)] * m,
        [],
        [keep_grads, hop(give_grads, "fsdp", 1)],
        0,
        memory,
    )
    near = across_chips(grad_sends)
    grad_msg, grad_out, code = run(
        functools.partial(grads_kernel, n),
        [((1, rows, channels), bf16)] * 2 + [((2 * (rows + SLOT), FRAG), bf16)],
        [((n, rows, LANES), bf16), ((rows, channels), f32)],
        [fragment, *near, hop(give_part, "fsdp", 1), own_part],
        4,
        memory,
        scalars=1,
    )
    sums = across_chips(sums)
    step = 1
    codes = [code]
    if replicas > 1:
        codes.append(hop(code, "replica", step))
    (outer_sum,) = run(
        pair_kernel, [((2, rows, FRAG), f32 if replicas <= 2 else bf16)], [], codes, 0, memory
    )
    while 4 * step < replicas:
        step = 2 * step
        (outer_sum,) = run(
            outer_kernel,
            [((2, rows, FRAG), bf16)],
            [],
            [outer_sum, hop(outer_sum, "replica", step)],
            0,
            memory,
        )
    pair = [outer_sum]
    if replicas > 2:
        pair.append(hop(outer_sum, "replica", 2 * step))
    outer_sum, node_out = run(
        functools.partial(last_kernel, len(pair)),
        [((2, rows, FRAG), f32), ((atoms, channels), bf16)],
        [],
        [*pair, node_feats, *sums],
        0,
        memory,
    )
    return node_out, grad_msg, grad_out, outer_sum


def solution(mesh):
    placed = (
        P(("replica", "fsdp"), None),
        P(None, ("replica", "fsdp")),
        P(None, ("replica", "fsdp")),
        P("replica", "fsdp"),
        P("fsdp", None),
        P("fsdp", None),
        P(),
        P(("replica", "fsdp"), None),
        P(),
    )
    return jax.shard_map(
        shards,
        mesh=mesh,
        in_specs=placed,
        out_specs=(
            P(("replica", "fsdp"), None),
            P("replica", "fsdp", None),
            P("replica", "fsdp", None),
            P(None, "fsdp", None),
        ),
        check_vma=False,
    )
```

```python
import functools
import math

import jax
import jax.numpy as jnp
from jax import lax
from jax.experimental import pallas as pl
from jax.experimental.pallas import tpu as pltpu
from jax.sharding import PartitionSpec as P

FRAG = 128
GRAPHS = 8
LANES = 128
SLOT = 16

cutoff = 5.0
sharpness = 2.0
tiny = 1e-06

bf16 = jnp.bfloat16
f32 = jnp.float32


def rows_at(index, count):
    return pl.ds(pl.multiple_of(index * count, count), count)


def column_of(k, neighbors):
    free = SLOT - neighbors
    return (k // free) * SLOT + neighbors + k % free


def chunk_of(rows, pieces):
    return -(-rows // (pieces * SLOT)) * SLOT


def pack_kernel(n, width, *refs):
    far, refs = refs[:7], refs[7:]
    m = n // 2
    packed, (feats_out, cot_out, own_radial) = refs[: m - 2], refs[m - 2 : m + 1]
    (blocks, radials, group, bundle), refs = refs[m + 1 : m + 5], refs[m + 5 :]
    held, done = refs[:7], refs[7]
    copies = [pltpu.make_async_copy(a, b, done.at[i]) for i, (a, b) in enumerate(zip(far, held))]
    for copy in copies:
        copy.start()
    for copy in copies:
        copy.wait()
    weight, src, dist, ids, radial_weight, feats, cot = held
    me = lax.axis_index("fsdp")
    rows = weight.shape[0]
    neighbors, atoms = src.shape
    if width < LANES:
        blocks[...] = jnp.zeros_like(blocks)
        radials[...] = jnp.zeros_like(radials)
    for e in range(n):
        blocks[e, :, :width] = weight[:, e * width : (e + 1) * width]
        radials[e, :, :width] = radial_weight[:, e * width : (e + 1) * width]
    own_radial[...] = radials[me]
    position = lax.broadcasted_iota(jnp.int32, src.shape, 1) + me * atoms
    group[...] = jnp.zeros_like(group)
    group[:neighbors] = (src[...] - position).astype(f32)
    group[neighbors : neighbors + 1] = ids[...].astype(f32)
    meta = [group[...].astype(bf16)]
    group[...] = jnp.ones_like(group)
    group[:neighbors] = dist[...]
    left = group[...]
    for _ in range(3):
        part = left.astype(bf16)
        meta.append(part)
        left = left - part.astype(f32)
    feats_out[:atoms] = feats[...]
    cot_out[:atoms] = cot[...]
    direct = 0
    for c in range(m):
        wide = {1: feats_out, m // 2: cot_out}.get(c)
        if wide is None:
            target = packed[direct]
            direct += 1
        else:
            target = bundle
        target[:rows] = blocks[me ^ (2 * c)]
        target[rows : 2 * rows] = blocks[me ^ (2 * c + 1)]
        for i, part in enumerate(meta):
            target[2 * rows + i * SLOT : 2 * rows + (i + 1) * SLOT] = part
        if wide is not None:
            size = wide.shape[0] - atoms
            for q in range(wide.shape[1] // LANES):
                stop = min((q + 1) * size, bundle.shape[0])
                if stop > q * size:
                    wide[atoms : atoms + stop - q * size, q * LANES : (q + 1) * LANES] = bundle[
                        q * size : stop
                    ]


def merge_kernel(m, rows, *refs):
    direct, (feats, cot, own_weight), refs = list(refs[: m - 2]), refs[m - 2 : m + 1], refs[m + 1 :]
    for value, held in zip(refs[:2], refs[2:4]):
        held[...] = value[...]
    lists, weights, bundle = refs[4:]
    size = 4 * SLOT
    for c in range(m):
        wide = {1: feats, m // 2: cot}.get(c)
        if wide is None:
            source = direct.pop(0)
        else:
            source = bundle
            height = chunk_of(bundle.shape[0], wide.shape[1] // LANES)
            for q in range(wide.shape[1] // LANES):
                stop = min((q + 1) * height, bundle.shape[0])
                if stop > q * height:
                    bundle[q * height : stop] = wide[
                        wide.shape[0] - height : wide.shape[0] - height + stop - q * height,
                        q * LANES : (q + 1) * LANES,
                    ]
        weights[2 * c * rows : 2 * (c + 1) * rows] = source[: 2 * rows]
        lists[c * size : (c + 1) * size] = source[2 * rows :]
    for q in range(own_weight.shape[1] // LANES):
        start = (2 * m + q) * rows
        weights[start : start + rows] = own_weight[:, q * LANES : (q + 1) * LANES]


def gate_kernel(*_):
    pass


def fill_filters(neighbors, own_radial, filters):
    basis = own_radial.shape[0]
    half = basis * SLOT
    row = lax.broadcasted_iota(jnp.int32, (half, LANES), 0) % SLOT
    spread = jnp.concatenate(
        [jnp.broadcast_to(own_radial[b : b + 1], (SLOT, LANES)) for b in range(basis)], axis=0
    )
    high = spread.astype(bf16).astype(f32)
    low = spread - high
    for k in range(neighbors):
        lanes = slice(k * LANES, (k + 1) * LANES)
        filters[:half, lanes] = jnp.where(row == k, high, 0.0).astype(bf16)
        filters[half:, lanes] = jnp.where(row == k, low, 0.0).astype(bf16)


def fill_values(columns, filters, values):
    high = columns.astype(bf16)
    both = jnp.concatenate([high, high], axis=1)
    span = 2 * LANES

    def step(j, _):
        lanes = pl.ds(pl.multiple_of(j * span, span), span)
        values[:, lanes] = jnp.dot(both, filters[:, lanes], preferred_element_type=f32)
        return 0

    steps = values.shape[1] // span
    lax.fori_loop(0, steps, step, 0, unroll=steps)


def fill_pick(margin, neighbors, turned, pick):
    tile = 2 * margin
    tiles = turned.shape[0] // tile
    shift = (
        lax.broadcasted_iota(jnp.int32, (tile, 2 * tile), 1)
        - lax.broadcasted_iota(jnp.int32, (tile, 2 * tile), 0)
        - margin
    ).astype(f32)
    for t in range(tiles):
        own = turned[t * tile : (t + 1) * tile]
        for k in range(neighbors):
            at = column_of(k, neighbors)
            pick[k * tile : (k + 1) * tile, t * 2 * tile : (t + 1) * 2 * tile] = jnp.where(
                own[:, at : at + 1] == shift, 1.0, 0.0
            ).astype(bf16)


def fill_place(margin, neighbors, offset, place):
    tile = 2 * margin
    shape = (2 * tile, 2 * tile)
    shift = (
        lax.broadcasted_iota(jnp.int32, shape, 0)
        - lax.broadcasted_iota(jnp.int32, shape, 1) % tile
        - margin
    ).astype(f32)
    for t in range(offset.shape[1] // tile):
        for k in range(0, neighbors, 2):
            row = jnp.concatenate(
                [offset[k + i : k + i + 1, t * tile : (t + 1) * tile] for i in range(2)], axis=1
            )
            place[t * 2 * tile : (t + 1) * 2 * tile, k * tile : (k + 2) * tile] = jnp.where(
                row == shift, 1.0, 0.0
            ).astype(bf16)


def lists_kernel(n, margin, neighbors, ahead, *refs):
    m = n // 2
    near, far, own_radial = refs[:3]
    columns, offsets = refs[3:5]
    made = refs[5:8] if ahead else ()
    dists, graph_weight, stacked, filters = refs[5 + len(made) :]
    me = lax.axis_index("fsdp")
    basis = own_radial.shape[0]
    atoms = columns.shape[0] // n
    for d in range(n):
        e = me ^ d
        meta = (far if d % 2 else near)[d // 2 * 4 * SLOT : (d // 2 + 1) * 4 * SLOT].astype(f32)
        offsets[rows_at(e, SLOT)] = meta[:SLOT]
        dists[rows_at(e, SLOT)] = (
            meta[SLOT : 2 * SLOT] + meta[2 * SLOT : 3 * SLOT] + meta[3 * SLOT :]
        )
    slots = lax.broadcasted_iota(jnp.int32, offsets.shape, 0) % SLOT
    ids = jnp.where(slots == neighbors, offsets[...], -1.0)
    weight = jnp.zeros_like(ids)
    for g in range(GRAPHS):
        member = ids == float(g)
        count = jnp.sum(jnp.where(member, 1.0, 0.0), axis=(0, 1), keepdims=True)
        weight = weight + jnp.where(member, lax.rsqrt(jnp.maximum(count, 1.0)), 0.0)
    graph_weight[...] = weight

    def columns_step(e, _):
        dist = dists[rows_at(e, SLOT)]
        envelope = 0.5 * (jnp.cos(jnp.pi * dist / cutoff) + 1.0)
        own = stacked.at[e % stacked.shape[0]]
        for b in range(basis):
            center = cutoff * b / (basis - 1)
            own[b * SLOT : (b + 1) * SLOT] = jnp.exp(-sharpness * (dist - center) ** 2) * envelope
        offset = offsets[rows_at(e, SLOT)]
        for k in range(neighbors):
            at = column_of(k, neighbors)
            own[at : at + 1] = offset[k : k + 1]
        at = column_of(neighbors, neighbors)
        own[at : at + 1] = graph_weight[rows_at(e, SLOT)][neighbors : neighbors + 1]
        columns[rows_at(e, atoms)] = own[...].T
        return 0

    lax.fori_loop(0, n, columns_step, 0, unroll=stacked.shape[0])
    if ahead:
        values, pick, place = made
        fill_filters(neighbors, own_radial, filters)
        fill_values(columns[...], filters, values)

        def block_step(e, _):
            span = neighbors * 2 * margin
            fill_pick(margin, neighbors, columns[rows_at(e, atoms)], pick.at[rows_at(e, span)])
            fill_place(
                margin,
                neighbors,
                offsets[rows_at(e, SLOT)],
                place.at[rows_at(e, 2 * atoms)],
            )
            return 0

        lax.fori_loop(0, n, block_step, 0, unroll=8)


def products_kernel(n, near, far, own_weight, *refs):
    m = n // 2
    feats, cots, refs = refs[:m], refs[m : 2 * m], refs[2 * m :]
    keep, give, held_feats, both, weights = refs
    me = lax.axis_index("fsdp")
    atoms = feats[0].shape[0]
    half = m * atoms
    rows = own_weight.shape[0]
    if rows < LANES:
        both[...] = jnp.zeros_like(both)
    both[:rows] = own_weight[...]
    for q in range(both.shape[1] // LANES):
        start = (2 * m + q) * rows
        both[LANES : LANES + rows, q * LANES : (q + 1) * LANES] = far[start : start + rows]
    for c in range(m):
        for k, source in enumerate((near, far)):
            block = rows_at(me ^ (2 * c + k), rows)
            for i in range(2):
                start = (2 * c + i) * rows
                side = slice(LANES, None) if i != k else slice(0, LANES)
                weights[block, side] = source[start : start + rows]
    for c in range(m):
        held_feats[c * atoms : (c + 1) * atoms] = feats[c][:atoms]
    projected = jnp.dot(held_feats[...], weights[...], preferred_element_type=f32).astype(bf16)
    flow = jnp.concatenate([cots[c][:atoms] for c in range(m)], axis=0)
    dact = lax.dot_general(
        flow, both[...], (((1,), (1,)), ((), ())), preferred_element_type=f32
    ).astype(bf16)
    for c in range(m):
        chip = (me // 2) ^ c
        here = slice(c * atoms, (c + 1) * atoms)
        keep[rows_at(chip, atoms)] = projected[here, :LANES]
        give[rows_at(chip, atoms)] = projected[here, LANES:]
        keep[rows_at(chip + m, atoms)] = dact[here, :LANES]
        give[rows_at(chip + m, atoms)] = dact[here, LANES:]


def forward_kernel(n, margin, neighbors, norm, ahead, *refs):
    own, got, columns, own_radial = refs[:4]
    made = refs[4:6] if ahead else ()
    keep, give, dagg, projected, act = refs[4 + len(made) : 9 + len(made)]
    scratch = refs[9 + len(made) :]
    me = lax.axis_index("fsdp")
    core = me % 2
    atoms = columns.shape[0] // n
    half = n // 2 * atoms
    projected[:margin] = jnp.zeros_like(projected[:margin])
    projected[n * atoms + margin :] = jnp.zeros_like(projected[:margin])
    for c in range(n // 2):
        for source, parity in ((own, core), (got, 1 - core)):
            start = pl.multiple_of((2 * c + parity) * atoms + margin, margin)
            projected[pl.ds(start, atoms)] = source[c * atoms : (c + 1) * atoms]
            dact = source[half + c * atoms : half + (c + 1) * atoms]
            dagg[rows_at(2 * c + parity, atoms)] = dact.astype(f32)
    if ahead:
        values, pick = made
    else:
        filters, values, pick = scratch
        fill_filters(neighbors, own_radial, filters)
    tile = 2 * margin
    span = neighbors * tile

    def block_step(e, _):
        turned = columns[rows_at(e, atoms)]
        if ahead:
            own_values = values.at[rows_at(e, atoms)]
            own_pick = pick[rows_at(e, span)]
        else:
            own_values = values
            fill_values(turned, filters, values)
            fill_pick(margin, neighbors, turned, pick)
            own_pick = pick[...]
        start = pl.multiple_of(e * atoms, atoms)
        halves = []
        for t in range(2):
            found = jnp.dot(
                own_pick[:, t * 2 * tile : (t + 1) * 2 * tile],
                projected[pl.ds(start + t * tile, 2 * tile)],
                preferred_element_type=f32,
            )
            total = jnp.zeros((tile, LANES), f32)
            for k in range(neighbors):
                total = total + (
                    own_values[t * tile : (t + 1) * tile, k * LANES : (k + 1) * LANES]
                    * found[k * tile : (k + 1) * tile]
                )
            halves.append(total)
        agg = jnp.concatenate(halves, axis=0) * norm
        sig = 1.0 / (1.0 + jnp.exp(-agg))
        active = (agg * sig).astype(bf16)
        at = column_of(neighbors, neighbors)
        graph = turned[:, at : at + 1]
        slope = sig * (1.0 + agg * (1.0 - sig)) * (graph * norm)
        dagg[rows_at(e, atoms)] = dagg[rows_at(e, atoms)] * slope
        act[rows_at(e, atoms)] = active
        return 0

    lax.fori_loop(0, n, block_step, 0, unroll=min(n, 8) if ahead else 1)
    for c in range(n // 2):
        keep[c * atoms : (c + 1) * atoms] = act[rows_at(2 * c + core, atoms)]
        give[c * atoms : (c + 1) * atoms] = act[rows_at(2 * c + 1 - core, atoms)]


def backward_kernel(n, margin, neighbors, ahead, *refs):
    m = n // 2
    dagg, own_radial, columns, offsets = refs[:4]
    made = refs[4:6] if ahead else ()
    refs = refs[4 + len(made) :]
    turned, terms, spread = refs[:3]
    scratch = refs[3:]
    me = lax.axis_index("fsdp")
    atoms = columns.shape[0] // n
    tile = 2 * margin
    spread[0, n * atoms :] = jnp.zeros_like(spread[0, n * atoms :])
    spread[1, :tile] = jnp.zeros_like(spread[1, :tile])
    if ahead:
        values, place = made
    else:
        filters, values, place = scratch
        fill_filters(neighbors, own_radial, filters)

    def block_step(e, _):
        flow = dagg[rows_at(e, atoms)]
        if ahead:
            own_values = values.at[rows_at(e, atoms)]
            own_place = place.at[rows_at(e, 2 * atoms)]
        else:
            own_values = values
            fill_values(columns[rows_at(e, atoms)], filters, values)
            fill_place(margin, neighbors, offsets[rows_at(e, SLOT)], place)
            own_place = place
        for t in range(2):
            own = terms.at[2 * (e % (terms.shape[0] // 2)) + t]
            here = slice(t * tile, (t + 1) * tile)
            for k in range(neighbors):
                own[k * tile : (k + 1) * tile] = (
                    own_values[here, k * LANES : (k + 1) * LANES] * flow[here]
                ).astype(bf16)
            window = pl.ds(pl.multiple_of(e * atoms + t * tile, tile), 2 * tile)
            spread[t, window] = jnp.dot(
                own_place[t * 2 * tile : (t + 1) * 2 * tile], own[...], preferred_element_type=f32
            )
        return 0

    lax.fori_loop(0, n, block_step, 0, unroll=min(n, 8) if ahead else 1)

    half = m * atoms
    for k in range(2):
        for c in range(m):
            e = me ^ (2 * c + k)
            start = pl.multiple_of(e * atoms + margin, margin)
            turned[:, k * half + c * atoms : k * half + (c + 1) * atoms] = (
                (spread[0, pl.ds(start, atoms)] + spread[1, pl.ds(start, atoms)]).T.astype(bf16)
            )


def gradient_kernel(n, rows, turned, own_feats, other_feats, *refs):
    m = n // 2
    keep, give, grads = refs
    me = lax.axis_index("fsdp")
    half = own_feats.shape[0]
    total = jnp.dot(turned[:, :half], own_feats[...], preferred_element_type=f32)
    total = total + jnp.dot(turned[:, half:], other_feats[...], preferred_element_type=f32)
    for q in range(total.shape[1] // LANES):
        grads[q * LANES : (q + 1) * LANES] = total[:, q * LANES : (q + 1) * LANES].T
    for c in range(m):
        keep[c * rows : (c + 1) * rows] = grads[rows_at(me ^ (2 * c), rows)].astype(bf16)
        give[c * rows : (c + 1) * rows] = grads[rows_at(me ^ (2 * c + 1), rows)]


def join_kernel(keep, got, *sends):
    rows = sends[0].shape[0]
    for c, send in enumerate(sends):
        send[:, :LANES] = keep[c * rows : (c + 1) * rows]
        send[:, LANES:] = got[c * rows : (c + 1) * rows].astype(bf16)


def write_code(piece, code):
    rows = piece.shape[0]
    scale = (jnp.max(jnp.abs(piece), axis=-1, keepdims=True) + tiny).astype(bf16)
    wide = jnp.broadcast_to(scale.astype(f32), piece.shape)
    code[:rows] = (piece / wide).astype(bf16)
    if rows < LANES:
        wide = jnp.concatenate([wide, jnp.zeros((LANES - rows, LANES), f32)], axis=0)
    code[rows:] = wide.T[:SLOT].astype(bf16)


def chip_kernel(n, margin, neighbors, width, *refs):
    m = n // 2
    columns, keep, got, own_weight, other_weight, _after = refs[:6]
    cots, sends, (own, give) = refs[6 : 6 + m], refs[6 + m : 6 + 2 * m], refs[6 + 2 * m :]
    me = lax.axis_index("fsdp")
    atoms = cots[0].shape[0]
    rows = own.shape[0]
    at = column_of(neighbors, neighbors)
    pieces = own_weight.shape[1] // LANES
    first = other_weight.shape[0] - pieces * rows
    other_weight = jnp.concatenate(
        [other_weight[first + q * rows : first + (q + 1) * rows] for q in range(pieces)], axis=1
    )
    acts = [
        jnp.concatenate([act[rows_at((me // 2) ^ c, atoms)] for c in range(m)], axis=0)
        for act in (keep, got)
    ]
    total = jnp.dot(acts[0][:, :width], own_weight[...], preferred_element_type=f32) + jnp.dot(
        acts[1][:, :width], other_weight, preferred_element_type=f32
    )
    for c in range(m):
        sends[c][...] = total[c * atoms : (c + 1) * atoms].astype(bf16)
    graph = jnp.concatenate(
        [columns[rows_at(me ^ (2 * c), atoms)][:, at : at + 1] for c in range(m)], axis=0
    )
    left = jnp.concatenate([(act.astype(f32) * graph).T.astype(bf16) for act in acts], axis=0)
    flow = jnp.concatenate([cots[c][:atoms] for c in range(m)], axis=0)
    parts = jnp.dot(left, flow, preferred_element_type=f32)
    own[...] = parts[:rows]
    give[...] = parts[LANES : LANES + rows].astype(bf16)


def grads_kernel(n, fragment, *refs):
    m = n // 2
    near, got_part, own_part = refs[:m], refs[m], refs[m + 1]
    msg_grad, out_grad, code, blocks, total = refs[m + 2 :]
    me = lax.axis_index("fsdp")
    rows = msg_grad.shape[1]
    width = msg_grad.shape[2] // n
    lanes = pl.ds(pl.multiple_of(fragment[0] * FRAG, FRAG), FRAG)
    for c in range(m):
        blocks[me ^ (2 * c)] = near[c][:, :LANES]
        blocks[me ^ (2 * c + 1)] = near[c][:, LANES:]
    for e in range(n):
        msg_grad[0, :, e * width : (e + 1) * width] = blocks[e][:, :width]
    write_code(msg_grad[0, :, lanes].astype(f32), code.at[: rows + SLOT])
    total[...] = own_part[...] + got_part[...].astype(f32)
    out_grad[0] = total[...].astype(bf16)
    write_code(total[:, lanes], code.at[rows + SLOT :])


def pair_kernel(*refs):
    codes, out = refs[:-1], refs[-1]
    rows = out.shape[1]
    for piece in range(2):
        total = jnp.zeros((rows, FRAG), f32)
        for code in codes:
            own = code.at[piece * (rows + SLOT) : (piece + 1) * (rows + SLOT)]
            wide = jnp.broadcast_to(own[rows:].astype(f32)[:1], (LANES, LANES)).T
            total = total + wide[:rows] * own[:rows].astype(f32)
        out[piece] = total.astype(out.dtype)


def outer_kernel(own, other, out):
    out[...] = (own[...].astype(f32) + other[...].astype(f32)).astype(out.dtype)


def last_kernel(count, *refs):
    pair, (feats, *parts), (outer, node) = refs[:count], refs[count:-2], refs[-2:]
    outer[...] = functools.reduce(jnp.add, [value[...].astype(f32) for value in pair])
    total = feats[...].astype(f32)
    for part in parts:
        total = total + part[...].astype(f32)
    node[...] = total.astype(bf16)


def run(kernel, outs, scratch, args, micros, memory=16, scalars=0, outside=0):
    whole = pl.BlockSpec(memory_space=pltpu.VMEM)
    scalar = pl.BlockSpec(memory_space=pltpu.SMEM)
    remote = pl.BlockSpec(memory_space=pltpu.HBM)
    return pl.pallas_call(
        kernel,
        out_shape=[jax.ShapeDtypeStruct(shape, dtype) for shape, dtype in outs],
        in_specs=[scalar] * scalars
        + [whole] * (len(args) - scalars - outside)
        + [remote] * outside,
        out_specs=[whole] * len(outs),
        scratch_shapes=[
            pltpu.SemaphoreType.DMA(shape) if dtype is None else pltpu.VMEM(shape, dtype)
            for shape, dtype in scratch
        ],
        compiler_params=pltpu.CompilerParams(vmem_limit_bytes=memory << 20),
        cost_estimate=pl.CostEstimate(
            flops=int(micros * 1e9), bytes_accessed=int(micros * 3e6), transcendentals=0
        ),
    )(*args)


def after(values, other, micros):
    anywhere = pl.BlockSpec(memory_space=pl.ANY)
    return pl.pallas_call(
        gate_kernel,
        out_shape=[jax.ShapeDtypeStruct(value.shape, value.dtype) for value in values],
        in_specs=[anywhere] * (len(values) + 1),
        out_specs=[anywhere] * len(values),
        input_output_aliases={i: i for i in range(len(values))},
        compiler_params=pltpu.CompilerParams(vmem_limit_bytes=1 << 20),
        cost_estimate=pl.CostEstimate(
            flops=int(micros * 1e9), bytes_accessed=int(micros * 3e6), transcendentals=0
        ),
    )(*values, other)


def hop(value, axis, step):
    count = lax.axis_size(axis)
    return lax.ppermute(value, axis, [(i, i ^ step) for i in range(count)])


def across_chips(sends):
    return [sends[0]] + [hop(sends[c], "fsdp", 2 * c) for c in range(1, len(sends))]


def exchanged(value, held, m, side):
    pieces = {0: value, **held}
    for c in range(1, m):
        if c not in pieces:
            used = [1 << i for i in range(m.bit_length()) if c >> i & 1][side]
            pieces[c] = hop(pieces[c ^ used], "fsdp", 2 * used)
    return [pieces[c] for c in range(m)]


def shards(
    node_feats,
    neighbor_src,
    distances,
    graph_ids,
    msg_weight,
    out_weight,
    radial_weight,
    cotangent,
    fragment,
):
    n = lax.axis_size("fsdp")
    replicas = lax.axis_size("replica")
    m = n // 2
    atoms, channels = node_feats.shape
    neighbors = neighbor_src.shape[0]
    basis = radial_weight.shape[0]
    rows = msg_weight.shape[0]
    width = channels // n
    margin = atoms // 4
    norm = 1.0 / math.sqrt(neighbors)
    all_atoms = n * atoms
    lanes = neighbors * LANES
    ahead = all_atoms * lanes * 4 <= 8 << 20
    memory = 24 if ahead else 56
    step_scratch = [
        ((2 * basis * SLOT, lanes), bf16),
        ((atoms, lanes), f32),
    ]

    pack_inputs = [
        msg_weight,
        neighbor_src,
        distances,
        graph_ids,
        radial_weight,
        node_feats,
        cotangent,
    ]
    bundle = 2 * rows + 4 * SLOT
    wide = (atoms + chunk_of(bundle, channels // LANES), channels)
    *packed, wide_feats, wide_cot, own_radial = run(
        functools.partial(pack_kernel, n, width),
        [((bundle, LANES), bf16)] * (m - 2) + [(wide, bf16)] * 2 + [((basis, LANES), f32)],
        [
            ((n, rows, LANES), bf16),
            ((n, basis, LANES), f32),
            ((SLOT, LANES), f32),
            ((bundle, LANES), bf16),
        ]
        + [(piece.shape, piece.dtype) for piece in pack_inputs]
        + [((len(pack_inputs),), None)],
        pack_inputs,
        1,
        60,
        outside=len(pack_inputs),
    )
    others = [c for c in range(1, m) if c not in (1, m // 2)]
    feats = exchanged(node_feats, {1: hop(wide_feats, "fsdp", 2)}, m, 0)
    cots = exchanged(cotangent, {m // 2: hop(wide_cot, "fsdp", 2 * (m // 2))}, m, -1)
    own_feats, own_cot, near_lists, near_weights = run(
        functools.partial(merge_kernel, m, rows),
        [((atoms, channels), bf16)] * 2
        + [
            ((m * 4 * SLOT, LANES), bf16),
            (((2 * m + channels // LANES) * rows, LANES), bf16),
        ],
        [((bundle, LANES), bf16)],
        [packed[0]]
        + list(after([hop(value, "fsdp", 2 * c) for c, value in zip(others, packed[1:])], own_radial, 10))
        + [feats[1], cots[m // 2], out_weight, node_feats, cotangent],
        0,
        memory,
    )
    far_weights = hop(near_weights, "fsdp", 1)
    columns, offsets, *made = run(
        functools.partial(lists_kernel, n, margin, neighbors, ahead),
        [
            ((all_atoms, LANES), f32),
            ((n * SLOT, LANES), f32),
        ]
        + [
            ((all_atoms, lanes), f32),
            ((n * neighbors * 2 * margin, 8 * margin), bf16),
            ((2 * all_atoms, neighbors * 2 * margin), bf16),
        ]
        * ahead,
        [
            ((n * SLOT, LANES), f32),
            ((n * SLOT, LANES), f32),
            ((min(n, 8), basis * SLOT, LANES), f32),
            ((2 * basis * SLOT, lanes), bf16),
        ],
        [near_lists, hop(near_lists, "fsdp", 1), own_radial],
        0,
        memory,
    )
    feats[0], cots[0] = own_feats, own_cot
    passed = [(pieces, c) for pieces in (feats, cots) for c in range(1, m) if c & (c - 1)]
    held = after([pieces[c] for pieces, c in passed], offsets, 10)
    for (pieces, c), value in zip(passed, held):
        pieces[c] = value
    own_products, give_products, held_feats = run(
        functools.partial(products_kernel, n),
        [((all_atoms, LANES), bf16)] * 2 + [((all_atoms // 2, channels), bf16)],
        [((2 * LANES, channels), bf16), ((channels, 2 * LANES), bf16)],
        [near_weights, far_weights, out_weight, *feats, *cots],
        1,
        memory,
    )
    got_products = hop(give_products, "fsdp", 1)
    (held_feats,) = after([held_feats], got_products, 0)
    keep, give, dagg = run(
        functools.partial(forward_kernel, n, margin, neighbors, norm, ahead),
        [
            ((all_atoms // 2, LANES), bf16),
            ((all_atoms // 2, LANES), bf16),
            ((all_atoms, LANES), f32),
        ],
        [((all_atoms + 2 * margin, LANES), bf16), ((all_atoms, LANES), bf16)]
        + (step_scratch + [((neighbors * 2 * margin, 8 * margin), bf16)]) * (not ahead),
        [own_products, got_products, columns, own_radial, *made[:2]],
        1,
        memory,
    )
    other_act = hop(give, "fsdp", 1)
    (turned,) = run(
        functools.partial(backward_kernel, n, margin, neighbors, ahead),
        [((LANES, all_atoms), bf16)],
        [
            ((2 * min(n, 8) if ahead else 2, neighbors * 2 * margin, LANES), bf16),
            ((2, all_atoms + 2 * margin, LANES), f32),
        ]
        + (step_scratch + [((2 * atoms, neighbors * 2 * margin), bf16)]) * (not ahead),
        [dagg, own_radial, columns, offsets, *made[::2]],
        1,
        memory,
    )
    keep_grads, give_grads = run(
        functools.partial(gradient_kernel, n, rows),
        [((m * rows, LANES), bf16), ((m * rows, LANES), f32)],
        [((channels, LANES), f32)],
        [turned, held_feats, hop(held_feats, "fsdp", 1)],
        1,
        memory,
    )
    *sums, own_part, give_part = run(
        functools.partial(chip_kernel, n, margin, neighbors, width),
        [((atoms, channels), bf16)] * m + [((rows, channels), f32), ((rows, channels), bf16)],
        [],
        [columns, keep, other_act, out_weight, far_weights, give_grads, *cots],
        1,
        memory,
    )
    grad_sends = run(
        join_kernel,
        [((rows, 2 * LANES), bf16)] * m,
        [],
        [keep_grads, hop(give_grads, "fsdp", 1)],
        0,
        memory,
    )
    near = across_chips(grad_sends)
    grad_msg, grad_out, code = run(
        functools.partial(grads_kernel, n),
        [((1, rows, channels), bf16)] * 2 + [((2 * (rows + SLOT), FRAG), bf16)],
        [((n, rows, LANES), bf16), ((rows, channels), f32)],
        [fragment, *near, hop(give_part, "fsdp", 1), own_part],
        4,
        memory,
        scalars=1,
    )
    sums = across_chips(sums)
    step = 1
    codes = [code]
    if replicas > 1:
        codes.append(hop(code, "replica", step))
    (outer_sum,) = run(
        pair_kernel, [((2, rows, FRAG), f32 if replicas <= 2 else bf16)], [], codes, 0, memory
    )
    while 4 * step < replicas:
        step = 2 * step
        (outer_sum,) = run(
            outer_kernel,
            [((2, rows, FRAG), bf16)],
            [],
            [outer_sum, hop(outer_sum, "replica", step)],
            0,
            memory,
        )
    pair = [outer_sum]
    if replicas > 2:
        pair.append(hop(outer_sum, "replica", 2 * step))
    outer_sum, node_out = run(
        functools.partial(last_kernel, len(pair)),
        [((2, rows, FRAG), f32), ((atoms, channels), bf16)],
        [],
        [*pair, node_feats, *sums],
        0,
        memory,
    )
    return node_out, grad_msg, grad_out, outer_sum


def solution(mesh):
    placed = (
        P(("replica", "fsdp"), None),
        P(None, ("replica", "fsdp")),
        P(None, ("replica", "fsdp")),
        P("replica", "fsdp"),
        P("fsdp", None),
        P("fsdp", None),
        P(),
        P(("replica", "fsdp"), None),
        P(),
    )
    return jax.shard_map(
        shards,
        mesh=mesh,
        in_specs=placed,
        out_specs=(
            P(("replica", "fsdp"), None),
            P("replica", "fsdp", None),
            P("replica", "fsdp", None),
            P(None, "fsdp", None),
        ),
        check_vma=False,
    )
```

```python
import functools
import math

import jax
import jax.numpy as jnp
from jax import lax
from jax.experimental import pallas as pl
from jax.experimental.pallas import tpu as pltpu
from jax.sharding import PartitionSpec as P

FRAG = 128
GRAPHS = 8
LANES = 128
SLOT = 16

cutoff = 5.0
sharpness = 2.0
tiny = 1e-06

bf16 = jnp.bfloat16
f32 = jnp.float32


def rows_at(index, count):
    return pl.ds(pl.multiple_of(index * count, count), count)


def column_of(k, neighbors):
    free = SLOT - neighbors
    return (k // free) * SLOT + neighbors + k % free


def chunk_of(rows, pieces):
    return -(-rows // (pieces * SLOT)) * SLOT


def pack_kernel(n, width, *refs):
    far, refs = refs[:7], refs[7:]
    m = n // 2
    packed, (feats_out, cot_out, own_radial) = refs[: m - 2], refs[m - 2 : m + 1]
    (blocks, radials, group, bundle), refs = refs[m + 1 : m + 5], refs[m + 5 :]
    held, done = refs[:7], refs[7]
    copies = [pltpu.make_async_copy(a, b, done.at[i]) for i, (a, b) in enumerate(zip(far, held))]
    for copy in copies:
        copy.start()
    for copy in copies:
        copy.wait()
    weight, src, dist, ids, radial_weight, feats, cot = held
    me = lax.axis_index("fsdp")
    rows = weight.shape[0]
    neighbors, atoms = src.shape
    if width < LANES:
        blocks[...] = jnp.zeros_like(blocks)
        radials[...] = jnp.zeros_like(radials)
    for e in range(n):
        blocks[e, :, :width] = weight[:, e * width : (e + 1) * width]
        radials[e, :, :width] = radial_weight[:, e * width : (e + 1) * width]
    own_radial[...] = radials[me]
    position = lax.broadcasted_iota(jnp.int32, src.shape, 1) + me * atoms
    group[...] = jnp.zeros_like(group)
    group[:neighbors] = (src[...] - position).astype(f32)
    group[neighbors : neighbors + 1] = ids[...].astype(f32)
    meta = [group[...].astype(bf16)]
    group[...] = jnp.ones_like(group)
    group[:neighbors] = dist[...]
    left = group[...]
    for _ in range(3):
        part = left.astype(bf16)
        meta.append(part)
        left = left - part.astype(f32)
    feats_out[:atoms] = feats[...]
    cot_out[:atoms] = cot[...]
    direct = 0
    for c in range(m):
        wide = {1: feats_out, m // 2: cot_out}.get(c)
        if wide is None:
            target = packed[direct]
            direct += 1
        else:
            target = bundle
        target[:rows] = blocks[me ^ (2 * c)]
        target[rows : 2 * rows] = blocks[me ^ (2 * c + 1)]
        for i, part in enumerate(meta):
            target[2 * rows + i * SLOT : 2 * rows + (i + 1) * SLOT] = part
        if wide is not None:
            size = wide.shape[0] - atoms
            for q in range(wide.shape[1] // LANES):
                stop = min((q + 1) * size, bundle.shape[0])
                if stop > q * size:
                    wide[atoms : atoms + stop - q * size, q * LANES : (q + 1) * LANES] = bundle[
                        q * size : stop
                    ]


def merge_kernel(m, rows, *refs):
    direct, (feats, cot, own_weight), refs = list(refs[: m - 2]), refs[m - 2 : m + 1], refs[m + 1 :]
    for value, held in zip(refs[:2], refs[2:4]):
        held[...] = value[...]
    lists, weights, bundle = refs[4:]
    size = 4 * SLOT
    for c in range(m):
        wide = {1: feats, m // 2: cot}.get(c)
        if wide is None:
            source = direct.pop(0)
        else:
            source = bundle
            height = chunk_of(bundle.shape[0], wide.shape[1] // LANES)
            for q in range(wide.shape[1] // LANES):
                stop = min((q + 1) * height, bundle.shape[0])
                if stop > q * height:
                    bundle[q * height : stop] = wide[
                        wide.shape[0] - height : wide.shape[0] - height + stop - q * height,
                        q * LANES : (q + 1) * LANES,
                    ]
        weights[2 * c * rows : 2 * (c + 1) * rows] = source[: 2 * rows]
        lists[c * size : (c + 1) * size] = source[2 * rows :]
    for q in range(own_weight.shape[1] // LANES):
        start = (2 * m + q) * rows
        weights[start : start + rows] = own_weight[:, q * LANES : (q + 1) * LANES]


def gate_kernel(*_):
    pass


def fill_filters(neighbors, own_radial, filters):
    basis = own_radial.shape[0]
    half = basis * SLOT
    row = lax.broadcasted_iota(jnp.int32, (half, LANES), 0) % SLOT
    spread = jnp.concatenate(
        [jnp.broadcast_to(own_radial[b : b + 1], (SLOT, LANES)) for b in range(basis)], axis=0
    )
    high = spread.astype(bf16).astype(f32)
    low = spread - high
    for k in range(neighbors):
        lanes = slice(k * LANES, (k + 1) * LANES)
        filters[:half, lanes] = jnp.where(row == k, high, 0.0).astype(bf16)
        filters[half:, lanes] = jnp.where(row == k, low, 0.0).astype(bf16)


def fill_values(columns, filters, values):
    high = columns.astype(bf16)
    both = jnp.concatenate([high, high], axis=1)
    span = 2 * LANES

    def step(j, _):
        lanes = pl.ds(pl.multiple_of(j * span, span), span)
        values[:, lanes] = jnp.dot(both, filters[:, lanes], preferred_element_type=f32)
        return 0

    steps = values.shape[1] // span
    lax.fori_loop(0, steps, step, 0, unroll=steps)


def fill_pick(margin, neighbors, turned, pick):
    tile = 2 * margin
    tiles = turned.shape[0] // tile
    shift = (
        lax.broadcasted_iota(jnp.int32, (tile, 2 * tile), 1)
        - lax.broadcasted_iota(jnp.int32, (tile, 2 * tile), 0)
        - margin
    ).astype(f32)
    for t in range(tiles):
        own = turned[t * tile : (t + 1) * tile]
        for k in range(neighbors):
            at = column_of(k, neighbors)
            pick[k * tile : (k + 1) * tile, t * 2 * tile : (t + 1) * 2 * tile] = jnp.where(
                own[:, at : at + 1] == shift, 1.0, 0.0
            ).astype(bf16)


def fill_place(margin, neighbors, offset, place):
    tile = 2 * margin
    shape = (2 * tile, 2 * tile)
    shift = (
        lax.broadcasted_iota(jnp.int32, shape, 0)
        - lax.broadcasted_iota(jnp.int32, shape, 1) % tile
        - margin
    ).astype(f32)
    for t in range(offset.shape[1] // tile):
        for k in range(0, neighbors, 2):
            row = jnp.concatenate(
                [offset[k + i : k + i + 1, t * tile : (t + 1) * tile] for i in range(2)], axis=1
            )
            place[t * 2 * tile : (t + 1) * 2 * tile, k * tile : (k + 2) * tile] = jnp.where(
                row == shift, 1.0, 0.0
            ).astype(bf16)


def lists_kernel(n, margin, neighbors, ahead, *refs):
    m = n // 2
    near, far, own_radial = refs[:3]
    columns, offsets = refs[3:5]
    made = refs[5:8] if ahead else ()
    dists, graph_weight, stacked, filters = refs[5 + len(made) :]
    me = lax.axis_index("fsdp")
    basis = own_radial.shape[0]
    atoms = columns.shape[0] // n
    for d in range(n):
        e = me ^ d
        meta = (far if d % 2 else near)[d // 2 * 4 * SLOT : (d // 2 + 1) * 4 * SLOT].astype(f32)
        offsets[rows_at(e, SLOT)] = meta[:SLOT]
        dists[rows_at(e, SLOT)] = (
            meta[SLOT : 2 * SLOT] + meta[2 * SLOT : 3 * SLOT] + meta[3 * SLOT :]
        )
    slots = lax.broadcasted_iota(jnp.int32, offsets.shape, 0) % SLOT
    ids = jnp.where(slots == neighbors, offsets[...], -1.0)
    weight = jnp.zeros_like(ids)
    for g in range(GRAPHS):
        member = ids == float(g)
        count = jnp.sum(jnp.where(member, 1.0, 0.0), axis=(0, 1), keepdims=True)
        weight = weight + jnp.where(member, lax.rsqrt(jnp.maximum(count, 1.0)), 0.0)
    graph_weight[...] = weight

    def columns_step(e, _):
        dist = dists[rows_at(e, SLOT)]
        envelope = 0.5 * (jnp.cos(jnp.pi * dist / cutoff) + 1.0)
        own = stacked.at[e % stacked.shape[0]]
        for b in range(basis):
            center = cutoff * b / (basis - 1)
            own[b * SLOT : (b + 1) * SLOT] = jnp.exp(-sharpness * (dist - center) ** 2) * envelope
        offset = offsets[rows_at(e, SLOT)]
        for k in range(neighbors):
            at = column_of(k, neighbors)
            own[at : at + 1] = offset[k : k + 1]
        at = column_of(neighbors, neighbors)
        own[at : at + 1] = graph_weight[rows_at(e, SLOT)][neighbors : neighbors + 1]
        columns[rows_at(e, atoms)] = own[...].T
        return 0

    lax.fori_loop(0, n, columns_step, 0, unroll=stacked.shape[0])
    if ahead:
        values, pick, place = made
        fill_filters(neighbors, own_radial, filters)
        fill_values(columns[...], filters, values)

        def block_step(e, _):
            span = neighbors * 2 * margin
            fill_pick(margin, neighbors, columns[rows_at(e, atoms)], pick.at[rows_at(e, span)])
            fill_place(
                margin,
                neighbors,
                offsets[rows_at(e, SLOT)],
                place.at[rows_at(e, 2 * atoms)],
            )
            return 0

        lax.fori_loop(0, n, block_step, 0, unroll=8)


def products_kernel(n, near, far, own_weight, *refs):
    m = n // 2
    feats, cots, refs = refs[:m], refs[m : 2 * m], refs[2 * m :]
    keep, give, held_feats, both, weights = refs
    me = lax.axis_index("fsdp")
    atoms = feats[0].shape[0]
    half = m * atoms
    rows = own_weight.shape[0]
    if rows < LANES:
        both[...] = jnp.zeros_like(both)
    both[:rows] = own_weight[...]
    for q in range(both.shape[1] // LANES):
        start = (2 * m + q) * rows
        both[LANES : LANES + rows, q * LANES : (q + 1) * LANES] = far[start : start + rows]
    for c in range(m):
        for k, source in enumerate((near, far)):
            block = rows_at(me ^ (2 * c + k), rows)
            for i in range(2):
                start = (2 * c + i) * rows
                side = slice(LANES, None) if i != k else slice(0, LANES)
                weights[block, side] = source[start : start + rows]
    for c in range(m):
        held_feats[c * atoms : (c + 1) * atoms] = feats[c][:atoms]
    projected = jnp.dot(held_feats[...], weights[...], preferred_element_type=f32).astype(bf16)
    flow = jnp.concatenate([cots[c][:atoms] for c in range(m)], axis=0)
    dact = lax.dot_general(
        flow, both[...], (((1,), (1,)), ((), ())), preferred_element_type=f32
    ).astype(bf16)
    for c in range(m):
        chip = (me // 2) ^ c
        here = slice(c * atoms, (c + 1) * atoms)
        keep[rows_at(chip, atoms)] = projected[here, :LANES]
        give[rows_at(chip, atoms)] = projected[here, LANES:]
        keep[rows_at(chip + m, atoms)] = dact[here, :LANES]
        give[rows_at(chip + m, atoms)] = dact[here, LANES:]


def forward_kernel(n, margin, neighbors, norm, ahead, *refs):
    own, got, columns, own_radial = refs[:4]
    made = refs[4:6] if ahead else ()
    keep, give, dagg, projected, act = refs[4 + len(made) : 9 + len(made)]
    scratch = refs[9 + len(made) :]
    me = lax.axis_index("fsdp")
    core = me % 2
    atoms = columns.shape[0] // n
    half = n // 2 * atoms
    projected[:margin] = jnp.zeros_like(projected[:margin])
    projected[n * atoms + margin :] = jnp.zeros_like(projected[:margin])
    for c in range(n // 2):
        for source, parity in ((own, core), (got, 1 - core)):
            start = pl.multiple_of((2 * c + parity) * atoms + margin, margin)
            projected[pl.ds(start, atoms)] = source[c * atoms : (c + 1) * atoms]
            dact = source[half + c * atoms : half + (c + 1) * atoms]
            dagg[rows_at(2 * c + parity, atoms)] = dact.astype(f32)
    if ahead:
        values, pick = made
    else:
        filters, values, pick = scratch
        fill_filters(neighbors, own_radial, filters)
    tile = 2 * margin
    span = neighbors * tile

    def block_step(e, _):
        turned = columns[rows_at(e, atoms)]
        if ahead:
            own_values = values.at[rows_at(e, atoms)]
            own_pick = pick[rows_at(e, span)]
        else:
            own_values = values
            fill_values(turned, filters, values)
            fill_pick(margin, neighbors, turned, pick)
            own_pick = pick[...]
        start = pl.multiple_of(e * atoms, atoms)
        halves = []
        for t in range(2):
            found = jnp.dot(
                own_pick[:, t * 2 * tile : (t + 1) * 2 * tile],
                projected[pl.ds(start + t * tile, 2 * tile)],
                preferred_element_type=f32,
            )
            total = jnp.zeros((tile, LANES), f32)
            for k in range(neighbors):
                total = total + (
                    own_values[t * tile : (t + 1) * tile, k * LANES : (k + 1) * LANES]
                    * found[k * tile : (k + 1) * tile]
                )
            halves.append(total)
        agg = jnp.concatenate(halves, axis=0) * norm
        sig = 1.0 / (1.0 + jnp.exp(-agg))
        active = (agg * sig).astype(bf16)
        at = column_of(neighbors, neighbors)
        graph = turned[:, at : at + 1]
        slope = sig * (1.0 + agg * (1.0 - sig)) * (graph * norm)
        dagg[rows_at(e, atoms)] = dagg[rows_at(e, atoms)] * slope
        act[rows_at(e, atoms)] = active
        return 0

    lax.fori_loop(0, n, block_step, 0, unroll=min(n, 8) if ahead else 1)
    for c in range(n // 2):
        keep[c * atoms : (c + 1) * atoms] = act[rows_at(2 * c + core, atoms)]
        give[c * atoms : (c + 1) * atoms] = act[rows_at(2 * c + 1 - core, atoms)]


def backward_kernel(n, margin, neighbors, ahead, *refs):
    m = n // 2
    dagg, own_radial, columns, offsets = refs[:4]
    made = refs[4:6] if ahead else ()
    refs = refs[4 + len(made) :]
    turned, spread = refs[:2]
    scratch = refs[2:]
    me = lax.axis_index("fsdp")
    atoms = columns.shape[0] // n
    tile = 2 * margin
    spread[0, n * atoms :] = jnp.zeros_like(spread[0, n * atoms :])
    spread[1, :tile] = jnp.zeros_like(spread[1, :tile])
    if ahead:
        values, place = made
    else:
        filters, values, place = scratch
        fill_filters(neighbors, own_radial, filters)

    def block_step(e, _):
        flow = dagg[rows_at(e, atoms)]
        if ahead:
            own_values = values.at[rows_at(e, atoms)]
            own_place = place.at[rows_at(e, 2 * atoms)]
        else:
            own_values = values
            fill_values(columns[rows_at(e, atoms)], filters, values)
            fill_place(margin, neighbors, offsets[rows_at(e, SLOT)], place)
            own_place = place
        for t in range(2):
            here = slice(t * tile, (t + 1) * tile)
            own = jnp.concatenate(
                [
                    (own_values[here, k * LANES : (k + 1) * LANES] * flow[here]).astype(bf16)
                    for k in range(neighbors)
                ],
                axis=0,
            )
            window = pl.ds(pl.multiple_of(e * atoms + t * tile, tile), 2 * tile)
            spread[t, window] = jnp.dot(
                own_place[t * 2 * tile : (t + 1) * 2 * tile], own, preferred_element_type=f32
            )
        return 0

    lax.fori_loop(0, n, block_step, 0, unroll=min(n, 8) if ahead else 1)

    half = m * atoms
    for k in range(2):
        for c in range(m):
            e = me ^ (2 * c + k)
            start = pl.multiple_of(e * atoms + margin, margin)
            turned[:, k * half + c * atoms : k * half + (c + 1) * atoms] = (
                (spread[0, pl.ds(start, atoms)] + spread[1, pl.ds(start, atoms)]).T.astype(bf16)
            )


def gradient_kernel(n, rows, turned, own_feats, other_feats, *refs):
    m = n // 2
    keep, give, grads = refs
    me = lax.axis_index("fsdp")
    half = own_feats.shape[0]
    total = jnp.dot(turned[:, :half], own_feats[...], preferred_element_type=f32)
    total = total + jnp.dot(turned[:, half:], other_feats[...], preferred_element_type=f32)
    for q in range(total.shape[1] // LANES):
        grads[q * LANES : (q + 1) * LANES] = total[:, q * LANES : (q + 1) * LANES].T
    for c in range(m):
        keep[c * rows : (c + 1) * rows] = grads[rows_at(me ^ (2 * c), rows)].astype(bf16)
        give[c * rows : (c + 1) * rows] = grads[rows_at(me ^ (2 * c + 1), rows)]


def join_kernel(keep, got, *sends):
    rows = sends[0].shape[0]
    for c, send in enumerate(sends):
        send[:, :LANES] = keep[c * rows : (c + 1) * rows]
        send[:, LANES:] = got[c * rows : (c + 1) * rows].astype(bf16)


def write_code(piece, code):
    rows = piece.shape[0]
    scale = (jnp.max(jnp.abs(piece), axis=-1, keepdims=True) + tiny).astype(bf16)
    wide = jnp.broadcast_to(scale.astype(f32), piece.shape)
    code[:rows] = (piece / wide).astype(bf16)
    if rows < LANES:
        wide = jnp.concatenate([wide, jnp.zeros((LANES - rows, LANES), f32)], axis=0)
    code[rows:] = wide.T[:SLOT].astype(bf16)


def chip_kernel(n, margin, neighbors, width, *refs):
    m = n // 2
    columns, keep, got, own_weight, other_weight, _after = refs[:6]
    cots, sends, (own, give) = refs[6 : 6 + m], refs[6 + m : 6 + 2 * m], refs[6 + 2 * m :]
    me = lax.axis_index("fsdp")
    atoms = cots[0].shape[0]
    rows = own.shape[0]
    at = column_of(neighbors, neighbors)
    pieces = own_weight.shape[1] // LANES
    first = other_weight.shape[0] - pieces * rows
    other_weight = jnp.concatenate(
        [other_weight[first + q * rows : first + (q + 1) * rows] for q in range(pieces)], axis=1
    )
    acts = [
        jnp.concatenate([act[rows_at((me // 2) ^ c, atoms)] for c in range(m)], axis=0)
        for act in (keep, got)
    ]
    total = jnp.dot(acts[0][:, :width], own_weight[...], preferred_element_type=f32) + jnp.dot(
        acts[1][:, :width], other_weight, preferred_element_type=f32
    )
    for c in range(m):
        sends[c][...] = total[c * atoms : (c + 1) * atoms].astype(bf16)
    graph = jnp.concatenate(
        [columns[rows_at(me ^ (2 * c), atoms)][:, at : at + 1] for c in range(m)], axis=0
    )
    left = jnp.concatenate([(act.astype(f32) * graph).T.astype(bf16) for act in acts], axis=0)
    flow = jnp.concatenate([cots[c][:atoms] for c in range(m)], axis=0)
    parts = jnp.dot(left, flow, preferred_element_type=f32)
    own[...] = parts[:rows]
    give[...] = parts[LANES : LANES + rows].astype(bf16)


def grads_kernel(n, fragment, *refs):
    m = n // 2
    near, got_part, own_part = refs[:m], refs[m], refs[m + 1]
    msg_grad, out_grad, code, blocks, total = refs[m + 2 :]
    me = lax.axis_index("fsdp")
    rows = msg_grad.shape[1]
    width = msg_grad.shape[2] // n
    lanes = pl.ds(pl.multiple_of(fragment[0] * FRAG, FRAG), FRAG)
    for c in range(m):
        blocks[me ^ (2 * c)] = near[c][:, :LANES]
        blocks[me ^ (2 * c + 1)] = near[c][:, LANES:]
    for e in range(n):
        msg_grad[0, :, e * width : (e + 1) * width] = blocks[e][:, :width]
    write_code(msg_grad[0, :, lanes].astype(f32), code.at[: rows + SLOT])
    total[...] = own_part[...] + got_part[...].astype(f32)
    out_grad[0] = total[...].astype(bf16)
    write_code(total[:, lanes], code.at[rows + SLOT :])


def pair_kernel(*refs):
    codes, out = refs[:-1], refs[-1]
    rows = out.shape[1]
    for piece in range(2):
        total = jnp.zeros((rows, FRAG), f32)
        for code in codes:
            own = code.at[piece * (rows + SLOT) : (piece + 1) * (rows + SLOT)]
            wide = jnp.broadcast_to(own[rows:].astype(f32)[:1], (LANES, LANES)).T
            total = total + wide[:rows] * own[:rows].astype(f32)
        out[piece] = total.astype(out.dtype)


def outer_kernel(own, other, out):
    out[...] = (own[...].astype(f32) + other[...].astype(f32)).astype(out.dtype)


def last_kernel(count, *refs):
    pair, (feats, *parts), (outer, node) = refs[:count], refs[count:-2], refs[-2:]
    outer[...] = functools.reduce(jnp.add, [value[...].astype(f32) for value in pair])
    total = feats[...].astype(f32)
    for part in parts:
        total = total + part[...].astype(f32)
    node[...] = total.astype(bf16)


def run(kernel, outs, scratch, args, micros, memory=16, scalars=0, outside=0):
    whole = pl.BlockSpec(memory_space=pltpu.VMEM)
    scalar = pl.BlockSpec(memory_space=pltpu.SMEM)
    remote = pl.BlockSpec(memory_space=pltpu.HBM)
    return pl.pallas_call(
        kernel,
        out_shape=[jax.ShapeDtypeStruct(shape, dtype) for shape, dtype in outs],
        in_specs=[scalar] * scalars
        + [whole] * (len(args) - scalars - outside)
        + [remote] * outside,
        out_specs=[whole] * len(outs),
        scratch_shapes=[
            pltpu.SemaphoreType.DMA(shape) if dtype is None else pltpu.VMEM(shape, dtype)
            for shape, dtype in scratch
        ],
        compiler_params=pltpu.CompilerParams(vmem_limit_bytes=memory << 20),
        cost_estimate=pl.CostEstimate(
            flops=int(micros * 1e9), bytes_accessed=int(micros * 3e6), transcendentals=0
        ),
    )(*args)


def after(values, other, micros):
    anywhere = pl.BlockSpec(memory_space=pl.ANY)
    return pl.pallas_call(
        gate_kernel,
        out_shape=[jax.ShapeDtypeStruct(value.shape, value.dtype) for value in values],
        in_specs=[anywhere] * (len(values) + 1),
        out_specs=[anywhere] * len(values),
        input_output_aliases={i: i for i in range(len(values))},
        compiler_params=pltpu.CompilerParams(vmem_limit_bytes=1 << 20),
        cost_estimate=pl.CostEstimate(
            flops=int(micros * 1e9), bytes_accessed=int(micros * 3e6), transcendentals=0
        ),
    )(*values, other)


def hop(value, axis, step):
    count = lax.axis_size(axis)
    return lax.ppermute(value, axis, [(i, i ^ step) for i in range(count)])


def across_chips(sends):
    return [sends[0]] + [hop(sends[c], "fsdp", 2 * c) for c in range(1, len(sends))]


def exchanged(value, held, m, side):
    pieces = {0: value, **held}
    for c in range(1, m):
        if c not in pieces:
            used = [1 << i for i in range(m.bit_length()) if c >> i & 1][side]
            pieces[c] = hop(pieces[c ^ used], "fsdp", 2 * used)
    return [pieces[c] for c in range(m)]


def shards(
    node_feats,
    neighbor_src,
    distances,
    graph_ids,
    msg_weight,
    out_weight,
    radial_weight,
    cotangent,
    fragment,
):
    n = lax.axis_size("fsdp")
    replicas = lax.axis_size("replica")
    m = n // 2
    atoms, channels = node_feats.shape
    neighbors = neighbor_src.shape[0]
    basis = radial_weight.shape[0]
    rows = msg_weight.shape[0]
    width = channels // n
    margin = atoms // 4
    norm = 1.0 / math.sqrt(neighbors)
    all_atoms = n * atoms
    lanes = neighbors * LANES
    ahead = all_atoms * lanes * 4 <= 8 << 20
    memory = 24 if ahead else 56
    step_scratch = [
        ((2 * basis * SLOT, lanes), bf16),
        ((atoms, lanes), f32),
    ]

    pack_inputs = [
        msg_weight,
        neighbor_src,
        distances,
        graph_ids,
        radial_weight,
        node_feats,
        cotangent,
    ]
    bundle = 2 * rows + 4 * SLOT
    wide = (atoms + chunk_of(bundle, channels // LANES), channels)
    *packed, wide_feats, wide_cot, own_radial = run(
        functools.partial(pack_kernel, n, width),
        [((bundle, LANES), bf16)] * (m - 2) + [(wide, bf16)] * 2 + [((basis, LANES), f32)],
        [
            ((n, rows, LANES), bf16),
            ((n, basis, LANES), f32),
            ((SLOT, LANES), f32),
            ((bundle, LANES), bf16),
        ]
        + [(piece.shape, piece.dtype) for piece in pack_inputs]
        + [((len(pack_inputs),), None)],
        pack_inputs,
        1,
        60,
        outside=len(pack_inputs),
    )
    others = [c for c in range(1, m) if c not in (1, m // 2)]
    feats = exchanged(node_feats, {1: hop(wide_feats, "fsdp", 2)}, m, 0)
    cots = exchanged(cotangent, {m // 2: hop(wide_cot, "fsdp", 2 * (m // 2))}, m, -1)
    own_feats, own_cot, near_lists, near_weights = run(
        functools.partial(merge_kernel, m, rows),
        [((atoms, channels), bf16)] * 2
        + [
            ((m * 4 * SLOT, LANES), bf16),
            (((2 * m + channels // LANES) * rows, LANES), bf16),
        ],
        [((bundle, LANES), bf16)],
        [packed[0]]
        + list(after([hop(value, "fsdp", 2 * c) for c, value in zip(others, packed[1:])], own_radial, 10))
        + [feats[1], cots[m // 2], out_weight, node_feats, cotangent],
        0,
        memory,
    )
    far_weights = hop(near_weights, "fsdp", 1)
    columns, offsets, *made = run(
        functools.partial(lists_kernel, n, margin, neighbors, ahead),
        [
            ((all_atoms, LANES), f32),
            ((n * SLOT, LANES), f32),
        ]
        + [
            ((all_atoms, lanes), f32),
            ((n * neighbors * 2 * margin, 8 * margin), bf16),
            ((2 * all_atoms, neighbors * 2 * margin), bf16),
        ]
        * ahead,
        [
            ((n * SLOT, LANES), f32),
            ((n * SLOT, LANES), f32),
            ((min(n, 8), basis * SLOT, LANES), f32),
            ((2 * basis * SLOT, lanes), bf16),
        ],
        [near_lists, hop(near_lists, "fsdp", 1), own_radial],
        0,
        memory,
    )
    feats[0], cots[0] = own_feats, own_cot
    passed = [(pieces, c) for pieces in (feats, cots) for c in range(1, m) if c & (c - 1)]
    held = after([pieces[c] for pieces, c in passed], offsets, 10)
    for (pieces, c), value in zip(passed, held):
        pieces[c] = value
    own_products, give_products, held_feats = run(
        functools.partial(products_kernel, n),
        [((all_atoms, LANES), bf16)] * 2 + [((all_atoms // 2, channels), bf16)],
        [((2 * LANES, channels), bf16), ((channels, 2 * LANES), bf16)],
        [near_weights, far_weights, out_weight, *feats, *cots],
        1,
        memory,
    )
    got_products = hop(give_products, "fsdp", 1)
    (held_feats,) = after([held_feats], got_products, 0)
    keep, give, dagg = run(
        functools.partial(forward_kernel, n, margin, neighbors, norm, ahead),
        [
            ((all_atoms // 2, LANES), bf16),
            ((all_atoms // 2, LANES), bf16),
            ((all_atoms, LANES), f32),
        ],
        [((all_atoms + 2 * margin, LANES), bf16), ((all_atoms, LANES), bf16)]
        + (step_scratch + [((neighbors * 2 * margin, 8 * margin), bf16)]) * (not ahead),
        [own_products, got_products, columns, own_radial, *made[:2]],
        1,
        memory,
    )
    other_act = hop(give, "fsdp", 1)
    (turned,) = run(
        functools.partial(backward_kernel, n, margin, neighbors, ahead),
        [((LANES, all_atoms), bf16)],
        [
            ((2, all_atoms + 2 * margin, LANES), f32),
        ]
        + (step_scratch + [((2 * atoms, neighbors * 2 * margin), bf16)]) * (not ahead),
        [dagg, own_radial, columns, offsets, *made[::2]],
        1,
        memory,
    )
    keep_grads, give_grads = run(
        functools.partial(gradient_kernel, n, rows),
        [((m * rows, LANES), bf16), ((m * rows, LANES), f32)],
        [((channels, LANES), f32)],
        [turned, held_feats, hop(held_feats, "fsdp", 1)],
        1,
        memory,
    )
    *sums, own_part, give_part = run(
        functools.partial(chip_kernel, n, margin, neighbors, width),
        [((atoms, channels), bf16)] * m + [((rows, channels), f32), ((rows, channels), bf16)],
        [],
        [columns, keep, other_act, out_weight, far_weights, give_grads, *cots],
        1,
        memory,
    )
    grad_sends = run(
        join_kernel,
        [((rows, 2 * LANES), bf16)] * m,
        [],
        [keep_grads, hop(give_grads, "fsdp", 1)],
        0,
        memory,
    )
    near = across_chips(grad_sends)
    grad_msg, grad_out, code = run(
        functools.partial(grads_kernel, n),
        [((1, rows, channels), bf16)] * 2 + [((2 * (rows + SLOT), FRAG), bf16)],
        [((n, rows, LANES), bf16), ((rows, channels), f32)],
        [fragment, *near, hop(give_part, "fsdp", 1), own_part],
        4,
        memory,
        scalars=1,
    )
    sums = across_chips(sums)
    step = 1
    codes = [code]
    if replicas > 1:
        codes.append(hop(code, "replica", step))
    (outer_sum,) = run(
        pair_kernel, [((2, rows, FRAG), f32 if replicas <= 2 else bf16)], [], codes, 0, memory
    )
    while 4 * step < replicas:
        step = 2 * step
        (outer_sum,) = run(
            outer_kernel,
            [((2, rows, FRAG), bf16)],
            [],
            [outer_sum, hop(outer_sum, "replica", step)],
            0,
            memory,
        )
    pair = [outer_sum]
    if replicas > 2:
        pair.append(hop(outer_sum, "replica", 2 * step))
    outer_sum, node_out = run(
        functools.partial(last_kernel, len(pair)),
        [((2, rows, FRAG), f32), ((atoms, channels), bf16)],
        [],
        [*pair, node_feats, *sums],
        0,
        memory,
    )
    return node_out, grad_msg, grad_out, outer_sum


def solution(mesh):
    placed = (
        P(("replica", "fsdp"), None),
        P(None, ("replica", "fsdp")),
        P(None, ("replica", "fsdp")),
        P("replica", "fsdp"),
        P("fsdp", None),
        P("fsdp", None),
        P(),
        P(("replica", "fsdp"), None),
        P(),
    )
    return jax.shard_map(
        shards,
        mesh=mesh,
        in_specs=placed,
        out_specs=(
            P(("replica", "fsdp"), None),
            P("replica", "fsdp", None),
            P("replica", "fsdp", None),
            P(None, "fsdp", None),
        ),
        check_vma=False,
    )
```

```python
import functools
import math

import jax
import jax.numpy as jnp
from jax import lax
from jax.experimental import pallas as pl
from jax.experimental.pallas import tpu as pltpu
from jax.sharding import PartitionSpec as P

FRAG = 128
GRAPHS = 8
LANES = 128
SLOT = 16

cutoff = 5.0
sharpness = 2.0
tiny = 1e-06

bf16 = jnp.bfloat16
f32 = jnp.float32


def rows_at(index, count):
    return pl.ds(pl.multiple_of(index * count, count), count)


def column_of(k, neighbors):
    free = SLOT - neighbors
    return (k // free) * SLOT + neighbors + k % free


def chunk_of(rows, pieces):
    return -(-rows // (pieces * SLOT)) * SLOT


def pack_kernel(n, width, *refs):
    far, refs = refs[:7], refs[7:]
    m = n // 2
    packed, (feats_out, cot_out, own_radial) = refs[: m - 2], refs[m - 2 : m + 1]
    (blocks, radials, group, bundle), refs = refs[m + 1 : m + 5], refs[m + 5 :]
    held, done = refs[:7], refs[7]
    copies = [pltpu.make_async_copy(a, b, done.at[i]) for i, (a, b) in enumerate(zip(far, held))]
    for copy in copies:
        copy.start()
    for copy in copies:
        copy.wait()
    weight, src, dist, ids, radial_weight, feats, cot = held
    me = lax.axis_index("fsdp")
    rows = weight.shape[0]
    neighbors, atoms = src.shape
    if width < LANES:
        blocks[...] = jnp.zeros_like(blocks)
        radials[...] = jnp.zeros_like(radials)
    for e in range(n):
        blocks[e, :, :width] = weight[:, e * width : (e + 1) * width]
        radials[e, :, :width] = radial_weight[:, e * width : (e + 1) * width]
    own_radial[...] = radials[me]
    position = lax.broadcasted_iota(jnp.int32, src.shape, 1) + me * atoms
    group[...] = jnp.zeros_like(group)
    group[:neighbors] = (src[...] - position).astype(f32)
    group[neighbors : neighbors + 1] = ids[...].astype(f32)
    meta = [group[...].astype(bf16)]
    group[...] = jnp.ones_like(group)
    group[:neighbors] = dist[...]
    left = group[...]
    for _ in range(3):
        part = left.astype(bf16)
        meta.append(part)
        left = left - part.astype(f32)
    feats_out[:atoms] = feats[...]
    cot_out[:atoms] = cot[...]
    direct = 0
    for c in range(m):
        wide = {1: feats_out, m // 2: cot_out}.get(c)
        if wide is None:
            target = packed[direct]
            direct += 1
        else:
            target = bundle
        target[:rows] = blocks[me ^ (2 * c)]
        target[rows : 2 * rows] = blocks[me ^ (2 * c + 1)]
        for i, part in enumerate(meta):
            target[2 * rows + i * SLOT : 2 * rows + (i + 1) * SLOT] = part
        if wide is not None:
            size = wide.shape[0] - atoms
            for q in range(wide.shape[1] // LANES):
                stop = min((q + 1) * size, bundle.shape[0])
                if stop > q * size:
                    wide[atoms : atoms + stop - q * size, q * LANES : (q + 1) * LANES] = bundle[
                        q * size : stop
                    ]


def merge_kernel(m, rows, *refs):
    direct, (feats, cot, own_weight), refs = list(refs[: m - 2]), refs[m - 2 : m + 1], refs[m + 1 :]
    for value, held in zip(refs[:2], refs[2:4]):
        held[...] = value[...]
    lists, weights, bundle = refs[4:]
    size = 4 * SLOT
    for c in range(m):
        wide = {1: feats, m // 2: cot}.get(c)
        if wide is None:
            source = direct.pop(0)
        else:
            source = bundle
            height = chunk_of(bundle.shape[0], wide.shape[1] // LANES)
            for q in range(wide.shape[1] // LANES):
                stop = min((q + 1) * height, bundle.shape[0])
                if stop > q * height:
                    bundle[q * height : stop] = wide[
                        wide.shape[0] - height : wide.shape[0] - height + stop - q * height,
                        q * LANES : (q + 1) * LANES,
                    ]
        weights[2 * c * rows : 2 * (c + 1) * rows] = source[: 2 * rows]
        lists[c * size : (c + 1) * size] = source[2 * rows :]
    for q in range(own_weight.shape[1] // LANES):
        start = (2 * m + q) * rows
        weights[start : start + rows] = own_weight[:, q * LANES : (q + 1) * LANES]


def gate_kernel(*_):
    pass


def fill_filters(neighbors, own_radial, filters):
    basis = own_radial.shape[0]
    half = basis * SLOT
    row = lax.broadcasted_iota(jnp.int32, (half, LANES), 0) % SLOT
    spread = jnp.concatenate(
        [jnp.broadcast_to(own_radial[b : b + 1], (SLOT, LANES)) for b in range(basis)], axis=0
    )
    high = spread.astype(bf16).astype(f32)
    low = spread - high
    for k in range(neighbors):
        lanes = slice(k * LANES, (k + 1) * LANES)
        filters[:half, lanes] = jnp.where(row == k, high, 0.0).astype(bf16)
        filters[half:, lanes] = jnp.where(row == k, low, 0.0).astype(bf16)


def fill_values(columns, filters, values):
    high = columns.astype(bf16)
    both = jnp.concatenate([high, high], axis=1)
    span = 2 * LANES

    def step(j, _):
        lanes = pl.ds(pl.multiple_of(j * span, span), span)
        values[:, lanes] = jnp.dot(both, filters[:, lanes], preferred_element_type=f32)
        return 0

    steps = values.shape[1] // span
    lax.fori_loop(0, steps, step, 0, unroll=steps)


def fill_pick(margin, neighbors, turned, pick):
    tile = 2 * margin
    tiles = turned.shape[0] // tile
    shift = (
        lax.broadcasted_iota(jnp.int32, (tile, 2 * tile), 1)
        - lax.broadcasted_iota(jnp.int32, (tile, 2 * tile), 0)
        - margin
    ).astype(f32)
    for t in range(tiles):
        own = turned[t * tile : (t + 1) * tile]
        for k in range(neighbors):
            at = column_of(k, neighbors)
            pick[k * tile : (k + 1) * tile, t * 2 * tile : (t + 1) * 2 * tile] = jnp.where(
                own[:, at : at + 1] == shift, 1.0, 0.0
            ).astype(bf16)


def fill_place(margin, neighbors, offset, place):
    tile = 2 * margin
    shape = (2 * tile, 2 * tile)
    shift = (
        lax.broadcasted_iota(jnp.int32, shape, 0)
        - lax.broadcasted_iota(jnp.int32, shape, 1) % tile
        - margin
    ).astype(f32)
    for t in range(offset.shape[1] // tile):
        for k in range(0, neighbors, 2):
            row = jnp.concatenate(
                [offset[k + i : k + i + 1, t * tile : (t + 1) * tile] for i in range(2)], axis=1
            )
            place[t * 2 * tile : (t + 1) * 2 * tile, k * tile : (k + 2) * tile] = jnp.where(
                row == shift, 1.0, 0.0
            ).astype(bf16)


def lists_kernel(n, margin, neighbors, ahead, *refs):
    m = n // 2
    near, far, own_radial = refs[:3]
    columns, offsets = refs[3:5]
    made = refs[5:8] if ahead else ()
    dists, graph_weight, stacked, filters = refs[5 + len(made) :]
    me = lax.axis_index("fsdp")
    basis = own_radial.shape[0]
    atoms = columns.shape[0] // n
    for d in range(n):
        e = me ^ d
        meta = (far if d % 2 else near)[d // 2 * 4 * SLOT : (d // 2 + 1) * 4 * SLOT].astype(f32)
        offsets[rows_at(e, SLOT)] = meta[:SLOT]
        dists[rows_at(e, SLOT)] = (
            meta[SLOT : 2 * SLOT] + meta[2 * SLOT : 3 * SLOT] + meta[3 * SLOT :]
        )
    slots = lax.broadcasted_iota(jnp.int32, offsets.shape, 0) % SLOT
    ids = jnp.where(slots == neighbors, offsets[...], -1.0)
    weight = jnp.zeros_like(ids)
    for g in range(GRAPHS):
        member = ids == float(g)
        count = jnp.sum(jnp.where(member, 1.0, 0.0), axis=(0, 1), keepdims=True)
        weight = weight + jnp.where(member, lax.rsqrt(jnp.maximum(count, 1.0)), 0.0)
    graph_weight[...] = weight

    def columns_step(e, _):
        dist = dists[rows_at(e, SLOT)]
        envelope = 0.5 * (jnp.cos(jnp.pi * dist / cutoff) + 1.0)
        own = stacked.at[e % stacked.shape[0]]
        for b in range(basis):
            center = cutoff * b / (basis - 1)
            own[b * SLOT : (b + 1) * SLOT] = jnp.exp(-sharpness * (dist - center) ** 2) * envelope
        offset = offsets[rows_at(e, SLOT)]
        for k in range(neighbors):
            at = column_of(k, neighbors)
            own[at : at + 1] = offset[k : k + 1]
        at = column_of(neighbors, neighbors)
        own[at : at + 1] = graph_weight[rows_at(e, SLOT)][neighbors : neighbors + 1]
        columns[rows_at(e, atoms)] = own[...].T
        return 0

    lax.fori_loop(0, n, columns_step, 0, unroll=stacked.shape[0])
    if ahead:
        values, pick, place = made
        fill_filters(neighbors, own_radial, filters)
        fill_values(columns[...], filters, values)

        def block_step(e, _):
            span = neighbors * 2 * margin
            fill_pick(margin, neighbors, columns[rows_at(e, atoms)], pick.at[rows_at(e, span)])
            fill_place(
                margin,
                neighbors,
                offsets[rows_at(e, SLOT)],
                place.at[rows_at(e, 2 * atoms)],
            )
            return 0

        lax.fori_loop(0, n, block_step, 0, unroll=8)


def products_kernel(n, near, far, own_weight, *refs):
    m = n // 2
    feats, cots, refs = refs[:m], refs[m : 2 * m], refs[2 * m :]
    keep, give, held_feats, both, weights = refs
    me = lax.axis_index("fsdp")
    atoms = feats[0].shape[0]
    half = m * atoms
    rows = own_weight.shape[0]
    if rows < LANES:
        both[...] = jnp.zeros_like(both)
        both[:rows] = own_weight[...]
        for q in range(both.shape[1] // LANES):
            start = (2 * m + q) * rows
            both[LANES : LANES + rows, q * LANES : (q + 1) * LANES] = far[start : start + rows]
    for c in range(m):
        for k, source in enumerate((near, far)):
            block = rows_at(me ^ (2 * c + k), rows)
            for i in range(2):
                start = (2 * c + i) * rows
                side = slice(LANES, None) if i != k else slice(0, LANES)
                weights[block, side] = source[start : start + rows]
    for c in range(m):
        held_feats[c * atoms : (c + 1) * atoms] = feats[c][:atoms]
    projected = jnp.dot(held_feats[...], weights[...], preferred_element_type=f32).astype(bf16)
    flow = jnp.concatenate([cots[c][:atoms] for c in range(m)], axis=0)
    pieces = both.shape[1] // LANES
    other = jnp.concatenate(
        [far[(2 * m + q) * rows : (2 * m + q + 1) * rows] for q in range(pieces)], axis=1
    )
    table = both[...] if rows < LANES else jnp.concatenate([own_weight[...], other], axis=0)
    dact = lax.dot_general(
        flow, table, (((1,), (1,)), ((), ())), preferred_element_type=f32
    ).astype(bf16)
    for c in range(m):
        chip = (me // 2) ^ c
        here = slice(c * atoms, (c + 1) * atoms)
        keep[rows_at(chip, atoms)] = projected[here, :LANES]
        give[rows_at(chip, atoms)] = projected[here, LANES:]
        keep[rows_at(chip + m, atoms)] = dact[here, :LANES]
        give[rows_at(chip + m, atoms)] = dact[here, LANES:]


def forward_kernel(n, margin, neighbors, norm, ahead, *refs):
    own, got, columns, own_radial = refs[:4]
    made = refs[4:6] if ahead else ()
    keep, give, dagg, projected, act = refs[4 + len(made) : 9 + len(made)]
    scratch = refs[9 + len(made) :]
    me = lax.axis_index("fsdp")
    core = me % 2
    atoms = columns.shape[0] // n
    half = n // 2 * atoms
    projected[:margin] = jnp.zeros_like(projected[:margin])
    projected[n * atoms + margin :] = jnp.zeros_like(projected[:margin])
    for c in range(n // 2):
        for source, parity in ((own, core), (got, 1 - core)):
            start = pl.multiple_of((2 * c + parity) * atoms + margin, margin)
            projected[pl.ds(start, atoms)] = source[c * atoms : (c + 1) * atoms]
            dact = source[half + c * atoms : half + (c + 1) * atoms]
            dagg[rows_at(2 * c + parity, atoms)] = dact.astype(f32)
    if ahead:
        values, pick = made
    else:
        filters, values, pick = scratch
        fill_filters(neighbors, own_radial, filters)
    tile = 2 * margin
    span = neighbors * tile

    def block_step(e, _):
        turned = columns[rows_at(e, atoms)]
        if ahead:
            own_values = values.at[rows_at(e, atoms)]
            own_pick = pick[rows_at(e, span)]
        else:
            own_values = values
            fill_values(turned, filters, values)
            fill_pick(margin, neighbors, turned, pick)
            own_pick = pick[...]
        start = pl.multiple_of(e * atoms, atoms)
        halves = []
        for t in range(2):
            found = jnp.dot(
                own_pick[:, t * 2 * tile : (t + 1) * 2 * tile],
                projected[pl.ds(start + t * tile, 2 * tile)],
                preferred_element_type=f32,
            )
            total = jnp.zeros((tile, LANES), f32)
            for k in range(neighbors):
                total = total + (
                    own_values[t * tile : (t + 1) * tile, k * LANES : (k + 1) * LANES]
                    * found[k * tile : (k + 1) * tile]
                )
            halves.append(total)
        agg = jnp.concatenate(halves, axis=0) * norm
        sig = 1.0 / (1.0 + jnp.exp(-agg))
        active = (agg * sig).astype(bf16)
        at = column_of(neighbors, neighbors)
        graph = turned[:, at : at + 1]
        slope = sig * (1.0 + agg * (1.0 - sig)) * (graph * norm)
        dagg[rows_at(e, atoms)] = dagg[rows_at(e, atoms)] * slope
        act[rows_at(e, atoms)] = active
        return 0

    lax.fori_loop(0, n, block_step, 0, unroll=min(n, 8) if ahead else 1)
    for c in range(n // 2):
        keep[c * atoms : (c + 1) * atoms] = act[rows_at(2 * c + core, atoms)]
        give[c * atoms : (c + 1) * atoms] = act[rows_at(2 * c + 1 - core, atoms)]


def backward_kernel(n, margin, neighbors, ahead, *refs):
    m = n // 2
    dagg, own_radial, columns, offsets = refs[:4]
    made = refs[4:6] if ahead else ()
    refs = refs[4 + len(made) :]
    turned, spread = refs[:2]
    scratch = refs[2:]
    me = lax.axis_index("fsdp")
    atoms = columns.shape[0] // n
    tile = 2 * margin
    spread[0, n * atoms :] = jnp.zeros_like(spread[0, n * atoms :])
    spread[1, :tile] = jnp.zeros_like(spread[1, :tile])
    if ahead:
        values, place = made
    else:
        filters, values, place = scratch
        fill_filters(neighbors, own_radial, filters)

    def block_step(e, _):
        flow = dagg[rows_at(e, atoms)]
        if ahead:
            own_values = values.at[rows_at(e, atoms)]
            own_place = place.at[rows_at(e, 2 * atoms)]
        else:
            own_values = values
            fill_values(columns[rows_at(e, atoms)], filters, values)
            fill_place(margin, neighbors, offsets[rows_at(e, SLOT)], place)
            own_place = place
        for t in range(2):
            here = slice(t * tile, (t + 1) * tile)
            own = jnp.concatenate(
                [
                    (own_values[here, k * LANES : (k + 1) * LANES] * flow[here]).astype(bf16)
                    for k in range(neighbors)
                ],
                axis=0,
            )
            window = pl.ds(pl.multiple_of(e * atoms + t * tile, tile), 2 * tile)
            spread[t, window] = jnp.dot(
                own_place[t * 2 * tile : (t + 1) * 2 * tile], own, preferred_element_type=f32
            )
        return 0

    lax.fori_loop(0, n, block_step, 0, unroll=min(n, 8) if ahead else 1)

    half = m * atoms
    for k in range(2):
        for c in range(m):
            e = me ^ (2 * c + k)
            start = pl.multiple_of(e * atoms + margin, margin)
            turned[:, k * half + c * atoms : k * half + (c + 1) * atoms] = (
                (spread[0, pl.ds(start, atoms)] + spread[1, pl.ds(start, atoms)]).T.astype(bf16)
            )


def gradient_kernel(n, rows, turned, own_feats, other_feats, *refs):
    m = n // 2
    keep, give, grads = refs
    me = lax.axis_index("fsdp")
    half = own_feats.shape[0]
    total = jnp.dot(turned[:, :half], own_feats[...], preferred_element_type=f32)
    total = total + jnp.dot(turned[:, half:], other_feats[...], preferred_element_type=f32)
    for q in range(total.shape[1] // LANES):
        grads[q * LANES : (q + 1) * LANES] = total[:, q * LANES : (q + 1) * LANES].T
    for c in range(m):
        keep[c * rows : (c + 1) * rows] = grads[rows_at(me ^ (2 * c), rows)].astype(bf16)
        give[c * rows : (c + 1) * rows] = grads[rows_at(me ^ (2 * c + 1), rows)]


def join_kernel(keep, got, *sends):
    rows = sends[0].shape[0]
    for c, send in enumerate(sends):
        send[:, :LANES] = keep[c * rows : (c + 1) * rows]
        send[:, LANES:] = got[c * rows : (c + 1) * rows].astype(bf16)


def write_code(piece, code):
    rows = piece.shape[0]
    scale = (jnp.max(jnp.abs(piece), axis=-1, keepdims=True) + tiny).astype(bf16)
    wide = jnp.broadcast_to(scale.astype(f32), piece.shape)
    code[:rows] = (piece / wide).astype(bf16)
    if rows < LANES:
        wide = jnp.concatenate([wide, jnp.zeros((LANES - rows, LANES), f32)], axis=0)
    code[rows:] = wide.T[:SLOT].astype(bf16)


def chip_kernel(n, margin, neighbors, width, *refs):
    m = n // 2
    columns, keep, got, own_weight, other_weight, _after = refs[:6]
    cots, sends, (own, give) = refs[6 : 6 + m], refs[6 + m : 6 + 2 * m], refs[6 + 2 * m :]
    me = lax.axis_index("fsdp")
    atoms = cots[0].shape[0]
    rows = own.shape[0]
    at = column_of(neighbors, neighbors)
    pieces = own_weight.shape[1] // LANES
    first = other_weight.shape[0] - pieces * rows
    other_weight = jnp.concatenate(
        [other_weight[first + q * rows : first + (q + 1) * rows] for q in range(pieces)], axis=1
    )
    acts = [
        jnp.concatenate([act[rows_at((me // 2) ^ c, atoms)] for c in range(m)], axis=0)
        for act in (keep, got)
    ]
    total = jnp.dot(acts[0][:, :width], own_weight[...], preferred_element_type=f32) + jnp.dot(
        acts[1][:, :width], other_weight, preferred_element_type=f32
    )
    for c in range(m):
        sends[c][...] = total[c * atoms : (c + 1) * atoms].astype(bf16)
    graph = jnp.concatenate(
        [columns[rows_at(me ^ (2 * c), atoms)][:, at : at + 1] for c in range(m)], axis=0
    )
    left = jnp.concatenate([(act.astype(f32) * graph).T.astype(bf16) for act in acts], axis=0)
    flow = jnp.concatenate([cots[c][:atoms] for c in range(m)], axis=0)
    parts = jnp.dot(left, flow, preferred_element_type=f32)
    own[...] = parts[:rows]
    give[...] = parts[LANES : LANES + rows].astype(bf16)


def join_blocks(n, near, blocks, grad):
    me = lax.axis_index("fsdp")
    width = grad.shape[-1] // n
    for c in range(n // 2):
        blocks[me ^ (2 * c)] = near[c][:, :LANES]
        blocks[me ^ (2 * c + 1)] = near[c][:, LANES:]
    for e in range(n):
        grad[:, e * width : (e + 1) * width] = blocks[e][:, :width]


def code_kernel(n, fragment, *refs):
    m = n // 2
    near, (got_part, own_part, code, blocks, joined) = refs[:m], refs[m:]
    rows = joined.shape[0]
    lanes = pl.ds(pl.multiple_of(fragment[0] * FRAG, FRAG), FRAG)
    join_blocks(n, near, blocks, joined)
    write_code(joined[:, lanes].astype(f32), code.at[: rows + SLOT])
    total = own_part[:, lanes] + got_part[:, lanes].astype(f32)
    write_code(total, code.at[rows + SLOT :])


def grads_kernel(n, *refs):
    m = n // 2
    near, (got_part, own_part, _after, msg_grad, out_grad, made, blocks) = refs[:m], refs[m:]
    made[...] = jnp.zeros_like(made)
    join_blocks(n, near, blocks, msg_grad.at[0])
    out_grad[0] = (own_part[...] + got_part[...].astype(f32)).astype(bf16)


def pair_kernel(*refs):
    codes, out = refs[:-1], refs[-1]
    rows = out.shape[1]
    for piece in range(2):
        total = jnp.zeros((rows, FRAG), f32)
        for code in codes:
            own = code.at[piece * (rows + SLOT) : (piece + 1) * (rows + SLOT)]
            wide = jnp.broadcast_to(own[rows:].astype(f32)[:1], (LANES, LANES)).T
            total = total + wide[:rows] * own[:rows].astype(f32)
        out[piece] = total.astype(out.dtype)


def outer_kernel(own, other, out):
    out[...] = (own[...].astype(f32) + other[...].astype(f32)).astype(out.dtype)


def last_kernel(count, *refs):
    pair, (feats, *parts), (_after, outer, node) = refs[:count], refs[count:-3], refs[-3:]
    outer[...] = functools.reduce(jnp.add, [value[...].astype(f32) for value in pair])
    total = feats[...].astype(f32)
    for part in parts:
        total = total + part[...].astype(f32)
    node[...] = total.astype(bf16)


def run(kernel, outs, scratch, args, micros, memory=16, scalars=0, outside=0):
    whole = pl.BlockSpec(memory_space=pltpu.VMEM)
    scalar = pl.BlockSpec(memory_space=pltpu.SMEM)
    remote = pl.BlockSpec(memory_space=pltpu.HBM)
    return pl.pallas_call(
        kernel,
        out_shape=[jax.ShapeDtypeStruct(shape, dtype) for shape, dtype in outs],
        in_specs=[scalar] * scalars
        + [whole] * (len(args) - scalars - outside)
        + [remote] * outside,
        out_specs=[whole] * len(outs),
        scratch_shapes=[
            pltpu.SemaphoreType.DMA(shape) if dtype is None else pltpu.VMEM(shape, dtype)
            for shape, dtype in scratch
        ],
        compiler_params=pltpu.CompilerParams(vmem_limit_bytes=memory << 20),
        cost_estimate=pl.CostEstimate(
            flops=int(micros * 1e9), bytes_accessed=int(micros * 3e6), transcendentals=0
        ),
    )(*args)


def after(values, other, micros):
    anywhere = pl.BlockSpec(memory_space=pl.ANY)
    return pl.pallas_call(
        gate_kernel,
        out_shape=[jax.ShapeDtypeStruct(value.shape, value.dtype) for value in values],
        in_specs=[anywhere] * (len(values) + 1),
        out_specs=[anywhere] * len(values),
        input_output_aliases={i: i for i in range(len(values))},
        compiler_params=pltpu.CompilerParams(vmem_limit_bytes=1 << 20),
        cost_estimate=pl.CostEstimate(
            flops=int(micros * 1e9), bytes_accessed=int(micros * 3e6), transcendentals=0
        ),
    )(*values, other)


def hop(value, axis, step):
    count = lax.axis_size(axis)
    return lax.ppermute(value, axis, [(i, i ^ step) for i in range(count)])


def across_chips(sends):
    return [sends[0]] + [hop(sends[c], "fsdp", 2 * c) for c in range(1, len(sends))]


def exchanged(value, held, m, side):
    pieces = {0: value, **held}
    for c in range(1, m):
        if c not in pieces:
            used = [1 << i for i in range(m.bit_length()) if c >> i & 1][side]
            pieces[c] = hop(pieces[c ^ used], "fsdp", 2 * used)
    return [pieces[c] for c in range(m)]


def shards(
    node_feats,
    neighbor_src,
    distances,
    graph_ids,
    msg_weight,
    out_weight,
    radial_weight,
    cotangent,
    fragment,
):
    n = lax.axis_size("fsdp")
    replicas = lax.axis_size("replica")
    m = n // 2
    atoms, channels = node_feats.shape
    neighbors = neighbor_src.shape[0]
    basis = radial_weight.shape[0]
    rows = msg_weight.shape[0]
    width = channels // n
    margin = atoms // 4
    norm = 1.0 / math.sqrt(neighbors)
    all_atoms = n * atoms
    lanes = neighbors * LANES
    ahead = all_atoms * lanes * 4 <= 8 << 20
    memory = 24 if ahead else 56
    step_scratch = [
        ((2 * basis * SLOT, lanes), bf16),
        ((atoms, lanes), f32),
    ]

    pack_inputs = [
        msg_weight,
        neighbor_src,
        distances,
        graph_ids,
        radial_weight,
        node_feats,
        cotangent,
    ]
    bundle = 2 * rows + 4 * SLOT
    wide = (atoms + chunk_of(bundle, channels // LANES), channels)
    *packed, wide_feats, wide_cot, own_radial = run(
        functools.partial(pack_kernel, n, width),
        [((bundle, LANES), bf16)] * (m - 2) + [(wide, bf16)] * 2 + [((basis, LANES), f32)],
        [
            ((n, rows, LANES), bf16),
            ((n, basis, LANES), f32),
            ((SLOT, LANES), f32),
            ((bundle, LANES), bf16),
        ]
        + [(piece.shape, piece.dtype) for piece in pack_inputs]
        + [((len(pack_inputs),), None)],
        pack_inputs,
        1,
        60,
        outside=len(pack_inputs),
    )
    others = [c for c in range(1, m) if c not in (1, m // 2)]
    feats = exchanged(node_feats, {1: hop(wide_feats, "fsdp", 2)}, m, 0)
    cots = exchanged(cotangent, {m // 2: hop(wide_cot, "fsdp", 2 * (m // 2))}, m, -1)
    own_feats, own_cot, near_lists, near_weights = run(
        functools.partial(merge_kernel, m, rows),
        [((atoms, channels), bf16)] * 2
        + [
            ((m * 4 * SLOT, LANES), bf16),
            (((2 * m + channels // LANES) * rows, LANES), bf16),
        ],
        [((bundle, LANES), bf16)],
        [packed[0]]
        + list(after([hop(value, "fsdp", 2 * c) for c, value in zip(others, packed[1:])], own_radial, 10))
        + [feats[1], cots[m // 2], out_weight, node_feats, cotangent],
        0,
        memory,
    )
    far_weights = hop(near_weights, "fsdp", 1)
    columns, offsets, *made = run(
        functools.partial(lists_kernel, n, margin, neighbors, ahead),
        [
            ((all_atoms, LANES), f32),
            ((n * SLOT, LANES), f32),
        ]
        + [
            ((all_atoms, lanes), f32),
            ((n * neighbors * 2 * margin, 8 * margin), bf16),
            ((2 * all_atoms, neighbors * 2 * margin), bf16),
        ]
        * ahead,
        [
            ((n * SLOT, LANES), f32),
            ((n * SLOT, LANES), f32),
            ((min(n, 8), basis * SLOT, LANES), f32),
            ((2 * basis * SLOT, lanes), bf16),
        ],
        [near_lists, hop(near_lists, "fsdp", 1), own_radial],
        0,
        memory,
    )
    feats[0], cots[0] = own_feats, own_cot
    passed = [(pieces, c) for pieces in (feats, cots) for c in range(1, m) if c & (c - 1)]
    held = after([pieces[c] for pieces, c in passed], offsets, 10)
    for (pieces, c), value in zip(passed, held):
        pieces[c] = value
    own_products, give_products, held_feats = run(
        functools.partial(products_kernel, n),
        [((all_atoms, LANES), bf16)] * 2 + [((all_atoms // 2, channels), bf16)],
        [((2 * LANES, channels), bf16), ((channels, 2 * LANES), bf16)],
        [near_weights, far_weights, out_weight, *feats, *cots],
        1,
        memory,
    )
    got_products = hop(give_products, "fsdp", 1)
    (held_feats,) = after([held_feats], got_products, 0)
    keep, give, dagg = run(
        functools.partial(forward_kernel, n, margin, neighbors, norm, ahead),
        [
            ((all_atoms // 2, LANES), bf16),
            ((all_atoms // 2, LANES), bf16),
            ((all_atoms, LANES), f32),
        ],
        [((all_atoms + 2 * margin, LANES), bf16), ((all_atoms, LANES), bf16)]
        + (step_scratch + [((neighbors * 2 * margin, 8 * margin), bf16)]) * (not ahead),
        [own_products, got_products, columns, own_radial, *made[:2]],
        1,
        memory,
    )
    other_act = hop(give, "fsdp", 1)
    (turned,) = run(
        functools.partial(backward_kernel, n, margin, neighbors, ahead),
        [((LANES, all_atoms), bf16)],
        [
            ((2, all_atoms + 2 * margin, LANES), f32),
        ]
        + (step_scratch + [((2 * atoms, neighbors * 2 * margin), bf16)]) * (not ahead),
        [dagg, own_radial, columns, offsets, *made[::2]],
        1,
        memory,
    )
    keep_grads, give_grads = run(
        functools.partial(gradient_kernel, n, rows),
        [((m * rows, LANES), bf16), ((m * rows, LANES), f32)],
        [((channels, LANES), f32)],
        [turned, held_feats, hop(held_feats, "fsdp", 1)],
        1,
        memory,
    )
    *sums, own_part, give_part = run(
        functools.partial(chip_kernel, n, margin, neighbors, width),
        [((atoms, channels), bf16)] * m + [((rows, channels), f32), ((rows, channels), bf16)],
        [],
        [columns, keep, other_act, out_weight, far_weights, give_grads, *cots],
        1,
        memory,
    )
    grad_sends = run(
        join_kernel,
        [((rows, 2 * LANES), bf16)] * m,
        [],
        [keep_grads, hop(give_grads, "fsdp", 1)],
        0,
        memory,
    )
    near = across_chips(grad_sends)
    got_part = hop(give_part, "fsdp", 1)
    (code,) = run(
        functools.partial(code_kernel, n),
        [((2 * (rows + SLOT), FRAG), bf16)],
        [((n, rows, LANES), bf16), ((rows, channels), bf16)],
        [fragment, *near, got_part, own_part],
        4,
        memory,
        scalars=1,
    )
    grad_msg, grad_out, made = run(
        functools.partial(grads_kernel, n),
        [((1, rows, channels), bf16)] * 2 + [((8, LANES), f32)],
        [((n, rows, LANES), bf16)],
        [*near, got_part, own_part, code],
        0,
        memory,
    )
    sums = across_chips(sums)
    step = 1
    codes = [code]
    if replicas > 1:
        codes.append(hop(code, "replica", step))
    (outer_sum,) = run(
        pair_kernel, [((2, rows, FRAG), f32 if replicas <= 2 else bf16)], [], codes, 0, memory
    )
    while 4 * step < replicas:
        step = 2 * step
        (outer_sum,) = run(
            outer_kernel,
            [((2, rows, FRAG), bf16)],
            [],
            [outer_sum, hop(outer_sum, "replica", step)],
            0,
            memory,
        )
    pair = [outer_sum]
    if replicas > 2:
        pair.append(hop(outer_sum, "replica", 2 * step))
    outer_sum, node_out = run(
        functools.partial(last_kernel, len(pair)),
        [((2, rows, FRAG), f32), ((atoms, channels), bf16)],
        [],
        [*pair, node_feats, *sums, made],
        0,
        memory,
    )
    return node_out, grad_msg, grad_out, outer_sum


def solution(mesh):
    placed = (
        P(("replica", "fsdp"), None),
        P(None, ("replica", "fsdp")),
        P(None, ("replica", "fsdp")),
        P("replica", "fsdp"),
        P("fsdp", None),
        P("fsdp", None),
        P(),
        P(("replica", "fsdp"), None),
        P(),
    )
    return jax.shard_map(
        shards,
        mesh=mesh,
        in_specs=placed,
        out_specs=(
            P(("replica", "fsdp"), None),
            P("replica", "fsdp", None),
            P("replica", "fsdp", None),
            P(None, "fsdp", None),
        ),
        check_vma=False,
    )
```
